32 devices in a mesh: groups: 2 (over y), dp: 4 (over z), din: 2 (over x), dout: 2 (over core).
Axes of the slice: x: 2, y: 2, z: 4, core: 2. Of those that a mesh axis runs over, the one named last changes fastest.
Arguments:
- activations: bfloat16 [2048, 4096], P(('groups', 'dp'), 'din'), parts along dimension 0, may hold values from -6 to 6
- out_grads: bfloat16 [2048, 14336], P(('groups', 'dp'), 'dout'), parts along dimension 0, may hold values from -6 to 6
- queries: bfloat16 [2, 2, 7168, 4096], P(None, 'dout', 'dp', 'din'), may hold values from -0.0007324219 to 0.0007324219
Outputs:
- scores: float32 [2, 2048], P(None, ('groups', 'dp')), parts along dimension 1
The draws below stay inside these ranges and needn't reach their ends.
There are 2 independent parts, one for each index of `groups`. The reference program is written for one: setup_inputs(seed, part) draws one part's arguments, and reference() takes and returns one part's arrays. A program takes and returns all parts, laid end to end along the dimension named above; an argument that names none is the same for every part. Nothing has to cross between parts.
All inputs are finite; a program needn't handle non-finite values.
Results may differ from the reference program's by a relative error of at most 0.0003.
Values may be sent and summed in bfloat16 or wider, within the bound.
No kernel may reach another device: no remote copies, remote signals or barrier semaphores. Data moves between devices by JAX's collectives and lax.ppermute only.
A program may use at most 128 MiB of HBM per device.

```python
import jax
import jax.numpy as jnp
from jax import lax

DIN = 4096
DOUT = 14336
NQ = 2
TOKENS = 1024
OUT_SPLIT = 2


def steps_of(stream_key, dims, cuts, smallest, largest):
    def one(axis_at, shards_of):
        heights = jax.random.uniform(jax.random.fold_in(jax.random.fold_in(stream_key, 6), axis_at), (shards_of,), jnp.float32, smallest / len(cuts), largest / len(cuts))
        return jnp.repeat(jnp.exp(heights), dims[axis_at] // shards_of).reshape((-1,) + (1,) * (len(dims) - axis_at - 1))

    factor_of = one(*cuts[0])
    for cut in cuts[1:]:
        factor_of = factor_of * one(*cut)
    return factor_of


def bell_draw(rng, dims, spread, limit, split=(), dtype=jnp.bfloat16):
    drawn = jax.random.normal(rng, dims, jnp.float32) * spread
    if len(split) > 0:
        drawn = steps_of(rng, dims, split, -0.22, 0.18) * drawn
    return jnp.clip(drawn, min=-limit, max=limit).astype(dtype)


def setup_inputs(seed: int = 0, part: int = 0) -> dict:
    keys = jax.random.split(jax.random.key(seed), 4)
    part_splits = jax.random.split(jax.random.fold_in(keys[3], part), 4)
    activations = bell_draw(part_splits[0], (TOKENS, DIN), 1.0, 6.0, ((0, 4), (1, 2)))
    out_grads = bell_draw(part_splits[1], (TOKENS, DOUT), 1.0, 6.0, ((0, 4), (1, 2)))
    queries = bell_draw(keys[2], (NQ, OUT_SPLIT, DOUT // OUT_SPLIT, DIN), (DOUT * DIN) ** -0.5, 0.0007324219, ((1, 2), (2, 4), (3, 2)))
    return dict(activations=activations, out_grads=out_grads, queries=queries)


def reference(activations, out_grads, queries):
    whole = queries.reshape(NQ, DOUT, DIN)
    act_f = activations.astype(jnp.float32)

    def one_query(matrix):
        proj = jnp.dot(out_grads, matrix, preferred_element_type=jnp.float32)
        return jnp.sum(act_f * proj, axis=1)

    return lax.map(one_query, whole)
```

```python
import jax
import jax.numpy as jnp
from jax import lax
from jax.sharding import PartitionSpec as P


def share(block, axis):
    part = block.shape[0] // lax.axis_size(axis)
    return lax.dynamic_slice_in_dim(block, lax.axis_index(axis) * part, part, 0)


def on_device(activations, out_grads, queries):
    count = lax.axis_size("dp")
    tokens = activations.shape[0]
    rows = queries.shape[2]

    mine = share(out_grads, "din")
    part = mine.shape[0]
    blocks = mine.reshape(part, count, rows).transpose(1, 0, 2)
    blocks = lax.all_to_all(blocks, "dp", 0, 0)
    grads = lax.all_gather(blocks, "din", axis=1).reshape(count * tokens, rows)

    acts = lax.all_gather(share(activations, "dout"), ("dp", "dout"), axis=0, tiled=True)

    proj = jnp.einsum("tc,qci->qti", grads, queries[:, 0], preferred_element_type=jnp.float32)
    total = jnp.sum(acts.astype(jnp.float32)[None] * proj, axis=2)
    total = lax.psum(total, ("dp", "din", "dout"))
    return lax.dynamic_slice_in_dim(total, lax.axis_index("dp") * tokens, tokens, 1)


def solution(mesh):
    placed = (P(("groups", "dp"), "din"), P(("groups", "dp"), "dout"), P(None, "dout", "dp", "din"))
    return jax.shard_map(
        on_device, mesh=mesh, in_specs=placed, out_specs=P(None, ("groups", "dp")), check_vma=False
    )
```

```python
import functools

import jax
import jax.numpy as jnp
from jax import lax
from jax.experimental import pallas as pl
from jax.experimental.pallas import tpu as pltpu
from jax.sharding import PartitionSpec as P


def partner(index, step, count):
    if count & (count - 1) == 0:
        return index ^ step
    return (step - index) % count


def trade(block, steps):
    axes = tuple(steps)
    sizes = [lax.axis_size(axis) for axis in axes]
    route = []
    for source in range(functools.reduce(lambda a, b: a * b, sizes)):
        rest, target, scale = source, 0, 1
        for axis, size in zip(reversed(axes), reversed(sizes)):
            target += partner(rest % size, steps[axis], size) * scale
            rest //= size
            scale *= size
        route.append((source, target))
    return lax.ppermute(block, axes, route)


def slot_kernel(where, *refs):
    parts, (acts_ref, query_ref, out_ref, grads, sums) = refs[:-5], refs[-5:]
    query, tile = pl.program_id(0), pl.program_id(1)
    rows = parts[0].shape[0]

    @pl.when((query == 0) & (tile == 0))
    def _():
        for r, part in enumerate(parts):
            at = pl.multiple_of(where[1 + r] * rows, rows)
            grads[pl.ds(at, rows), :] = part[...]

    @pl.when(tile == 0)
    def _():
        sums[...] = jnp.zeros_like(sums)

    proj = jnp.dot(grads[...], query_ref[0, 0], preferred_element_type=jnp.float32)
    terms = acts_ref[...].astype(jnp.float32) * proj
    lanes = sums.shape[1]
    total = sums[...]
    for at in range(0, terms.shape[1], lanes):
        total = total + terms[:, at : at + lanes]
    sums[...] = total

    @pl.when(tile == pl.num_programs(1) - 1)
    def _():
        out_ref[pl.ds(query, 1), :] = jnp.sum(total.T, axis=0, keepdims=True)


def slot_scores(parts, order, acts, block, queries):
    nq, _, depth, width = queries.shape
    tokens = sum(part.shape[0] for part in parts)
    tile = min(512, width)
    where = jnp.stack([block] + list(order)).astype(jnp.int32)
    spec = pltpu.PrefetchScalarGridSpec(
        num_scalar_prefetch=1,
        grid=(nq, width // tile),
        in_specs=[pl.BlockSpec(part.shape, lambda q, i, where: (0, 0)) for part in parts]
        + [
            pl.BlockSpec((tokens, tile), lambda q, i, where: (where[0], i)),
            pl.BlockSpec((1, 1, depth, tile), lambda q, i, where: (q, 0, 0, i)),
        ],
        out_specs=pl.BlockSpec((nq, tokens), lambda q, i, where: (0, 0)),
        scratch_shapes=[pltpu.VMEM((tokens, depth), parts[0].dtype), pltpu.VMEM((tokens, 128), jnp.float32)],
    )
    return pl.pallas_call(
        slot_kernel,
        grid_spec=spec,
        out_shape=jax.ShapeDtypeStruct((nq, tokens), jnp.float32),
        compiler_params=pltpu.CompilerParams(vmem_limit_bytes=52 * 1024 * 1024),
        cost_estimate=pl.CostEstimate(
            flops=2 * nq * tokens * depth * width,
            bytes_accessed=2 * (nq * depth * width + tokens * (depth + width)),
            transcendentals=0,
        ),
    )(where, *parts, acts, queries)


def on_device(activations, out_grads, queries):
    count, spread = lax.axis_size("dp"), lax.axis_size("din")
    me, column = lax.axis_index("dp"), lax.axis_index("din")
    tokens, rows = activations.shape[0], queries.shape[2]
    part, half = tokens // spread, tokens // lax.axis_size("dout")

    def grads_for(device):
        return lax.dynamic_slice(out_grads, (column * part, device * rows), (part, rows))

    acts = lax.dynamic_slice_in_dim(activations, lax.axis_index("dout") * half, half, 0)
    acts = lax.all_gather(acts, ("dp", "dout"), axis=0, tiled=True)

    steps = sorted(range(1, count), key=lambda d: -d)
    arrived = {d: trade(grads_for(partner(me, d, count)), {"dp": d}) for d in steps}

    own = lax.dynamic_slice_in_dim(out_grads, me * rows, rows, 1)
    zero = jnp.zeros((), jnp.int32)
    home = slot_scores([own], [zero], activations, zero, queries)

    sides = range(spread)
    order = [partner(column, r, spread) for r in sides]
    last = None
    for d in steps:
        parts = [arrived[d]] + [trade(arrived[d], {"din": r}) for r in sides[1:]]
        last = slot_scores(parts, order, acts, partner(me, d, count), queries)
        if d != steps[-1]:
            home = home + trade(last, {"dp": d})
    pairs = [(r, c) for r in sides for c in range(lax.axis_size("dout"))]
    total = home
    for r, c in pairs[1:]:
        total = total + trade(home, {"din": r, "dout": c})
    for r, c in pairs:
        total = total + trade(last, {"dp": steps[-1], "din": r, "dout": c})
    return total


def solution(mesh):
    placed = (P(("groups", "dp"), "din"), P(("groups", "dp"), "dout"), P(None, "dout", "dp", "din"))
    return jax.shard_map(
        on_device, mesh=mesh, in_specs=placed, out_specs=P(None, ("groups", "dp")), check_vma=False
    )
```

```python
import functools
import math

import jax
import jax.numpy as jnp
from jax import lax
from jax.experimental import pallas as pl
from jax.experimental.pallas import tpu as pltpu
from jax.sharding import PartitionSpec as P


def trade(block, steps):
    axes = tuple(steps)
    sizes = [lax.axis_size(axis) for axis in axes]
    mask = 0
    for axis, size in zip(axes, sizes):
        mask = mask * size + steps[axis]
    return lax.ppermute(block, axes, [(i, i ^ mask) for i in range(math.prod(sizes))])


def after(value, *others):
    return lax.optimization_barrier((value, *others))[0]


def pass_on(block, step, count):
    up = lax.ppermute(block[0], "dp", [(i, i + 1) for i in range(step - 1, count - 1)])
    down = lax.ppermute(block[1], "dp", [(i, i - 1) for i in range(1, count - step + 1)])
    return up, down


def from_partner(hops, me, d, count):
    groups = {}
    for z in range(count):
        away = z - (z ^ d)
        groups.setdefault((abs(away), away < 0), []).append(z)
    chosen = None
    for (step, down), members in groups.items():
        block = hops[step][int(down)]
        if chosen is None:
            chosen = block
        else:
            chosen = jnp.where(functools.reduce(jnp.logical_or, [me == z for z in members]), block, chosen)
    return chosen


def mix_kernel(where, mine_ref, other_ref, query_ref, out_ref, acts):
    half = mine_ref.shape[0]

    @pl.when((pl.program_id(0) == 0) & (pl.program_id(1) == 0))
    def _():
        acts[pl.ds(pl.multiple_of(where[0] * half, half), half), :] = mine_ref[...]
        acts[pl.ds(pl.multiple_of(where[1] * half, half), half), :] = other_ref[...]

    out_ref[0] = lax.dot_general(
        query_ref[0, 0], acts[...], (((1,), (1,)), ((), ())), preferred_element_type=jnp.float32
    )


def mixed(mine, other, core, queries):
    nq, _, depth, width = queries.shape
    half = mine.shape[0]
    tokens = 2 * half
    tile = depth // 2
    spec = pltpu.PrefetchScalarGridSpec(
        num_scalar_prefetch=1,
        grid=(nq, depth // tile),
        in_specs=[
            pl.BlockSpec((half, width), lambda q, o, where: (0, 0)),
            pl.BlockSpec((half, width), lambda q, o, where: (0, 0)),
            pl.BlockSpec((1, 1, tile, width), lambda q, o, where: (q, 0, o, 0)),
        ],
        out_specs=pl.BlockSpec((1, tile, tokens), lambda q, o, where: (q, o, 0)),
        scratch_shapes=[pltpu.VMEM((tokens, width), mine.dtype)],
    )
    return pl.pallas_call(
        mix_kernel,
        grid_spec=spec,
        out_shape=jax.ShapeDtypeStruct((nq, depth, tokens), jnp.float32),
        compiler_params=pltpu.CompilerParams(vmem_limit_bytes=36 * 1024 * 1024),
        cost_estimate=pl.CostEstimate(
            flops=2 * nq * tokens * depth * width,
            bytes_accessed=2 * (nq * depth * width + tokens * width) + 4 * nq * depth * tokens,
            transcendentals=0,
        ),
    )(jnp.stack([core, 1 - core]).astype(jnp.int32), mine, other, queries)


def score_kernel(where, *refs):
    parts, (mix_ref, out_ref) = refs[:-2], refs[-2:]
    found = []
    for p in range(len(parts)):
        chosen = parts[0][...]
        for r in range(1, len(parts)):
            chosen = jnp.where(where[0] == p ^ r, parts[r][...], chosen)
        found.append(chosen.astype(jnp.float32))
    grads = found[0] if len(found) == 1 else jnp.concatenate(found, axis=1)
    for q in range(mix_ref.shape[0]):
        out_ref[q : q + 1, :] = jnp.sum(grads * mix_ref[q], axis=0, keepdims=True)


def piece_scores(parts, column, mix, piece, pieces):
    nq, depth, tokens = mix.shape
    rows = depth // pieces
    spec = pltpu.PrefetchScalarGridSpec(
        num_scalar_prefetch=1,
        grid=(1,),
        in_specs=[pl.BlockSpec(part.shape, lambda i, where: (0, 0)) for part in parts]
        + [pl.BlockSpec((nq, rows, tokens), lambda i, where: (0, piece, 0))],
        out_specs=pl.BlockSpec((nq, tokens), lambda i, where: (0, 0)),
    )
    return pl.pallas_call(
        score_kernel,
        grid_spec=spec,
        out_shape=jax.ShapeDtypeStruct((nq, tokens), jnp.float32),
        compiler_params=pltpu.CompilerParams(vmem_limit_bytes=36 * 1024 * 1024),
        cost_estimate=pl.CostEstimate(
            flops=2 * nq * rows * tokens,
            bytes_accessed=4 * nq * rows * tokens + 2 * rows * tokens,
            transcendentals=0,
        ),
    )(jnp.reshape(column, (1,)).astype(jnp.int32), *parts, mix)


def on_device(activations, out_grads, queries):
    count, spread = lax.axis_size("dp"), lax.axis_size("din")
    me, column, core = lax.axis_index("dp"), lax.axis_index("din"), lax.axis_index("dout")
    tokens, rows = activations.shape[0], queries.shape[2]
    part, half = tokens // spread, tokens // 2

    mine = lax.dynamic_slice_in_dim(activations, core * half, half, 0)
    hops = [(mine, mine)]
    hops.append(pass_on(hops[0], 1, count))

    turned = lax.dynamic_slice_in_dim(out_grads, column * part, part, 0).T

    def grads_for(d, piece=0, pieces=1):
        size = rows // pieces
        return lax.dynamic_slice_in_dim(turned, (me ^ d) * rows + piece * size, size, 0)

    def to_column(arrived):
        return [arrived] + [trade(arrived, {"din": r}) for r in range(1, spread)]

    def mixed_for(d):
        block = from_partner(hops, me, d, count)
        return mixed(block, trade(block, {"dout": 1}), core, queries)

    steps = list(range(count - 1, 0, -1))
    last = 2 if count > 2 else 1
    steps.remove(last)
    arrived = {steps[0]: trade(grads_for(steps[0]), {"dp": steps[0]})}

    own_mix = mixed(activations[:half], activations[half:], jnp.zeros_like(core), queries)
    own = lax.dynamic_slice_in_dim(out_grads, me * rows, rows, 1).T
    home = piece_scores([own], jnp.zeros_like(column), own_mix, 0, 1)

    pieces = 2
    tail = []
    for step in range(2, count):
        hops.append(pass_on(hops[-1], step, count))
        if step == 2:
            for piece in range(pieces):
                ready = after(grads_for(last, piece, pieces), *hops[1])
                tail.append(trade(ready, {"dp": last}))
        if step < count:
            for d in steps[step - 1 : step]:
                arrived[d] = trade(after(grads_for(d), *hops[step]), {"dp": d})
    if not tail:
        tail = [trade(grads_for(last, piece, pieces), {"dp": last}) for piece in range(pieces)]

    mixes = {d: mixed_for(d) for d in sorted(steps + [last])}
    for d in steps:
        home = home + trade(piece_scores(to_column(arrived[d]), column, mixes[d], 0, 1), {"dp": d})
    pairs = [(r, c) for r in range(spread) for c in range(2)]
    total = home
    for r, c in pairs[1:]:
        total = total + trade(home, {"din": r, "dout": c})
    final = None
    for piece, block in enumerate(tail):
        scores = piece_scores(to_column(block), column, mixes[last], piece, pieces)
        final = scores if final is None else final + scores
    for r, c in pairs:
        total = total + trade(final, {"dp": last, "din": r, "dout": c})
    return total


def solution(mesh):
    placed = (P(("groups", "dp"), "din"), P(("groups", "dp"), "dout"), P(None, "dout", "dp", "din"))
    return jax.shard_map(
        on_device, mesh=mesh, in_specs=placed, out_specs=P(None, ("groups", "dp")), check_vma=False
    )
```

```python
import functools
import math

import jax
import jax.numpy as jnp
from jax import lax
from jax.experimental import pallas as pl
from jax.experimental.pallas import tpu as pltpu
from jax.sharding import PartitionSpec as P


MATMUL_FLOPS = 5_000_000_000


def trade(block, steps):
    axes = tuple(steps)
    sizes = [lax.axis_size(axis) for axis in axes]
    mask = 0
    for axis, size in zip(axes, sizes):
        mask = mask * size + steps[axis]
    return lax.ppermute(block, axes, [(i, i ^ mask) for i in range(math.prod(sizes))])


def pass_on(block, step, count):
    up = lax.ppermute(block[0], "dp", [(i, i + 1) for i in range(step - 1, count - 1)])
    down = lax.ppermute(block[1], "dp", [(i, i - 1) for i in range(1, count - step + 1)])
    return up, down


ANYWHERE = pl.BlockSpec(memory_space=pl.ANY)


def call(kernel, grid, where, inputs, shape, out_spec, scratch, flops, tokens):
    arrays = [array for array, _ in inputs]
    skip = len(tokens)

    def body(where, *refs):
        kernel(where, *refs[: len(arrays)], *refs[len(arrays) + skip :])

    return pl.pallas_call(
        body,
        grid_spec=pltpu.PrefetchScalarGridSpec(
            num_scalar_prefetch=1,
            grid=grid,
            in_specs=[spec for _, spec in inputs] + [ANYWHERE] * skip,
            out_specs=out_spec,
            scratch_shapes=scratch,
        ),
        out_shape=shape,
        compiler_params=pltpu.CompilerParams(vmem_limit_bytes=36 * 1024 * 1024),
        cost_estimate=pl.CostEstimate(flops=flops, bytes_accessed=1024, transcendentals=0),
    )(jnp.stack([jnp.asarray(w, jnp.int32) for w in where]), *arrays, *tokens)


def hold(blocks, tokens):
    count = len(blocks)
    return pl.pallas_call(
        lambda *refs: None,
        in_specs=[ANYWHERE] * (count + len(tokens)),
        out_specs=[ANYWHERE] * count,
        out_shape=[jax.ShapeDtypeStruct(block.shape, block.dtype) for block in blocks],
        input_output_aliases={i: i for i in range(count)},
        cost_estimate=pl.CostEstimate(flops=1024, bytes_accessed=1024, transcendentals=0),
    )(*blocks, *tokens)


def cut_kernel(turn, where, block_ref, out_ref):
    block = block_ref[...]
    out_ref[...] = block.astype(jnp.float32).T.astype(block.dtype) if turn else block


def cut(out_grads, shape, at, turn, tokens=()):
    out = shape[::-1] if turn else shape
    if shape[0] % 128 or shape[1] % 128:
        block = lax.dynamic_slice(out_grads, [i * size for i, size in zip(at, shape)], shape)
        return block.T if turn else block
    return call(
        functools.partial(cut_kernel, turn), (1,), at,
        [(out_grads, pl.BlockSpec(shape, lambda i, where: (where[0], where[1])))],
        jax.ShapeDtypeStruct(out, out_grads.dtype), pl.BlockSpec(out, lambda i, where: (0, 0)), [], 1024, tokens,
    )


def pick_kernel(where, *refs):
    *blocks, out_ref = refs
    for k, block in enumerate(blocks):

        @pl.when(where[0] == k)
        def _():
            out_ref[...] = block[...]


def from_partner(hops, me, d, count, tokens=()):
    sources, choice = [], []
    for z in range(count):
        away = z - (z ^ d)
        source = (abs(away), int(away < 0))
        if source not in sources:
            sources.append(source)
        choice.append(sources.index(source))
    where = functools.reduce(lambda found, z: jnp.where(me == z, choice[z], found), range(count), 0)
    blocks = [hops[step][way] for step, way in sources]
    spec = pl.BlockSpec(blocks[0].shape, lambda i, where: (0, 0))
    return call(
        pick_kernel, (1,), [where], [(block, spec) for block in blocks],
        jax.ShapeDtypeStruct(blocks[0].shape, blocks[0].dtype), spec, [], 1024, tokens,
    )


def joined(parts, where, axis):
    found = []
    for p in range(len(parts)):
        chosen = parts[0][...]
        for r in range(1, len(parts)):
            chosen = jnp.where(where[0] == p ^ r, parts[r][...], chosen)
        found.append(chosen)
    return found[0] if len(found) == 1 else jnp.concatenate(found, axis=axis)


def mix_kernel(where, mine_ref, other_ref, query_ref, out_ref, acts):
    half = mine_ref.shape[0]

    @pl.when((pl.program_id(0) == 0) & (pl.program_id(1) == 0))
    def _():
        acts[pl.ds(pl.multiple_of(where[0] * half, half), half), :] = mine_ref[...]
        acts[pl.ds(pl.multiple_of((1 - where[0]) * half, half), half), :] = other_ref[...]

    out_ref[0] = lax.dot_general(
        query_ref[0, 0], acts[...], (((1,), (1,)), ((), ())), preferred_element_type=jnp.float32
    )


def mixed(mine, other, core, queries, tokens=()):
    nq, _, depth, width = queries.shape
    pairs = [block if isinstance(block, tuple) else (block, 0) for block in (mine, other)]
    half = pairs[1][0].shape[0] // (2 if isinstance(other, tuple) else 1)
    tile = depth // 2
    inputs = [(array, pl.BlockSpec((half, width), lambda q, o, where, k=k: (k, 0))) for array, k in pairs]
    inputs.append((queries, pl.BlockSpec((1, 1, tile, width), lambda q, o, where: (q, 0, o, 0))))
    return call(
        mix_kernel, (nq, depth // tile), [core], inputs,
        jax.ShapeDtypeStruct((nq, depth, 2 * half), jnp.float32),
        pl.BlockSpec((1, tile, 2 * half), lambda q, o, where: (q, o, 0)),
        [pltpu.VMEM((2 * half, width), queries.dtype)], MATMUL_FLOPS, tokens,
    )


def score_kernel(where, *refs):
    parts, (mix_ref, out_ref) = refs[:-2], refs[-2:]
    grads = joined(parts, where, 1).astype(jnp.float32)
    for q in range(mix_ref.shape[0]):
        out_ref[q : q + 1, :] = jnp.sum(grads * mix_ref[q], axis=0, keepdims=True)


def scores_of_grads(parts, column, mix, piece, pieces, tokens=()):
    nq, depth, count = mix.shape
    inputs = [(part, pl.BlockSpec(part.shape, lambda i, where: (0, 0))) for part in parts]
    inputs.append((mix, pl.BlockSpec((nq, depth // pieces, count), lambda i, where: (0, piece, 0))))
    return call(
        score_kernel, (1,), [column], inputs, jax.ShapeDtypeStruct((nq, count), jnp.float32),
        pl.BlockSpec((nq, count), lambda i, where: (0, 0)), [], 1024, tokens,
    )


def deliver_kernel(number, copies, where, *refs):
    (*parts, mix_ref), terms, out_ref = refs[: -number - 2], refs[-number - 2 : -1], refs[-1]
    grads = joined(parts, where, 1).astype(jnp.float32)
    last = [jnp.sum(grads * mix_ref[q], axis=0, keepdims=True) for q in range(mix_ref.shape[0])]
    last = jnp.concatenate(last, axis=0) + terms[0][...]
    for k in range(number + 1):
        value = last if k == 0 else terms[k][...]
        for c in range(copies):
            out_ref[where[1 + k] * copies + c] = value


def delivered(parts, column, mix, piece, pieces, terms, targets, copies):
    nq, depth, count = mix.shape
    inputs = [(part, pl.BlockSpec(part.shape, lambda i, where: (0, 0))) for part in parts]
    inputs.append((mix, pl.BlockSpec((nq, depth // pieces, count), lambda i, where: (0, piece, 0))))
    inputs += [(term, pl.BlockSpec(term.shape, lambda i, where: (0, 0))) for term in terms]
    shape = (len(terms) * copies, nq, count)
    return call(
        functools.partial(deliver_kernel, len(terms) - 1, copies), (1,), [column] + list(targets), inputs,
        jax.ShapeDtypeStruct(shape, jnp.float32), pl.BlockSpec(shape, lambda i, where: (0, 0, 0)), [], 1024, (),
    )


def project_kernel(where, *refs):
    parts, (query_ref, out_ref, grads) = refs[:-3], refs[-3:]

    @pl.when((pl.program_id(0) == 0) & (pl.program_id(1) == 0))
    def _():
        grads[...] = joined(parts, where, 0)

    out_ref[0] = jnp.dot(grads[...], query_ref[0, 0], preferred_element_type=jnp.float32)


def projected(parts, column, queries, tokens=()):
    nq, _, depth, width = queries.shape
    count = sum(part.shape[0] for part in parts)
    tile = width // 2
    inputs = [(part, pl.BlockSpec(part.shape, lambda q, i, where: (0, 0))) for part in parts]
    inputs.append((queries, pl.BlockSpec((1, 1, depth, tile), lambda q, i, where: (q, 0, 0, i))))
    return call(
        project_kernel, (nq, width // tile), [column], inputs,
        jax.ShapeDtypeStruct((nq, count, width), jnp.float32),
        pl.BlockSpec((1, count, tile), lambda q, i, where: (q, 0, i)),
        [pltpu.VMEM((count, depth), queries.dtype)], MATMUL_FLOPS, tokens,
    )


def finish_kernel(where, mine_ref, other_ref, proj_ref, out_ref):
    half, width = mine_ref.shape
    swapped = where[0] == 1
    for h, (first, second) in enumerate(((mine_ref, other_ref), (other_ref, mine_ref))):
        acts = jnp.where(swapped, second[...], first[...]).astype(jnp.float32)
        for q in range(proj_ref.shape[0]):
            terms = acts * proj_ref[q, h * half : (h + 1) * half, :]
            lanes = terms[:, :128]
            for at in range(128, width, 128):
                lanes = lanes + terms[:, at : at + 128]
            out_ref[q : q + 1, h * half : (h + 1) * half] = jnp.sum(lanes.T, axis=0, keepdims=True)


def scores_of_acts(mine, other, core, proj, tokens=()):
    nq, count, _ = proj.shape
    inputs = [(block, pl.BlockSpec(block.shape, lambda i, where: (0, 0))) for block in (mine, other)]
    inputs.append((proj, pl.BlockSpec(proj.shape, lambda i, where: (0, 0, 0))))
    return call(
        finish_kernel, (1,), [core], inputs, jax.ShapeDtypeStruct((nq, count), jnp.float32),
        pl.BlockSpec((nq, count), lambda i, where: (0, 0)), [], 1024, tokens,
    )


def on_device(activations, out_grads, queries):
    count, spread = lax.axis_size("dp"), lax.axis_size("din")
    me, column, core = lax.axis_index("dp"), lax.axis_index("din"), lax.axis_index("dout")
    tokens, rows = activations.shape[0], queries.shape[2]
    part, half = tokens // spread, tokens // 2
    pieces = 2

    def grads_for(d, turn, piece=0, pieces=1, tokens=()):
        size = rows // pieces
        return cut(out_grads, (part, size), (column, (me ^ d) * pieces + piece), turn, tokens)

    def to_columns(arrived):
        return [arrived] + [trade(arrived, {"din": r}) for r in range(1, spread)]

    def acts_of(d, tokens=()):
        block = from_partner(hops, me, d, count, tokens)
        return block, trade(block, {"dout": 1})

    far, late = count - 1, count // 2
    early = [d for d in range(1, count) if d not in (far, late)]

    mine = lax.dynamic_slice_in_dim(activations, core * half, half, 0)
    hops = [(mine, mine)]
    hops.append(pass_on(hops[0], 1, count))

    sent = {far: grads_for(far, False)}
    for d in early:
        sent[d] = grads_for(d, True)
    arrived = {d: trade(block, {"dp": d}) for d, block in sent.items()}

    zero = jnp.zeros((), jnp.int32)
    own_mix = mixed((activations, 0), (activations, 1), zero, queries, list(sent.values()))
    own = cut(out_grads, (tokens, rows), (zero, me), True)
    scores = {0: scores_of_grads([own], zero, own_mix, 0, 1)}

    mixes, token = {}, own_mix
    tail = []
    for step in range(1, count):
        if step > 1:
            hops.append(pass_on(hops[-1], step, count))
        if step == late:
            hops[step] = hold(hops[step], list(arrived.values()) + [token])
        if step in early:
            mixes[step] = token = mixed(*acts_of(step), core, queries, [token])
        if step <= pieces:
            waits = [token] if step == 1 else list(hops[step])
            tail.append(trade(grads_for(late, True, step - 1, pieces, waits), {"dp": late}))
    mixes[late] = token = mixed(*acts_of(late), core, queries, [token])
    proj = projected(to_columns(arrived[far]), column, queries, [token, tail[0], scores[0]])

    for d in early:
        scores[d] = scores_of_grads(to_columns(arrived[d]), column, mixes[d], 0, 1, [proj])
    scores[far] = scores_of_acts(*acts_of(far, [mixes[late]]), core, proj, [scores[d] for d in early])
    for piece, block in enumerate(tail[:-1]):
        term = scores_of_grads(to_columns(block), column, mixes[late], piece, pieces, [scores[far]])
        scores[late] = scores[late] + term if piece else term
    order = [late] + [d for d in range(count) if d != late]
    last, = hold(tail[-1:], [proj])
    blocks = delivered(
        to_columns(last), column, mixes[late], pieces - 1, pieces,
        [scores[d] for d in order], [me ^ d for d in order], spread * lax.axis_size("dout"),
    )
    return jnp.sum(lax.all_to_all(blocks, ("dp", "din", "dout"), 0, 0), axis=0)


def solution(mesh):
    placed = (P(("groups", "dp"), "din"), P(("groups", "dp"), "dout"), P(None, "dout", "dp", "din"))
    return jax.shard_map(
        on_device, mesh=mesh, in_specs=placed, out_specs=P(None, ("groups", "dp")), check_vma=False
    )
```

```python
import functools
import math

import jax
import jax.numpy as jnp
from jax import lax
from jax.experimental import pallas as pl
from jax.experimental.pallas import tpu as pltpu
from jax.sharding import PartitionSpec as P


MATMUL_FLOPS = 500_000_000
LATE_FLOPS = 20_000_000_000


def trade(block, steps, backwards=False):
    axes = tuple(steps)
    sizes = [lax.axis_size(axis) for axis in axes]
    mask = 0
    for axis, size in zip(axes, sizes):
        mask = mask * size + steps[axis]
    route = [(i, i ^ mask) for i in range(math.prod(sizes))]
    return lax.ppermute(block, axes, route[::-1] if backwards else route)


def pass_on(block, step, count):
    up = lax.ppermute(block[0], "dp", [(i, i + 1) for i in range(step - 1, count - 1)])
    down = lax.ppermute(block[1], "dp", [(i, i - 1) for i in range(1, count - step + 1)])
    return up, down


ANYWHERE = pl.BlockSpec(memory_space=pl.ANY)


def call(kernel, grid, where, inputs, shape, out_spec, scratch, flops, tokens, vmem=36):
    arrays = [array for array, _ in inputs]
    skip = len(tokens)

    def body(where, *refs):
        kernel(where, *refs[: len(arrays)], *refs[len(arrays) + skip :])

    return pl.pallas_call(
        body,
        grid_spec=pltpu.PrefetchScalarGridSpec(
            num_scalar_prefetch=1,
            grid=grid,
            in_specs=[spec for _, spec in inputs] + [ANYWHERE] * skip,
            out_specs=out_spec,
            scratch_shapes=scratch,
        ),
        out_shape=shape,
        compiler_params=pltpu.CompilerParams(vmem_limit_bytes=vmem * 1024 * 1024),
        cost_estimate=pl.CostEstimate(flops=flops, bytes_accessed=1024, transcendentals=0),
    )(jnp.stack([jnp.asarray(w, jnp.int32) for w in where]), *arrays, *tokens)


def hold(blocks, tokens):
    count = len(blocks)
    return pl.pallas_call(
        lambda *refs: None,
        in_specs=[ANYWHERE] * (count + len(tokens)),
        out_specs=[ANYWHERE] * count,
        out_shape=[jax.ShapeDtypeStruct(block.shape, block.dtype) for block in blocks],
        input_output_aliases={i: i for i in range(count)},
        cost_estimate=pl.CostEstimate(flops=1024, bytes_accessed=1024, transcendentals=0),
    )(*blocks, *tokens)


def turn_kernel(pieces, where, *refs):
    blocks, outs = refs[: len(pieces)], list(refs[len(pieces) :])
    for block, number in zip(blocks, pieces):
        turned = block[...].astype(jnp.float32).T.astype(block.dtype)
        size = turned.shape[0] // number
        for p in range(number):
            outs.pop(0)[...] = turned[p * size : (p + 1) * size]


def turned(blocks, pieces, tokens=()):
    rows, width = blocks[0].shape
    if rows % 128 or width % 128:
        return [piece for block, number in zip(blocks, pieces) for piece in jnp.split(block.T, number)]
    sizes = [width // number for number in pieces for _ in range(number)]
    return call(
        functools.partial(turn_kernel, pieces), (1,), [jnp.zeros((), jnp.int32)],
        [(block, pl.BlockSpec(block.shape, lambda i, where: (0, 0))) for block in blocks],
        [jax.ShapeDtypeStruct((size, rows), blocks[0].dtype) for size in sizes],
        [pl.BlockSpec((size, rows), lambda i, where: (0, 0)) for size in sizes], [], 1024, tokens,
    )


def pick_kernel(where, *refs):
    *blocks, out_ref = refs
    for k, block in enumerate(blocks):

        @pl.when(where[0] == k)
        def _():
            out_ref[...] = block[...]


def from_partner(hops, me, d, count, tokens=()):
    sources, choice = [], []
    for z in range(count):
        away = z - (z ^ d)
        source = (abs(away), int(away < 0))
        if source not in sources:
            sources.append(source)
        choice.append(sources.index(source))
    where = functools.reduce(lambda found, z: jnp.where(me == z, choice[z], found), range(count), 0)
    blocks = [hops[step][way] for step, way in sources]
    spec = pl.BlockSpec(blocks[0].shape, lambda i, where: (0, 0))
    return call(
        pick_kernel, (1,), [where], [(block, spec) for block in blocks],
        jax.ShapeDtypeStruct(blocks[0].shape, blocks[0].dtype), spec, [], 1024, tokens,
    )


def joined(parts, where, axis):
    found = []
    for p in range(len(parts)):
        chosen = parts[0][...]
        for r in range(1, len(parts)):
            chosen = jnp.where(where[0] == p ^ r, parts[r][...], chosen)
        found.append(chosen)
    return found[0] if len(found) == 1 else jnp.concatenate(found, axis=axis)


def mix_kernel(where, mine_ref, other_ref, query_ref, out_ref, acts):
    half = mine_ref.shape[0]

    @pl.when((pl.program_id(0) == 0) & (pl.program_id(1) == 0))
    def _():
        acts[pl.ds(pl.multiple_of(where[0] * half, half), half), :] = mine_ref[...]
        acts[pl.ds(pl.multiple_of((1 - where[0]) * half, half), half), :] = other_ref[...]

    out_ref[0] = lax.dot_general(
        query_ref[0, 0], acts[...], (((1,), (1,)), ((), ())), preferred_element_type=jnp.float32
    )


def mixed(mine, other, core, queries, tokens=()):
    nq, _, depth, width = queries.shape
    pairs = [block if isinstance(block, tuple) else (block, 0) for block in (mine, other)]
    half = pairs[1][0].shape[0] // (2 if isinstance(other, tuple) else 1)
    tile = depth // 2
    inputs = [(array, pl.BlockSpec((half, width), lambda q, o, where, k=k: (k, 0))) for array, k in pairs]
    inputs.append((queries, pl.BlockSpec((1, 1, tile, width), lambda q, o, where: (q, 0, o, 0))))
    return call(
        mix_kernel, (nq, depth // tile), [core], inputs,
        jax.ShapeDtypeStruct((nq, depth, 2 * half), jnp.float32),
        pl.BlockSpec((1, tile, 2 * half), lambda q, o, where: (q, o, 0)),
        [pltpu.VMEM((2 * half, width), queries.dtype)], MATMUL_FLOPS, tokens,
    )


def score_kernel(where, *refs):
    parts, (mix_ref, out_ref) = refs[:-2], refs[-2:]
    grads = joined(parts, where, 1).astype(jnp.float32)
    for q in range(mix_ref.shape[0]):
        out_ref[q : q + 1, :] = jnp.sum(grads * mix_ref[q], axis=0, keepdims=True)


def scores_of_grads(parts, column, mix, piece, pieces, tokens=(), flops=1024):
    nq, depth, count = mix.shape
    inputs = [(part, pl.BlockSpec(part.shape, lambda i, where: (0, 0))) for part in parts]
    inputs.append((mix, pl.BlockSpec((nq, depth // pieces, count), lambda i, where: (0, piece, 0))))
    return call(
        score_kernel, (1,), [column], inputs, jax.ShapeDtypeStruct((nq, count), jnp.float32),
        pl.BlockSpec((nq, count), lambda i, where: (0, 0)), [], flops, tokens,
    )


def project_kernel(where, *refs):
    parts, (query_ref, out_ref, grads) = refs[:-3], refs[-3:]

    @pl.when((pl.program_id(0) == 0) & (pl.program_id(1) == 0))
    def _():
        grads[...] = joined(parts, where, 0)

    out_ref[0] = jnp.dot(grads[...], query_ref[0, 0], preferred_element_type=jnp.float32)


def projected(parts, column, queries, tokens=()):
    nq, _, depth, width = queries.shape
    count = sum(part.shape[0] for part in parts)
    tile = width // 2
    inputs = [(part, pl.BlockSpec(part.shape, lambda q, i, where: (0, 0))) for part in parts]
    inputs.append((queries, pl.BlockSpec((1, 1, depth, tile), lambda q, i, where: (q, 0, 0, i))))
    return call(
        project_kernel, (nq, width // tile), [column], inputs,
        jax.ShapeDtypeStruct((nq, count, width), jnp.float32),
        pl.BlockSpec((1, count, tile), lambda q, i, where: (q, 0, i)),
        [pltpu.VMEM((count, depth), queries.dtype)], MATMUL_FLOPS, tokens,
    )


def finish_kernel(where, mine_ref, other_ref, proj_ref, out_ref):
    half, width = mine_ref.shape
    swapped = where[0] == 1
    for h, (first, second) in enumerate(((mine_ref, other_ref), (other_ref, mine_ref))):
        acts = jnp.where(swapped, second[...], first[...]).astype(jnp.float32)
        for q in range(proj_ref.shape[0]):
            terms = acts * proj_ref[q, h * half : (h + 1) * half, :]
            lanes = terms[:, :128]
            for at in range(128, width, 128):
                lanes = lanes + terms[:, at : at + 128]
            out_ref[q : q + 1, h * half : (h + 1) * half] = jnp.sum(lanes.T, axis=0, keepdims=True)


def scores_of_acts(mine, other, core, proj, tokens=()):
    nq, count, _ = proj.shape
    inputs = [(block, pl.BlockSpec(block.shape, lambda i, where: (0, 0))) for block in (mine, other)]
    inputs.append((proj, pl.BlockSpec(proj.shape, lambda i, where: (0, 0, 0))))
    return call(
        finish_kernel, (1,), [core], inputs, jax.ShapeDtypeStruct((nq, count), jnp.float32),
        pl.BlockSpec((nq, count), lambda i, where: (0, 0)), [], 1024, tokens,
    )


def on_device(activations, out_grads, queries):
    count, spread = lax.axis_size("dp"), lax.axis_size("din")
    me, column, core = lax.axis_index("dp"), lax.axis_index("din"), lax.axis_index("dout")
    tokens, rows = activations.shape[0], queries.shape[2]
    part, half = tokens // spread, tokens // 2
    pieces = 1

    def to_columns(arrived):
        return [arrived] + [trade(arrived, {"din": r}) for r in range(1, spread)]

    def acts_of(block):
        return block, trade(block, {"dout": 1})

    far, late = count - 1, count - 2
    early = [d for d in range(1, count) if d not in (far, late)]

    mine = lax.dynamic_slice_in_dim(activations, core * half, half, 0)
    hops = [(mine, mine)]
    hops.append(pass_on(hops[0], 1, count))

    def grads_for(device, first, size):
        return lax.dynamic_slice(out_grads, (first, device * rows), (size, rows))

    arrived = {far: trade(grads_for(me ^ far, column * part, part), {"dp": far})}
    others = early + [late]
    sent = turned([grads_for(me ^ d, column * part, part) for d in others], [1] * len(early) + [pieces])
    for d, block in zip(early, sent):
        arrived[d] = trade(block, {"dp": d})
    for step in range(2, count - 1):
        hops.append(pass_on(hops[-1], step, count))

    zero = jnp.zeros((), jnp.int32)
    token = own_mix = mixed((activations, 0), (activations, 1), zero, queries, list(sent) + list(hops[1]))
    tail = [trade(hold([block], [own_mix])[0], {"dp": late}) for block in sent[len(early) :]]
    own, = turned([grads_for(me, 0, tokens)], [1])
    scores = scores_of_grads([own], zero, own_mix, 0, 1)

    mixes = {}
    for d in others:
        block = from_partner(hops, me, d, count, [token] + [arrived[e] for e in early] if d == late else [])
        if d == late:
            end = lax.ppermute(block, "dp", [(1, 0), (count - 2, count - 1)])
            hops.append((end, end))
        mixes[d] = token = mixed(*acts_of(block), core, queries, [token])
    proj = projected(to_columns(arrived[far]), column, queries, [token, scores])

    token = proj
    for d in early:
        token = scores_of_grads(to_columns(arrived[d]), column, mixes[d], 0, 1, [token])
        scores = scores + trade(token, {"dp": d})
    total = None
    for piece, block in enumerate(tail):
        block = hold([block], [proj])[0]
        term = scores_of_grads(
            to_columns(block), column, mixes[late], piece, pieces, [token], LATE_FLOPS
        )
        total = term if total is None else total + term
    block = from_partner(hops, me, far, count, [mixes[late]])
    term = scores_of_acts(*acts_of(block), core, proj)
    scores = scores + trade(term, {"dp": far})
    total = scores + trade(total, {"dp": late})
    total = total + trade(total, {"dout": 1})
    return total + sum(trade(total, {"din": r}) for r in range(1, spread))


def solution(mesh):
    placed = (P(("groups", "dp"), "din"), P(("groups", "dp"), "dout"), P(None, "dout", "dp", "din"))
    return jax.shard_map(
        on_device, mesh=mesh, in_specs=placed, out_specs=P(None, ("groups", "dp")), check_vma=False
    )
```

```python
import functools
import math

import jax
import jax.numpy as jnp
from jax import lax
from jax.experimental import pallas as pl
from jax.experimental.pallas import tpu as pltpu
from jax.sharding import PartitionSpec as P


LONG, SHORT = 40_000_000_000, 1_000_000


def trade(block, steps, backwards=False):
    axes = tuple(steps)
    sizes = [lax.axis_size(axis) for axis in axes]
    mask = 0
    for axis, size in zip(axes, sizes):
        mask = mask * size + steps[axis]
    route = [(i, i ^ mask) for i in range(math.prod(sizes))]
    return lax.ppermute(block, axes, route[::-1] if backwards else route)


def pass_on(block, step, count):
    up = lax.ppermute(block[0], "dp", [(i, i + 1) for i in range(step - 1, count - 1)])
    down = lax.ppermute(block[1], "dp", [(i, i - 1) for i in range(1, count - step + 1)])
    return up, down


ANYWHERE = pl.BlockSpec(memory_space=pl.ANY)


def call(kernel, grid, where, inputs, shape, out_spec, scratch, flops, tokens, vmem=36):
    arrays = [array for array, _ in inputs]
    skip = len(tokens)

    def body(where, *refs):
        kernel(where, *refs[: len(arrays)], *refs[len(arrays) + skip :])

    return pl.pallas_call(
        body,
        grid_spec=pltpu.PrefetchScalarGridSpec(
            num_scalar_prefetch=1,
            grid=grid,
            in_specs=[spec for _, spec in inputs] + [ANYWHERE] * skip,
            out_specs=out_spec,
            scratch_shapes=scratch,
        ),
        out_shape=shape,
        compiler_params=pltpu.CompilerParams(vmem_limit_bytes=vmem * 1024 * 1024),
        cost_estimate=pl.CostEstimate(flops=flops, bytes_accessed=1024, transcendentals=0),
    )(jnp.stack([jnp.asarray(w, jnp.int32) for w in where]), *arrays, *tokens)


def hold(blocks, tokens):
    count = len(blocks)
    return pl.pallas_call(
        lambda *refs: None,
        in_specs=[ANYWHERE] * (count + len(tokens)),
        out_specs=[ANYWHERE] * count,
        out_shape=[jax.ShapeDtypeStruct(block.shape, block.dtype) for block in blocks],
        input_output_aliases={i: i for i in range(count)},
        cost_estimate=pl.CostEstimate(flops=1024, bytes_accessed=1024, transcendentals=0),
    )(*blocks, *tokens)


def turn_kernel(pieces, where, *refs):
    blocks, outs = refs[: len(pieces)], list(refs[len(pieces) :])
    for block, number in zip(blocks, pieces):
        turned = block[...].astype(jnp.float32).T.astype(block.dtype)
        size = turned.shape[0] // number
        for p in range(number):
            outs.pop(0)[...] = turned[p * size : (p + 1) * size]


def turned(blocks, pieces, tokens=()):
    rows, width = blocks[0].shape
    if rows % 128 or width % 128:
        return [piece for block, number in zip(blocks, pieces) for piece in jnp.split(block.T, number)]
    sizes = [width // number for number in pieces for _ in range(number)]
    return call(
        functools.partial(turn_kernel, pieces), (1,), [jnp.zeros((), jnp.int32)],
        [(block, pl.BlockSpec(block.shape, lambda i, where: (0, 0))) for block in blocks],
        [jax.ShapeDtypeStruct((size, rows), blocks[0].dtype) for size in sizes],
        [pl.BlockSpec((size, rows), lambda i, where: (0, 0)) for size in sizes], [], 1024, tokens,
    )


def pick_kernel(where, *refs):
    *blocks, out_ref = refs
    for k, block in enumerate(blocks):

        @pl.when(where[0] == k)
        def _():
            out_ref[...] = block[...]


def from_partner(hops, me, d, count, tokens=()):
    sources, choice = [], []
    for z in range(count):
        away = z - (z ^ d)
        source = (abs(away), int(away < 0))
        if source not in sources:
            sources.append(source)
        choice.append(sources.index(source))
    where = functools.reduce(lambda found, z: jnp.where(me == z, choice[z], found), range(count), 0)
    blocks = [hops[step][way] for step, way in sources]
    spec = pl.BlockSpec(blocks[0].shape, lambda i, where: (0, 0))
    return call(
        pick_kernel, (1,), [where], [(block, spec) for block in blocks],
        jax.ShapeDtypeStruct(blocks[0].shape, blocks[0].dtype), spec, [], 1024, tokens,
    )


def joined(parts, where, axis):
    found = []
    for p in range(len(parts)):
        chosen = parts[0][...]
        for r in range(1, len(parts)):
            chosen = jnp.where(where[0] == p ^ r, parts[r][...], chosen)
        found.append(chosen)
    return found[0] if len(found) == 1 else jnp.concatenate(found, axis=axis)


def mix_kernel(where, mine_ref, other_ref, query_ref, out_ref, acts):
    half = mine_ref.shape[0]

    @pl.when((pl.program_id(0) == 0) & (pl.program_id(1) == 0))
    def _():
        acts[pl.ds(pl.multiple_of(where[0] * half, half), half), :] = mine_ref[...]
        acts[pl.ds(pl.multiple_of((1 - where[0]) * half, half), half), :] = other_ref[...]

    out_ref[0] = lax.dot_general(
        query_ref[0, 0], acts[...], (((1,), (1,)), ((), ())), preferred_element_type=jnp.float32
    )


def mixed(mine, other, core, queries, flops, tokens=()):
    nq, _, depth, width = queries.shape
    pairs = [block if isinstance(block, tuple) else (block, 0) for block in (mine, other)]
    half = pairs[1][0].shape[0] // (2 if isinstance(other, tuple) else 1)
    tile = depth // 2
    inputs = [(array, pl.BlockSpec((half, width), lambda q, o, where, k=k: (k, 0))) for array, k in pairs]
    inputs.append((queries, pl.BlockSpec((1, 1, tile, width), lambda q, o, where: (q, 0, o, 0))))
    return call(
        mix_kernel, (nq, depth // tile), [core], inputs,
        jax.ShapeDtypeStruct((nq, depth, 2 * half), jnp.float32),
        pl.BlockSpec((1, tile, 2 * half), lambda q, o, where: (q, o, 0)),
        [pltpu.VMEM((2 * half, width), queries.dtype)], flops, tokens,
    )


def score_kernel(where, *refs):
    parts, (mix_ref, out_ref) = refs[:-2], refs[-2:]
    grads = joined(parts, where, 1).astype(jnp.float32)
    for q in range(mix_ref.shape[0]):
        out_ref[q : q + 1, :] = jnp.sum(grads * mix_ref[q], axis=0, keepdims=True)


def scores_of_grads(parts, column, mix, piece, pieces, tokens=(), flops=1024):
    nq, depth, count = mix.shape
    inputs = [(part, pl.BlockSpec(part.shape, lambda i, where: (0, 0))) for part in parts]
    inputs.append((mix, pl.BlockSpec((nq, depth // pieces, count), lambda i, where: (0, piece, 0))))
    return call(
        score_kernel, (1,), [column], inputs, jax.ShapeDtypeStruct((nq, count), jnp.float32),
        pl.BlockSpec((nq, count), lambda i, where: (0, 0)), [], flops, tokens,
    )


def project_kernel(where, *refs):
    parts, (query_ref, out_ref, grads) = refs[:-3], refs[-3:]

    @pl.when((pl.program_id(0) == 0) & (pl.program_id(1) == 0))
    def _():
        grads[...] = joined(parts, where, 0)

    out_ref[0] = jnp.dot(grads[...], query_ref[0, 0], preferred_element_type=jnp.float32)


def projected(parts, column, queries, flops, tokens=()):
    nq, _, depth, width = queries.shape
    count = sum(part.shape[0] for part in parts)
    tile = width // 2
    inputs = [(part, pl.BlockSpec(part.shape, lambda q, i, where: (0, 0))) for part in parts]
    inputs.append((queries, pl.BlockSpec((1, 1, depth, tile), lambda q, i, where: (q, 0, 0, i))))
    return call(
        project_kernel, (nq, width // tile), [column], inputs,
        jax.ShapeDtypeStruct((nq, count, width), jnp.float32),
        pl.BlockSpec((1, count, tile), lambda q, i, where: (q, 0, i)),
        [pltpu.VMEM((count, depth), queries.dtype)], flops, tokens,
    )


def finish_kernel(where, mine_ref, other_ref, proj_ref, out_ref):
    half, width = mine_ref.shape
    swapped = where[0] == 1
    for h, (first, second) in enumerate(((mine_ref, other_ref), (other_ref, mine_ref))):
        acts = jnp.where(swapped, second[...], first[...]).astype(jnp.float32)
        for q in range(proj_ref.shape[0]):
            terms = acts * proj_ref[q, h * half : (h + 1) * half, :]
            lanes = terms[:, :128]
            for at in range(128, width, 128):
                lanes = lanes + terms[:, at : at + 128]
            out_ref[q : q + 1, h * half : (h + 1) * half] = jnp.sum(lanes.T, axis=0, keepdims=True)


def scores_of_acts(mine, other, core, proj, tokens=()):
    nq, count, _ = proj.shape
    inputs = [(block, pl.BlockSpec(block.shape, lambda i, where: (0, 0))) for block in (mine, other)]
    inputs.append((proj, pl.BlockSpec(proj.shape, lambda i, where: (0, 0, 0))))
    return call(
        finish_kernel, (1,), [core], inputs, jax.ShapeDtypeStruct((nq, count), jnp.float32),
        pl.BlockSpec((nq, count), lambda i, where: (0, 0)), [], 1024, tokens,
    )


def on_device(activations, out_grads, queries):
    count, spread = lax.axis_size("dp"), lax.axis_size("din")
    me, column, core = lax.axis_index("dp"), lax.axis_index("din"), lax.axis_index("dout")
    tokens, rows = activations.shape[0], queries.shape[2]
    part, half = tokens // spread, tokens // 2
    pieces = 1

    def to_columns(arrived):
        return [arrived] + [trade(arrived, {"din": r}) for r in range(1, spread)]

    def acts_of(block):
        return block, trade(block, {"dout": 1})

    far, late = count - 1, count - 2
    early = [d for d in range(1, count) if d not in (far, late)]

    mine = lax.dynamic_slice_in_dim(activations, core * half, half, 0)
    hops = [(mine, mine)]
    hops.append(pass_on(hops[0], 1, count))

    def grads_for(device, first, size):
        return lax.dynamic_slice(out_grads, (first, device * rows), (size, rows))

    arrived = {far: trade(grads_for(me ^ far, column * part, part), {"dp": far})}
    others = early + [late]
    sent = turned([grads_for(me ^ d, column * part, part) for d in others], [1] * len(early) + [pieces])
    for d, block in zip(early, sent):
        arrived[d] = trade(block, {"dp": d})

    zero = jnp.zeros((), jnp.int32)
    token = own_mix = mixed((activations, 0), (activations, 1), zero, queries, LONG, list(sent))
    own, = turned([grads_for(me, 0, tokens)], [1])
    token = scores = scores_of_grads([own], zero, own_mix, 0, 1)
    hops[1] = hold(list(hops[1]), [own_mix])
    for step in range(2, count - 1):
        hops.append(pass_on(hops[-1], step, count))

    mixes = {}
    for d in others:
        block = from_partner(hops, me, d, count, [token] + list(arrived.values()) if d == late else [])
        if d == late:
            end = lax.ppermute(block, "dp", [(1, 0), (count - 2, count - 1)])
            hops.append((end, end))
        mixes[d] = mixed(*acts_of(block), core, queries, LONG if d == late else SHORT, [token])
        token = mixes[d]
    tail = [trade(hold([block], [mixes[early[-1]]])[0], {"dp": late}) for block in sent[len(early) :]]
    tail = [hold([block], [token])[0] for block in tail]
    proj = projected(to_columns(arrived[far]), column, queries, LONG, [token, scores] + tail)

    token = proj
    for d in early:
        token = scores_of_grads(to_columns(arrived[d]), column, mixes[d], 0, 1, [token])
        scores = scores + trade(token, {"dp": d})
    token = scores_of_acts(*acts_of(from_partner(hops, me, far, count, [mixes[late]])), core, proj, [token])
    scores = over_chips(scores + trade(token, {"dp": far}), spread)
    for piece, block in enumerate(tail):
        term = scores_of_grads(to_columns(block), column, mixes[late], piece, pieces, [token])
        term = term + trade(term, {"dout": 1})
        scores = scores + sum(trade(term, {"dp": late, "din": r}) for r in range(spread))
    return scores


def over_chips(scores, spread):
    scores = scores + trade(scores, {"dout": 1})
    return scores + sum(trade(scores, {"din": r}) for r in range(1, spread))


def solution(mesh):
    placed = (P(("groups", "dp"), "din"), P(("groups", "dp"), "dout"), P(None, "dout", "dp", "din"))
    return jax.shard_map(
        on_device, mesh=mesh, in_specs=placed, out_specs=P(None, ("groups", "dp")), check_vma=False
    )
```

```python
import functools
import math

import jax
import jax.numpy as jnp
from jax import lax
from jax.experimental import pallas as pl
from jax.experimental.pallas import tpu as pltpu
from jax.sharding import PartitionSpec as P


LONG = 8_000_000_000


def trade(block, steps, backwards=False):
    axes = tuple(steps)
    sizes = [lax.axis_size(axis) for axis in axes]
    mask = 0
    for axis, size in zip(axes, sizes):
        mask = mask * size + steps[axis]
    route = [(i, i ^ mask) for i in range(math.prod(sizes))]
    return lax.ppermute(block, axes, route[::-1] if backwards else route)


ANYWHERE = pl.BlockSpec(memory_space=pl.ANY)


def call(kernel, grid, where, inputs, shape, out_spec, scratch, flops, tokens, vmem=36):
    arrays = [array for array, _ in inputs]
    skip = len(tokens)

    def body(where, *refs):
        kernel(where, *refs[: len(arrays)], *refs[len(arrays) + skip :])

    return pl.pallas_call(
        body,
        grid_spec=pltpu.PrefetchScalarGridSpec(
            num_scalar_prefetch=1,
            grid=grid,
            in_specs=[spec for _, spec in inputs] + [ANYWHERE] * skip,
            out_specs=out_spec,
            scratch_shapes=scratch,
        ),
        out_shape=shape,
        compiler_params=pltpu.CompilerParams(vmem_limit_bytes=vmem * 1024 * 1024),
        cost_estimate=pl.CostEstimate(flops=flops, bytes_accessed=1024, transcendentals=0),
    )(jnp.stack([jnp.asarray(w, jnp.int32) for w in where]), *arrays, *tokens)


def hold(blocks, tokens):
    count = len(blocks)
    return pl.pallas_call(
        lambda *refs: None,
        in_specs=[ANYWHERE] * (count + len(tokens)),
        out_specs=[ANYWHERE] * count,
        out_shape=[jax.ShapeDtypeStruct(block.shape, block.dtype) for block in blocks],
        input_output_aliases={i: i for i in range(count)},
        cost_estimate=pl.CostEstimate(flops=1024, bytes_accessed=1024, transcendentals=0),
    )(*blocks, *tokens)


def joined(parts, where, axis):
    found = []
    for p in range(len(parts)):
        chosen = parts[0][...]
        for r in range(1, len(parts)):
            chosen = jnp.where(where[0] == p ^ r, parts[r][...], chosen)
        found.append(chosen)
    return found[0] if len(found) == 1 else jnp.concatenate(found, axis=axis)


def project_kernel(where, *refs):
    parts, (query_ref, out_ref, grads) = refs[:-3], refs[-3:]

    @pl.when((pl.program_id(0) == 0) & (pl.program_id(1) == 0))
    def _():
        grads[...] = joined(parts, where, 0)

    out_ref[0] = jnp.dot(grads[...], query_ref[0, 0], preferred_element_type=jnp.float32)


def projected(parts, column, queries, flops, tokens=()):
    nq, _, depth, width = queries.shape
    count = sum(part.shape[0] for part in parts)
    tile = width // 2
    inputs = [(part, pl.BlockSpec(part.shape, lambda q, i, where: (0, 0))) for part in parts]
    inputs.append((queries, pl.BlockSpec((1, 1, depth, tile), lambda q, i, where: (q, 0, 0, i))))
    return call(
        project_kernel, (nq, width // tile), [column], inputs,
        jax.ShapeDtypeStruct((nq, count, width), jnp.float32),
        pl.BlockSpec((1, count, tile), lambda q, i, where: (q, 0, i)),
        [pltpu.VMEM((count, depth), queries.dtype)], flops, tokens,
    )


def finish_kernel(where, mine_ref, other_ref, proj_ref, out_ref):
    half, width = mine_ref.shape
    swapped = where[0] == 1
    for h, (first, second) in enumerate(((mine_ref, other_ref), (other_ref, mine_ref))):
        acts = jnp.where(swapped, second[...], first[...]).astype(jnp.float32)
        for q in range(proj_ref.shape[0]):
            terms = acts * proj_ref[q, h * half : (h + 1) * half, :]
            lanes = terms[:, :128]
            for at in range(128, width, 128):
                lanes = lanes + terms[:, at : at + 128]
            out_ref[q : q + 1, h * half : (h + 1) * half] = jnp.sum(lanes.T, axis=0, keepdims=True)


def scores_of_acts(mine, other, core, proj, tokens=()):
    nq, count, _ = proj.shape
    inputs = [(block, pl.BlockSpec(block.shape, lambda i, where: (0, 0))) for block in (mine, other)]
    inputs.append((proj, pl.BlockSpec(proj.shape, lambda i, where: (0, 0, 0))))
    return call(
        finish_kernel, (1,), [core], inputs, jax.ShapeDtypeStruct((nq, count), jnp.float32),
        pl.BlockSpec((nq, count), lambda i, where: (0, 0)), [], 1024, tokens,
    )


def on_device(activations, out_grads, queries):
    count, spread = lax.axis_size("dp"), lax.axis_size("din")
    me, column, core = lax.axis_index("dp"), lax.axis_index("din"), lax.axis_index("dout")
    tokens, rows = activations.shape[0], queries.shape[2]
    part, half = tokens // spread, tokens // 2

    def grads_for(device, first, size):
        return lax.dynamic_slice(out_grads, (first, device * rows), (size, rows))

    steps = list(range(count - 1, 0, -1))
    mine = lax.dynamic_slice_in_dim(activations, core * half, half, 0)
    grads = {d: trade(grads_for(me ^ d, column * part, part), {"dp": d}) for d in steps}
    acts = {d: trade(mine, {"dp": d}) for d in steps}

    zero = jnp.zeros((), jnp.int32)
    proj = {0: projected([grads_for(me, 0, tokens)], zero, queries, LONG)}
    scores = scores_of_acts(activations[:half], activations[half:], zero, proj[0])
    token = proj[0]
    for d in steps:
        sides = [grads[d]] + [trade(grads[d], {"din": r}) for r in range(1, spread)]
        proj[d] = token = projected(sides, column, queries, LONG, [token])

    last = 2 if count > 2 else 1
    for d in sorted(steps, key=lambda d: d == last):
        if d == last:
            scores = over_chips(scores, spread)
            token = scores
        block, = hold([acts[d]], [proj[steps[-1]]])
        term = scores_of_acts(block, trade(block, {"dout": 1}), core, proj[d], [token])
        if d != last:
            scores = scores + trade(term, {"dp": d})
    term = term + trade(term, {"dout": 1})
    return scores + sum(trade(term, {"dp": last, "din": r}) for r in range(spread))


def over_chips(scores, spread):
    scores = scores + trade(scores, {"dout": 1})
    return scores + sum(trade(scores, {"din": r}) for r in range(1, spread))


def solution(mesh):
    placed = (P(("groups", "dp"), "din"), P(("groups", "dp"), "dout"), P(None, "dout", "dp", "din"))
    return jax.shard_map(
        on_device, mesh=mesh, in_specs=placed, out_specs=P(None, ("groups", "dp")), check_vma=False
    )
```

```python
import functools
import math

import jax
import jax.numpy as jnp
from jax import lax
from jax.experimental import pallas as pl
from jax.experimental.pallas import tpu as pltpu
from jax.sharding import PartitionSpec as P


LONG, SHORT = 14_000_000_000, 1_000_000


def trade(block, steps, backwards=False):
    axes = tuple(steps)
    sizes = [lax.axis_size(axis) for axis in axes]
    mask = 0
    for axis, size in zip(axes, sizes):
        mask = mask * size + steps[axis]
    route = [(i, i ^ mask) for i in range(math.prod(sizes))]
    return lax.ppermute(block, axes, route[::-1] if backwards else route)


def pass_on(block, step, count):
    up = lax.ppermute(block[0], "dp", [(i, i + 1) for i in range(step - 1, count - 1)])
    down = lax.ppermute(block[1], "dp", [(i, i - 1) for i in range(1, count - step + 1)])
    return up, down


ANYWHERE = pl.BlockSpec(memory_space=pl.ANY)


def call(kernel, grid, where, inputs, shape, out_spec, scratch, flops, tokens, vmem=36):
    arrays = [array for array, _ in inputs]
    skip = len(tokens)

    def body(where, *refs):
        kernel(where, *refs[: len(arrays)], *refs[len(arrays) + skip :])

    return pl.pallas_call(
        body,
        grid_spec=pltpu.PrefetchScalarGridSpec(
            num_scalar_prefetch=1,
            grid=grid,
            in_specs=[spec for _, spec in inputs] + [ANYWHERE] * skip,
            out_specs=out_spec,
            scratch_shapes=scratch,
        ),
        out_shape=shape,
        compiler_params=pltpu.CompilerParams(vmem_limit_bytes=vmem * 1024 * 1024),
        cost_estimate=pl.CostEstimate(flops=flops, bytes_accessed=1024, transcendentals=0),
    )(jnp.stack([jnp.asarray(w, jnp.int32) for w in where]), *arrays, *tokens)


def hold(blocks, tokens):
    count = len(blocks)
    return pl.pallas_call(
        lambda *refs: None,
        in_specs=[ANYWHERE] * (count + len(tokens)),
        out_specs=[ANYWHERE] * count,
        out_shape=[jax.ShapeDtypeStruct(block.shape, block.dtype) for block in blocks],
        input_output_aliases={i: i for i in range(count)},
        cost_estimate=pl.CostEstimate(flops=1024, bytes_accessed=1024, transcendentals=0),
    )(*blocks, *tokens)


def turn_kernel(pieces, where, *refs):
    blocks, outs = refs[: len(pieces)], list(refs[len(pieces) :])
    for block, number in zip(blocks, pieces):
        turned = block[...].astype(jnp.float32).T.astype(block.dtype)
        size = turned.shape[0] // number
        for p in range(number):
            outs.pop(0)[...] = turned[p * size : (p + 1) * size]


def turned(blocks, pieces, tokens=()):
    rows, width = blocks[0].shape
    if rows % 128 or width % 128:
        return [piece for block, number in zip(blocks, pieces) for piece in jnp.split(block.T, number)]
    sizes = [width // number for number in pieces for _ in range(number)]
    return call(
        functools.partial(turn_kernel, pieces), (1,), [jnp.zeros((), jnp.int32)],
        [(block, pl.BlockSpec(block.shape, lambda i, where: (0, 0))) for block in blocks],
        [jax.ShapeDtypeStruct((size, rows), blocks[0].dtype) for size in sizes],
        [pl.BlockSpec((size, rows), lambda i, where: (0, 0)) for size in sizes], [], 1024, tokens,
    )


def pick_kernel(where, *refs):
    *blocks, out_ref = refs
    for k, block in enumerate(blocks):

        @pl.when(where[0] == k)
        def _():
            out_ref[...] = block[...]


def from_partner(hops, me, d, count, tokens=()):
    sources, choice = [], []
    for z in range(count):
        away = z - (z ^ d)
        source = (abs(away), int(away < 0))
        if source not in sources:
            sources.append(source)
        choice.append(sources.index(source))
    where = functools.reduce(lambda found, z: jnp.where(me == z, choice[z], found), range(count), 0)
    blocks = [hops[step][way] for step, way in sources]
    spec = pl.BlockSpec(blocks[0].shape, lambda i, where: (0, 0))
    return call(
        pick_kernel, (1,), [where], [(block, spec) for block in blocks],
        jax.ShapeDtypeStruct(blocks[0].shape, blocks[0].dtype), spec, [], 1024, tokens,
    )


def joined(parts, where, axis):
    found = []
    for p in range(len(parts)):
        chosen = parts[0][...]
        for r in range(1, len(parts)):
            chosen = jnp.where(where[0] == p ^ r, parts[r][...], chosen)
        found.append(chosen)
    return found[0] if len(found) == 1 else jnp.concatenate(found, axis=axis)


def mix_kernel(where, mine_ref, other_ref, query_ref, out_ref, acts):
    half = mine_ref.shape[0]

    @pl.when((pl.program_id(0) == 0) & (pl.program_id(1) == 0))
    def _():
        acts[pl.ds(pl.multiple_of(where[0] * half, half), half), :] = mine_ref[...]
        acts[pl.ds(pl.multiple_of((1 - where[0]) * half, half), half), :] = other_ref[...]

    out_ref[0] = lax.dot_general(
        query_ref[0, 0], acts[...], (((1,), (1,)), ((), ())), preferred_element_type=jnp.float32
    )


def mixed(mine, other, core, queries, flops, tokens=()):
    nq, _, depth, width = queries.shape
    pairs = [block if isinstance(block, tuple) else (block, 0) for block in (mine, other)]
    half = pairs[1][0].shape[0] // (2 if isinstance(other, tuple) else 1)
    tile = depth // 2
    inputs = [(array, pl.BlockSpec((half, width), lambda q, o, where, k=k: (k, 0))) for array, k in pairs]
    inputs.append((queries, pl.BlockSpec((1, 1, tile, width), lambda q, o, where: (q, 0, o, 0))))
    return call(
        mix_kernel, (nq, depth // tile), [core], inputs,
        jax.ShapeDtypeStruct((nq, depth, 2 * half), jnp.float32),
        pl.BlockSpec((1, tile, 2 * half), lambda q, o, where: (q, o, 0)),
        [pltpu.VMEM((2 * half, width), queries.dtype)], flops, tokens,
    )


def score_kernel(where, *refs):
    parts, (mix_ref, out_ref) = refs[:-2], refs[-2:]
    grads = joined(parts, where, 1).astype(jnp.float32)
    for q in range(mix_ref.shape[0]):
        out_ref[q : q + 1, :] = jnp.sum(grads * mix_ref[q], axis=0, keepdims=True)


def scores_of_grads(parts, column, mix, piece, pieces, tokens=(), flops=1024):
    nq, depth, count = mix.shape
    inputs = [(part, pl.BlockSpec(part.shape, lambda i, where: (0, 0))) for part in parts]
    inputs.append((mix, pl.BlockSpec((nq, depth // pieces, count), lambda i, where: (0, piece, 0))))
    return call(
        score_kernel, (1,), [column], inputs, jax.ShapeDtypeStruct((nq, count), jnp.float32),
        pl.BlockSpec((nq, count), lambda i, where: (0, 0)), [], flops, tokens,
    )


def project_kernel(where, *refs):
    parts, (query_ref, out_ref, grads) = refs[:-3], refs[-3:]

    @pl.when((pl.program_id(0) == 0) & (pl.program_id(1) == 0))
    def _():
        grads[...] = joined(parts, where, 0)

    out_ref[0] = jnp.dot(grads[...], query_ref[0, 0], preferred_element_type=jnp.float32)


def projected(parts, column, queries, flops, tokens=()):
    nq, _, depth, width = queries.shape
    count = sum(part.shape[0] for part in parts)
    tile = width // 2
    inputs = [(part, pl.BlockSpec(part.shape, lambda q, i, where: (0, 0))) for part in parts]
    inputs.append((queries, pl.BlockSpec((1, 1, depth, tile), lambda q, i, where: (q, 0, 0, i))))
    return call(
        project_kernel, (nq, width // tile), [column], inputs,
        jax.ShapeDtypeStruct((nq, count, width), jnp.float32),
        pl.BlockSpec((1, count, tile), lambda q, i, where: (q, 0, i)),
        [pltpu.VMEM((count, depth), queries.dtype)], flops, tokens,
    )


def finish_kernel(where, mine_ref, other_ref, proj_ref, out_ref):
    half, width = mine_ref.shape
    swapped = where[0] == 1
    for h, (first, second) in enumerate(((mine_ref, other_ref), (other_ref, mine_ref))):
        acts = jnp.where(swapped, second[...], first[...]).astype(jnp.float32)
        for q in range(proj_ref.shape[0]):
            terms = acts * proj_ref[q, h * half : (h + 1) * half, :]
            lanes = terms[:, :128]
            for at in range(128, width, 128):
                lanes = lanes + terms[:, at : at + 128]
            out_ref[q : q + 1, h * half : (h + 1) * half] = jnp.sum(lanes.T, axis=0, keepdims=True)


def scores_of_acts(mine, other, core, proj, tokens=()):
    nq, count, _ = proj.shape
    inputs = [(block, pl.BlockSpec(block.shape, lambda i, where: (0, 0))) for block in (mine, other)]
    inputs.append((proj, pl.BlockSpec(proj.shape, lambda i, where: (0, 0, 0))))
    return call(
        finish_kernel, (1,), [core], inputs, jax.ShapeDtypeStruct((nq, count), jnp.float32),
        pl.BlockSpec((nq, count), lambda i, where: (0, 0)), [], 1024, tokens,
    )


def on_device(activations, out_grads, queries):
    count, spread = lax.axis_size("dp"), lax.axis_size("din")
    me, column, core = lax.axis_index("dp"), lax.axis_index("din"), lax.axis_index("dout")
    tokens, rows = activations.shape[0], queries.shape[2]
    part, half = tokens // spread, tokens // 2

    def to_columns(arrived):
        return [arrived] + [trade(arrived, {"din": r}) for r in range(1, spread)]

    def acts_of(block):
        return block, trade(block, {"dout": 1})

    far, late = count - 1, count - 2
    early = list(range(1, late))

    mine = lax.dynamic_slice_in_dim(activations, core * half, half, 0)
    hops = [(mine, mine)]
    hops.append(pass_on(hops[0], 1, count))

    def grads_for(device, first, size):
        return lax.dynamic_slice(out_grads, (first, device * rows), (size, rows))

    sent = turned([grads_for(me ^ d, column * part, part) for d in early + [late]], [1] * (len(early) + 1))
    sent = [*sent, grads_for(me ^ far, column * part, part)]
    arrived = {d: trade(block, {"dp": d}) for d, block in zip(early + [late, far], sent)}

    zero = jnp.zeros((), jnp.int32)
    mix = mixed((activations, 0), (activations, 1), zero, queries, SHORT, sent)
    own, = turned([grads_for(me, 0, tokens)], [1])
    token = scores = scores_of_grads([own], zero, mix, 0, 1)
    hops[1] = hold(list(hops[1]), [mix])
    for step in range(2, count - 1):
        hops.append(pass_on(hops[-1], step, count))

    mixes = {}
    for d in early:
        mixes[d] = token = mixed(*acts_of(from_partner(hops, me, d, count)), core, queries, SHORT, [token])
    sides = to_columns(hold([arrived[far]], list(hops[1]))[0])
    proj = projected(sides, column, queries, SHORT, [token])
    token = proj
    for d in early:
        sides = to_columns(hold([arrived[d]], list(hops[1]))[0])
        token = scores_of_grads(sides, column, mixes[d], 0, 1, [token])
        scores = scores + trade(token, {"dp": d})
    scores = over_chips(scores, spread)

    block = from_partner(hops, me, late, count, [token])
    end = lax.ppermute(block, "dp", [(1, 0), (count - 2, count - 1)])
    hops.append((end, end))
    sides = to_columns(hold([arrived[late]], [proj])[0])
    mix = mixed(*acts_of(block), core, queries, SHORT, [scores])
    sides = sides[:1] + list(hold(sides[1:], [mix]))
    near = trade(scores_of_grads(sides, column, mix, 0, 1, (), LONG), {"dp": late})
    block = from_partner(hops, me, far, count, [mix])
    total = near + trade(scores_of_acts(*acts_of(block), core, proj), {"dp": far})
    return scores + over_chips(total, spread)


def over_chips(scores, spread):
    scores = scores + trade(scores, {"dout": 1})
    return scores + sum(trade(scores, {"din": r}) for r in range(1, spread))


def solution(mesh):
    placed = (P(("groups", "dp"), "din"), P(("groups", "dp"), "dout"), P(None, "dout", "dp", "din"))
    return jax.shard_map(
        on_device, mesh=mesh, in_specs=placed, out_specs=P(None, ("groups", "dp")), check_vma=False
    )
```

```python
import functools
import math

import jax
import jax.numpy as jnp
from jax import lax
from jax.experimental import pallas as pl
from jax.experimental.pallas import tpu as pltpu
from jax.sharding import PartitionSpec as P


LONG, SHORT = 14_000_000_000, 1_000_000


def trade(block, steps, backwards=False):
    axes = tuple(steps)
    sizes = [lax.axis_size(axis) for axis in axes]
    mask = 0
    for axis, size in zip(axes, sizes):
        mask = mask * size + steps[axis]
    route = [(i, i ^ mask) for i in range(math.prod(sizes))]
    return lax.ppermute(block, axes, route[::-1] if backwards else route)


def pass_on(block, step, count):
    up = lax.ppermute(block[0], "dp", [(i, i + 1) for i in range(step - 1, count - 1)])
    down = lax.ppermute(block[1], "dp", [(i, i - 1) for i in range(1, count - step + 1)])
    return up, down


ANYWHERE = pl.BlockSpec(memory_space=pl.ANY)


def call(kernel, grid, where, inputs, shape, out_spec, scratch, flops, tokens, vmem=36):
    arrays = [array for array, _ in inputs]
    skip = len(tokens)

    def body(where, *refs):
        kernel(where, *refs[: len(arrays)], *refs[len(arrays) + skip :])

    return pl.pallas_call(
        body,
        grid_spec=pltpu.PrefetchScalarGridSpec(
            num_scalar_prefetch=1,
            grid=grid,
            in_specs=[spec for _, spec in inputs] + [ANYWHERE] * skip,
            out_specs=out_spec,
            scratch_shapes=scratch,
        ),
        out_shape=shape,
        compiler_params=pltpu.CompilerParams(vmem_limit_bytes=vmem * 1024 * 1024),
        cost_estimate=pl.CostEstimate(flops=flops, bytes_accessed=1024, transcendentals=0),
    )(jnp.stack([jnp.asarray(w, jnp.int32) for w in where]), *arrays, *tokens)


def hold(blocks, tokens):
    count = len(blocks)
    return pl.pallas_call(
        lambda *refs: None,
        in_specs=[ANYWHERE] * (count + len(tokens)),
        out_specs=[ANYWHERE] * count,
        out_shape=[jax.ShapeDtypeStruct(block.shape, block.dtype) for block in blocks],
        input_output_aliases={i: i for i in range(count)},
        cost_estimate=pl.CostEstimate(flops=1024, bytes_accessed=1024, transcendentals=0),
    )(*blocks, *tokens)


def turn_kernel(pieces, where, *refs):
    blocks, outs = refs[: len(pieces)], list(refs[len(pieces) :])
    for block, number in zip(blocks, pieces):
        turned = block[...].astype(jnp.float32).T.astype(block.dtype)
        size = turned.shape[0] // number
        for p in range(number):
            outs.pop(0)[...] = turned[p * size : (p + 1) * size]


def turned(blocks, pieces, tokens=()):
    rows, width = blocks[0].shape
    if rows % 128 or width % 128:
        return [piece for block, number in zip(blocks, pieces) for piece in jnp.split(block.T, number)]
    sizes = [width // number for number in pieces for _ in range(number)]
    return call(
        functools.partial(turn_kernel, pieces), (1,), [jnp.zeros((), jnp.int32)],
        [(block, pl.BlockSpec(block.shape, lambda i, where: (0, 0))) for block in blocks],
        [jax.ShapeDtypeStruct((size, rows), blocks[0].dtype) for size in sizes],
        [pl.BlockSpec((size, rows), lambda i, where: (0, 0)) for size in sizes], [], 1024, tokens,
    )


def pick_kernel(where, *refs):
    *blocks, out_ref = refs
    for k, block in enumerate(blocks):

        @pl.when(where[0] == k)
        def _():
            out_ref[...] = block[...]


def from_partner(hops, me, d, count, tokens=()):
    sources, choice = [], []
    for z in range(count):
        away = z - (z ^ d)
        source = (abs(away), int(away < 0))
        if source not in sources:
            sources.append(source)
        choice.append(sources.index(source))
    where = functools.reduce(lambda found, z: jnp.where(me == z, choice[z], found), range(count), 0)
    blocks = [hops[step][way] for step, way in sources]
    spec = pl.BlockSpec(blocks[0].shape, lambda i, where: (0, 0))
    return call(
        pick_kernel, (1,), [where], [(block, spec) for block in blocks],
        jax.ShapeDtypeStruct(blocks[0].shape, blocks[0].dtype), spec, [], 1024, tokens,
    )


def joined(parts, where, axis):
    found = []
    for p in range(len(parts)):
        chosen = parts[0][...]
        for r in range(1, len(parts)):
            chosen = jnp.where(where[0] == p ^ r, parts[r][...], chosen)
        found.append(chosen)
    return found[0] if len(found) == 1 else jnp.concatenate(found, axis=axis)


def mix_kernel(where, mine_ref, other_ref, query_ref, out_ref, acts):
    half = mine_ref.shape[0]

    @pl.when((pl.program_id(0) == 0) & (pl.program_id(1) == 0))
    def _():
        acts[pl.ds(pl.multiple_of(where[0] * half, half), half), :] = mine_ref[...]
        acts[pl.ds(pl.multiple_of((1 - where[0]) * half, half), half), :] = other_ref[...]

    out_ref[0] = lax.dot_general(
        query_ref[0, 0], acts[...], (((1,), (1,)), ((), ())), preferred_element_type=jnp.float32
    )


def mixed(mine, other, core, queries, flops, tokens=()):
    nq, _, depth, width = queries.shape
    pairs = [block if isinstance(block, tuple) else (block, 0) for block in (mine, other)]
    half = pairs[1][0].shape[0] // (2 if isinstance(other, tuple) else 1)
    tile = depth // 2
    inputs = [(array, pl.BlockSpec((half, width), lambda q, o, where, k=k: (k, 0))) for array, k in pairs]
    inputs.append((queries, pl.BlockSpec((1, 1, tile, width), lambda q, o, where: (q, 0, o, 0))))
    return call(
        mix_kernel, (nq, depth // tile), [core], inputs,
        jax.ShapeDtypeStruct((nq, depth, 2 * half), jnp.float32),
        pl.BlockSpec((1, tile, 2 * half), lambda q, o, where: (q, o, 0)),
        [pltpu.VMEM((2 * half, width), queries.dtype)], flops, tokens,
    )


def score_kernel(where, *refs):
    parts, (mix_ref, out_ref) = refs[:-2], refs[-2:]
    grads = joined(parts, where, 1).astype(jnp.float32)
    for q in range(mix_ref.shape[0]):
        out_ref[q : q + 1, :] = jnp.sum(grads * mix_ref[q], axis=0, keepdims=True)


def scores_of_grads(parts, column, mix, piece, pieces, tokens=(), flops=1024):
    nq, depth, count = mix.shape
    inputs = [(part, pl.BlockSpec(part.shape, lambda i, where: (0, 0))) for part in parts]
    inputs.append((mix, pl.BlockSpec((nq, depth // pieces, count), lambda i, where: (0, piece, 0))))
    return call(
        score_kernel, (1,), [column], inputs, jax.ShapeDtypeStruct((nq, count), jnp.float32),
        pl.BlockSpec((nq, count), lambda i, where: (0, 0)), [], flops, tokens,
    )


def project_kernel(where, *refs):
    parts, (query_ref, out_ref, grads) = refs[:-3], refs[-3:]

    @pl.when((pl.program_id(0) == 0) & (pl.program_id(1) == 0))
    def _():
        grads[...] = joined(parts, where, 0)

    out_ref[0] = jnp.dot(grads[...], query_ref[0, 0], preferred_element_type=jnp.float32)


def projected(parts, column, queries, flops, tokens=()):
    nq, _, depth, width = queries.shape
    count = sum(part.shape[0] for part in parts)
    tile = width // 2
    inputs = [(part, pl.BlockSpec(part.shape, lambda q, i, where: (0, 0))) for part in parts]
    inputs.append((queries, pl.BlockSpec((1, 1, depth, tile), lambda q, i, where: (q, 0, 0, i))))
    return call(
        project_kernel, (nq, width // tile), [column], inputs,
        jax.ShapeDtypeStruct((nq, count, width), jnp.float32),
        pl.BlockSpec((1, count, tile), lambda q, i, where: (q, 0, i)),
        [pltpu.VMEM((count, depth), queries.dtype)], flops, tokens,
    )


def finish_kernel(where, mine_ref, other_ref, proj_ref, out_ref):
    half, width = mine_ref.shape
    swapped = where[0] == 1
    for h, (first, second) in enumerate(((mine_ref, other_ref), (other_ref, mine_ref))):
        acts = jnp.where(swapped, second[...], first[...]).astype(jnp.float32)
        for q in range(proj_ref.shape[0]):
            terms = acts * proj_ref[q, h * half : (h + 1) * half, :]
            lanes = terms[:, :128]
            for at in range(128, width, 128):
                lanes = lanes + terms[:, at : at + 128]
            out_ref[q : q + 1, h * half : (h + 1) * half] = jnp.sum(lanes.T, axis=0, keepdims=True)


def scores_of_acts(mine, other, core, proj, tokens=()):
    nq, count, _ = proj.shape
    inputs = [(block, pl.BlockSpec(block.shape, lambda i, where: (0, 0))) for block in (mine, other)]
    inputs.append((proj, pl.BlockSpec(proj.shape, lambda i, where: (0, 0, 0))))
    return call(
        finish_kernel, (1,), [core], inputs, jax.ShapeDtypeStruct((nq, count), jnp.float32),
        pl.BlockSpec((nq, count), lambda i, where: (0, 0)), [], 1024, tokens,
    )


def on_device(activations, out_grads, queries):
    count, spread = lax.axis_size("dp"), lax.axis_size("din")
    me, column, core = lax.axis_index("dp"), lax.axis_index("din"), lax.axis_index("dout")
    tokens, rows = activations.shape[0], queries.shape[2]
    part, half = tokens // spread, tokens // 2

    def to_columns(arrived):
        return [arrived] + [trade(arrived, {"din": r}) for r in range(1, spread)]

    def acts_of(block):
        return block, trade(block, {"dout": 1})

    far, late = count - 1, count - 2
    early = list(range(1, late))

    mine = lax.dynamic_slice_in_dim(activations, core * half, half, 0)
    hops = [(mine, mine)]
    hops.append(pass_on(hops[0], 1, count))

    def grads_for(device, first, size):
        return lax.dynamic_slice(out_grads, (first, device * rows), (size, rows))

    sent = turned([grads_for(me ^ d, column * part, part) for d in early + [late]], [1] * (len(early) + 1))
    sent = [*sent, grads_for(me ^ far, column * part, part)]
    arrived = {d: trade(block, {"dp": d}) for d, block in zip(early + [late, far], sent)}

    zero = jnp.zeros((), jnp.int32)
    mix = mixed((activations, 0), (activations, 1), zero, queries, SHORT, sent)
    own, = turned([grads_for(me, 0, tokens)], [1])
    token = scores = scores_of_grads([own], zero, mix, 0, 1)
    hops[1] = hold(list(hops[1]), [mix])
    for step in range(2, count - 1):
        hops.append(pass_on(hops[-1], step, count))

    mixes = {}
    for d in early:
        mixes[d] = token = mixed(*acts_of(from_partner(hops, me, d, count)), core, queries, SHORT, [token])
    sides = to_columns(hold([arrived[far]], list(hops[1]))[0])
    proj = projected(sides, column, queries, SHORT, [token])
    token = proj
    for d in early:
        sides = to_columns(hold([arrived[d]], list(hops[1]))[0])
        token = scores_of_grads(sides, column, mixes[d], 0, 1, [token])
        scores = scores + trade(token, {"dp": d})

    block = from_partner(hops, me, late, count, [token])
    end = lax.ppermute(block, "dp", [(1, 0), (count - 2, count - 1)])
    hops.append((end, end))
    sides = to_columns(hold([arrived[late]], [proj])[0])
    mix = mixed(*acts_of(block), core, queries, SHORT, [token])
    sides = sides[:1] + list(hold(sides[1:], [mix]))
    near = trade(scores_of_grads(sides, column, mix, 0, 1, (), LONG), {"dp": late})
    block = from_partner(hops, me, far, count, [mix])
    scores = scores + near + trade(scores_of_acts(*acts_of(block), core, proj), {"dp": far})
    return over_chips(scores, spread)


def over_chips(scores, spread):
    scores = scores + trade(scores, {"dout": 1})
    return scores + sum(trade(scores, {"din": r}) for r in range(1, spread))


def solution(mesh):
    placed = (P(("groups", "dp"), "din"), P(("groups", "dp"), "dout"), P(None, "dout", "dp", "din"))
    return jax.shard_map(
        on_device, mesh=mesh, in_specs=placed, out_specs=P(None, ("groups", "dp")), check_vma=False
    )
```

```python
import functools
import math

import jax
import jax.numpy as jnp
from jax import lax
from jax.experimental import pallas as pl
from jax.experimental.pallas import tpu as pltpu
from jax.sharding import PartitionSpec as P


LONG, SHORT = 14_000_000_000, 1_000_000


def trade(block, steps, backwards=False):
    axes = tuple(steps)
    sizes = [lax.axis_size(axis) for axis in axes]
    mask = 0
    for axis, size in zip(axes, sizes):
        mask = mask * size + steps[axis]
    route = [(i, i ^ mask) for i in range(math.prod(sizes))]
    return lax.ppermute(block, axes, route[::-1] if backwards else route)


def pass_on(block, step, count):
    up = lax.ppermute(block[0], "dp", [(i, i + 1) for i in range(step - 1, count - 1)])
    down = lax.ppermute(block[1], "dp", [(i, i - 1) for i in range(1, count - step + 1)])
    return up, down


ANYWHERE = pl.BlockSpec(memory_space=pl.ANY)


def call(kernel, grid, where, inputs, shape, out_spec, scratch, flops, tokens, vmem=20):
    arrays = [array for array, _ in inputs]
    skip = len(tokens)

    def body(where, *refs):
        kernel(where, *refs[: len(arrays)], *refs[len(arrays) + skip :])

    return pl.pallas_call(
        body,
        grid_spec=pltpu.PrefetchScalarGridSpec(
            num_scalar_prefetch=1,
            grid=grid,
            in_specs=[spec for _, spec in inputs] + [ANYWHERE] * skip,
            out_specs=out_spec,
            scratch_shapes=scratch,
        ),
        out_shape=shape,
        compiler_params=pltpu.CompilerParams(vmem_limit_bytes=vmem * 1024 * 1024),
        cost_estimate=pl.CostEstimate(flops=flops, bytes_accessed=1024, transcendentals=0),
    )(jnp.stack([jnp.asarray(w, jnp.int32) for w in where]), *arrays, *tokens)


def hold(blocks, tokens):
    count = len(blocks)
    return pl.pallas_call(
        lambda *refs: None,
        in_specs=[ANYWHERE] * (count + len(tokens)),
        out_specs=[ANYWHERE] * count,
        out_shape=[jax.ShapeDtypeStruct(block.shape, block.dtype) for block in blocks],
        input_output_aliases={i: i for i in range(count)},
        compiler_params=pltpu.CompilerParams(vmem_limit_bytes=1024 * 1024),
        cost_estimate=pl.CostEstimate(flops=1024, bytes_accessed=1024, transcendentals=0),
    )(*blocks, *tokens)


def turn_kernel(pieces, where, *refs):
    blocks, outs = refs[: len(pieces)], list(refs[len(pieces) :])
    for block, number in zip(blocks, pieces):
        turned = block[...].astype(jnp.float32).T.astype(block.dtype)
        size = turned.shape[0] // number
        for p in range(number):
            outs.pop(0)[...] = turned[p * size : (p + 1) * size]


def turned(blocks, pieces, tokens=()):
    rows, width = blocks[0].shape
    if rows % 128 or width % 128:
        return [piece for block, number in zip(blocks, pieces) for piece in jnp.split(block.T, number)]
    sizes = [width // number for number in pieces for _ in range(number)]
    return call(
        functools.partial(turn_kernel, pieces), (1,), [jnp.zeros((), jnp.int32)],
        [(block, pl.BlockSpec(block.shape, lambda i, where: (0, 0))) for block in blocks],
        [jax.ShapeDtypeStruct((size, rows), blocks[0].dtype) for size in sizes],
        [pl.BlockSpec((size, rows), lambda i, where: (0, 0)) for size in sizes], [], 1024, tokens,
    )


def pick_kernel(where, *refs):
    *blocks, out_ref = refs
    for k, block in enumerate(blocks):

        @pl.when(where[0] == k)
        def _():
            out_ref[...] = block[...]


def from_partner(hops, me, d, count, tokens=()):
    sources, choice = [], []
    for z in range(count):
        away = z - (z ^ d)
        source = (abs(away), int(away < 0))
        if source not in sources:
            sources.append(source)
        choice.append(sources.index(source))
    where = functools.reduce(lambda found, z: jnp.where(me == z, choice[z], found), range(count), 0)
    blocks = [hops[step][way] for step, way in sources]
    spec = pl.BlockSpec(blocks[0].shape, lambda i, where: (0, 0))
    return call(
        pick_kernel, (1,), [where], [(block, spec) for block in blocks],
        jax.ShapeDtypeStruct(blocks[0].shape, blocks[0].dtype), spec, [], 1024, tokens,
    )


def joined(parts, where, axis):
    found = []
    for p in range(len(parts)):
        chosen = parts[0][...]
        for r in range(1, len(parts)):
            chosen = jnp.where(where[0] == p ^ r, parts[r][...], chosen)
        found.append(chosen)
    return found[0] if len(found) == 1 else jnp.concatenate(found, axis=axis)


MARK = jax.ShapeDtypeStruct((8, 128), jnp.float32), pl.BlockSpec((8, 128), lambda *at: (0, 0))


def mix_kernel(where, mine_ref, other_ref, query_ref, out_ref, mark_ref, acts):
    half = mine_ref.shape[0]
    mark_ref[...] = jnp.zeros_like(mark_ref)

    @pl.when((pl.program_id(0) == 0) & (pl.program_id(1) == 0))
    def _():
        acts[pl.ds(pl.multiple_of(where[0] * half, half), half), :] = mine_ref[...]
        acts[pl.ds(pl.multiple_of((1 - where[0]) * half, half), half), :] = other_ref[...]

    out_ref[0] = lax.dot_general(
        query_ref[0, 0], acts[...], (((1,), (1,)), ((), ())), preferred_element_type=jnp.float32
    )


def mixed(mine, other, core, queries, flops, tokens=()):
    nq, _, depth, width = queries.shape
    pairs = [block if isinstance(block, tuple) else (block, 0) for block in (mine, other)]
    half = pairs[1][0].shape[0] // (2 if isinstance(other, tuple) else 1)
    tile = depth // 2
    inputs = [(array, pl.BlockSpec((half, width), lambda q, o, where, k=k: (k, 0))) for array, k in pairs]
    inputs.append((queries, pl.BlockSpec((1, 1, tile, width), lambda q, o, where: (q, 0, o, 0))))
    return call(
        mix_kernel, (nq, depth // tile), [core], inputs,
        [jax.ShapeDtypeStruct((nq, depth, 2 * half), jnp.float32), MARK[0]],
        [pl.BlockSpec((1, tile, 2 * half), lambda q, o, where: (q, o, 0)), MARK[1]],
        [pltpu.VMEM((2 * half, width), queries.dtype)], flops, tokens,
    )


def score_kernel(where, *refs):
    parts, (mix_ref, out_ref) = refs[:-2], refs[-2:]
    grads = joined(parts, where, 1).astype(jnp.float32)
    for q in range(mix_ref.shape[0]):
        out_ref[q : q + 1, :] = jnp.sum(grads * mix_ref[q], axis=0, keepdims=True)


def scores_of_grads(parts, column, mix, piece, pieces, tokens=(), flops=1024):
    nq, depth, count = mix.shape
    inputs = [(part, pl.BlockSpec(part.shape, lambda i, where: (0, 0))) for part in parts]
    inputs.append((mix, pl.BlockSpec((nq, depth // pieces, count), lambda i, where: (0, piece, 0))))
    return call(
        score_kernel, (1,), [column], inputs, jax.ShapeDtypeStruct((nq, count), jnp.float32),
        pl.BlockSpec((nq, count), lambda i, where: (0, 0)), [], flops, tokens,
    )


def project_kernel(where, *refs):
    parts, (query_ref, out_ref, mark_ref, grads) = refs[:-4], refs[-4:]
    mark_ref[...] = jnp.zeros_like(mark_ref)

    @pl.when((pl.program_id(0) == 0) & (pl.program_id(1) == 0))
    def _():
        grads[...] = joined(parts, where, 0)

    out_ref[0] = jnp.dot(grads[...], query_ref[0, 0], preferred_element_type=jnp.float32)


def projected(parts, column, queries, flops, tokens=()):
    nq, _, depth, width = queries.shape
    count = sum(part.shape[0] for part in parts)
    tile = width // 2
    inputs = [(part, pl.BlockSpec(part.shape, lambda q, i, where: (0, 0))) for part in parts]
    inputs.append((queries, pl.BlockSpec((1, 1, depth, tile), lambda q, i, where: (q, 0, 0, i))))
    return call(
        project_kernel, (nq, width // tile), [column], inputs,
        [jax.ShapeDtypeStruct((nq, count, width), jnp.float32), MARK[0]],
        [pl.BlockSpec((1, count, tile), lambda q, i, where: (q, 0, i)), MARK[1]],
        [pltpu.VMEM((count, depth), queries.dtype)], flops, tokens,
    )


def finish_kernel(where, mine_ref, other_ref, proj_ref, out_ref):
    half, width = mine_ref.shape
    swapped = where[0] == 1
    for h, (first, second) in enumerate(((mine_ref, other_ref), (other_ref, mine_ref))):
        acts = jnp.where(swapped, second[...], first[...]).astype(jnp.float32)
        for q in range(proj_ref.shape[0]):
            terms = acts * proj_ref[q, h * half : (h + 1) * half, :]
            lanes = terms[:, :128]
            for at in range(128, width, 128):
                lanes = lanes + terms[:, at : at + 128]
            out_ref[q : q + 1, h * half : (h + 1) * half] = jnp.sum(lanes.T, axis=0, keepdims=True)


def scores_of_acts(mine, other, core, proj, tokens=()):
    nq, count, _ = proj.shape
    inputs = [(block, pl.BlockSpec(block.shape, lambda i, where: (0, 0))) for block in (mine, other)]
    inputs.append((proj, pl.BlockSpec(proj.shape, lambda i, where: (0, 0, 0))))
    return call(
        finish_kernel, (1,), [core], inputs, jax.ShapeDtypeStruct((nq, count), jnp.float32),
        pl.BlockSpec((nq, count), lambda i, where: (0, 0)), [], 1024, tokens,
    )


def on_device(activations, out_grads, queries):
    count, spread = lax.axis_size("dp"), lax.axis_size("din")
    me, column, core = lax.axis_index("dp"), lax.axis_index("din"), lax.axis_index("dout")
    tokens, rows = activations.shape[0], queries.shape[2]
    part, half = tokens // spread, tokens // 2

    def to_columns(arrived):
        return [arrived] + [trade(arrived, {"din": r}) for r in range(1, spread)]

    def acts_of(block):
        return block, trade(block, {"dout": 1})

    far, late = count - 1, count - 2
    early = list(range(1, late))

    mine = lax.dynamic_slice_in_dim(activations, core * half, half, 0)
    hops = [(mine, mine)]
    hops.append(pass_on(hops[0], 1, count))

    def grads_for(device, first, size):
        return lax.dynamic_slice(out_grads, (first, device * rows), (size, rows))

    sent = turned([grads_for(me ^ d, column * part, part) for d in early + [late]], [1] * (len(early) + 1))
    sent = [*sent, grads_for(me ^ far, column * part, part)]
    arrived = {d: trade(block, {"dp": d}) for d, block in zip(early + [late, far], sent)}

    zero = jnp.zeros((), jnp.int32)
    mix, token = mixed((activations, 0), (activations, 1), zero, queries, SHORT, sent)
    own, = turned([grads_for(me, 0, tokens)], [1])
    scores = scores_of_grads([own], zero, mix, 0, 1)
    hops[1] = hold(list(hops[1]), [token])
    for step in range(2, count - 1):
        hops.append(pass_on(hops[-1], step, count))

    mixes, token = {}, scores
    for d in early:
        mixes[d], token = mixed(*acts_of(from_partner(hops, me, d, count)), core, queries, SHORT, [token])
    sides = to_columns(hold([arrived[far]], hops[1])[0])
    block = from_partner(hops, me, late, count, [token] + sides)
    end = lax.ppermute(block, "dp", [(1, 0), (count - 2, count - 1)])
    hops.append((end, end))

    proj, token = projected(sides, column, queries, SHORT, [token])
    for d in early:
        sides = to_columns(hold([arrived[d]], hops[1])[0])
        token = scores_of_grads(sides, column, mixes[d], 0, 1, [token])
        scores = scores + trade(token, {"dp": d})

    sides = to_columns(hold([arrived[late]], [token])[0])
    mix, token = mixed(*acts_of(block), core, queries, SHORT, [token])
    sides = sides[:1] + list(hold(sides[1:], [token]))
    near = trade(scores_of_grads(sides, column, mix, 0, 1, (), LONG), {"dp": late})
    block = from_partner(hops, me, far, count, [token])
    scores = scores + near + trade(scores_of_acts(*acts_of(block), core, proj), {"dp": far})
    return over_chips(scores, spread)


def over_chips(scores, spread):
    scores = scores + trade(scores, {"dout": 1})
    return scores + sum(trade(scores, {"din": r}) for r in range(1, spread))


def solution(mesh):
    placed = (P(("groups", "dp"), "din"), P(("groups", "dp"), "dout"), P(None, "dout", "dp", "din"))
    return jax.shard_map(
        on_device, mesh=mesh, in_specs=placed, out_specs=P(None, ("groups", "dp")), check_vma=False
    )
```

```python
import functools
import math

import jax
import jax.numpy as jnp
from jax import lax
from jax.experimental import pallas as pl
from jax.experimental.pallas import tpu as pltpu
from jax.sharding import PartitionSpec as P


LONG, SHORT = 14_000_000_000, 1_000_000


def trade(block, steps, backwards=False):
    axes = tuple(steps)
    sizes = [lax.axis_size(axis) for axis in axes]
    mask = 0
    for axis, size in zip(axes, sizes):
        mask = mask * size + steps[axis]
    route = [(i, i ^ mask) for i in range(math.prod(sizes))]
    return lax.ppermute(block, axes, route[::-1] if backwards else route)


def pass_on(block, step, count):
    up = lax.ppermute(block[0], "dp", [(i, i + 1) for i in range(step - 1, count - 1)])
    down = lax.ppermute(block[1], "dp", [(i, i - 1) for i in range(1, count - step + 1)])
    return up, down


ANYWHERE = pl.BlockSpec(memory_space=pl.ANY)
SCALARS = pl.BlockSpec(memory_space=pltpu.SMEM)
NEAR = pl.BlockSpec(memory_space=pltpu.VMEM)


def call(kernel, where, arrays, outs, flops, tokens=(), scratch=()):
    skip = len(tokens)

    def body(where, *refs):
        kernel(where, *refs[: len(arrays)], *refs[len(arrays) + skip :])

    return pl.pallas_call(
        body,
        in_specs=[SCALARS] + [NEAR] * len(arrays) + [ANYWHERE] * skip,
        out_specs=[NEAR] * len(outs),
        out_shape=[pltpu.VMEM(shape, dtype) for shape, dtype in outs],
        scratch_shapes=list(scratch),
        compiler_params=pltpu.CompilerParams(vmem_limit_bytes=12 * 1024 * 1024),
        cost_estimate=pl.CostEstimate(flops=flops, bytes_accessed=1024, transcendentals=0),
    )(
        jnp.stack([jnp.asarray(w, jnp.int32) for w in where]),
        *[pltpu.with_memory_space_constraint(array, pltpu.VMEM) for array in arrays],
        *tokens,
    )


def load_kernel(far_ref, near_ref, arrived):
    copy = pltpu.make_async_copy(far_ref, near_ref, arrived)
    copy.start()
    copy.wait()


def loaded(array):
    return pl.pallas_call(
        load_kernel,
        in_specs=[ANYWHERE],
        out_specs=NEAR,
        out_shape=pltpu.VMEM(array.shape, array.dtype),
        scratch_shapes=[pltpu.SemaphoreType.DMA],
        compiler_params=pltpu.CompilerParams(vmem_limit_bytes=1024 * 1024),
        cost_estimate=pl.CostEstimate(flops=1024, bytes_accessed=1024, transcendentals=0),
    )(pltpu.with_memory_space_constraint(array, pltpu.HBM))


def hold(blocks, tokens):
    count = len(blocks)
    return pl.pallas_call(
        lambda *refs: None,
        in_specs=[ANYWHERE] * (count + len(tokens)),
        out_specs=[ANYWHERE] * count,
        out_shape=[jax.ShapeDtypeStruct(block.shape, block.dtype) for block in blocks],
        input_output_aliases={i: i for i in range(count)},
        compiler_params=pltpu.CompilerParams(vmem_limit_bytes=1024 * 1024),
        cost_estimate=pl.CostEstimate(flops=1024, bytes_accessed=1024, transcendentals=0),
    )(*blocks, *tokens)


def turn_kernel(where, *refs):
    count = len(refs) // 2
    for block, out in zip(refs[:count], refs[count:]):
        out[...] = block[...].astype(jnp.float32).T.astype(block.dtype)


def turned(blocks):
    rows, width = blocks[0].shape
    if rows % 128 or width % 128:
        return [block.T for block in blocks]
    return call(turn_kernel, [0], blocks, [((width, rows), block.dtype) for block in blocks], 1024)


def pick_kernel(where, *refs):
    *blocks, out_ref = refs
    for k, block in enumerate(blocks):

        @pl.when(where[0] == k)
        def _():
            out_ref[...] = block[...]


def from_partner(hops, me, d, count, tokens=()):
    sources, choice = [], []
    for z in range(count):
        away = z - (z ^ d)
        source = (abs(away), int(away < 0))
        if source not in sources:
            sources.append(source)
        choice.append(sources.index(source))
    where = functools.reduce(lambda found, z: jnp.where(me == z, choice[z], found), range(count), 0)
    blocks = [hops[step][way] for step, way in sources]
    return call(pick_kernel, [where], blocks, [(blocks[0].shape, blocks[0].dtype)], 1024, tokens)[0]


def joined(parts, where, axis):
    found = []
    for p in range(len(parts)):
        chosen = parts[0][...]
        for r in range(1, len(parts)):
            chosen = jnp.where(where[0] == p ^ r, parts[r][...], chosen)
        found.append(chosen)
    return found[0] if len(found) == 1 else jnp.concatenate(found, axis=axis)


MARK = (8, 128), jnp.float32


def mix_kernel(where, *refs):
    *parts, query_ref, out_ref, mark_ref, acts = refs
    mark_ref[...] = jnp.zeros_like(mark_ref)
    half = parts[0].shape[0]
    acts[pl.ds(pl.multiple_of(where[0] * half, half), half), :] = parts[0][...]
    if len(parts) > 1:
        acts[pl.ds(pl.multiple_of((1 - where[0]) * half, half), half), :] = parts[1][...]
    nq, _, depth, _ = query_ref.shape
    tile = depth // 2

    def step(at, _):
        q, rows = at // 2, pl.ds(pl.multiple_of(at % 2 * tile, tile), tile)
        out_ref[q, rows, :] = lax.dot_general(
            query_ref[q, 0, rows, :], acts[...], (((1,), (1,)), ((), ())), preferred_element_type=jnp.float32
        )
        return 0

    lax.fori_loop(0, 2 * nq, step, 0)


def mixed(parts, core, queries, flops, tokens=()):
    nq, _, depth, width = queries.shape
    tokens_here = sum(part.shape[0] for part in parts)
    outs = [((nq, depth, tokens_here), jnp.float32), MARK]
    scratch = [pltpu.VMEM((tokens_here, width), queries.dtype)]
    return call(mix_kernel, [core], [*parts, queries], outs, flops, tokens, scratch)


def score_kernel(where, *refs):
    *parts, mix_ref, out_ref = refs
    grads = joined(parts, where, 1).astype(jnp.float32)
    for q in range(mix_ref.shape[0]):
        out_ref[q : q + 1, :] = jnp.sum(grads * mix_ref[q], axis=0, keepdims=True)


def scores_of_grads(parts, column, mix, tokens=(), flops=1024):
    nq, _, count = mix.shape
    return call(score_kernel, [column], [*parts, mix], [((nq, count), jnp.float32)], flops, tokens)[0]


def project_kernel(where, *refs):
    *parts, query_ref, out_ref, mark_ref, grads = refs
    mark_ref[...] = jnp.zeros_like(mark_ref)
    grads[...] = joined(parts, where, 0)
    nq, _, _, width = query_ref.shape
    tile = width // 2

    def step(at, _):
        q, columns = at // 2, pl.ds(pl.multiple_of(at % 2 * tile, tile), tile)
        out_ref[q, :, columns] = jnp.dot(
            grads[...], query_ref[q, 0, :, columns], preferred_element_type=jnp.float32
        )
        return 0

    lax.fori_loop(0, 2 * nq, step, 0)


def projected(parts, column, queries, flops, tokens=()):
    nq, _, depth, width = queries.shape
    count = sum(part.shape[0] for part in parts)
    outs = [((nq, count, width), jnp.float32), MARK]
    scratch = [pltpu.VMEM((count, depth), queries.dtype)]
    return call(project_kernel, [column], [*parts, queries], outs, flops, tokens, scratch)


def finish_kernel(where, mine_ref, other_ref, proj_ref, out_ref):
    half, width = mine_ref.shape
    swapped = where[0] == 1
    for h, (first, second) in enumerate(((mine_ref, other_ref), (other_ref, mine_ref))):
        acts = jnp.where(swapped, second[...], first[...]).astype(jnp.float32)
        for q in range(proj_ref.shape[0]):
            terms = acts * proj_ref[q, h * half : (h + 1) * half, :]
            lanes = terms[:, :128]
            for at in range(128, width, 128):
                lanes = lanes + terms[:, at : at + 128]
            out_ref[q : q + 1, h * half : (h + 1) * half] = jnp.sum(lanes.T, axis=0, keepdims=True)


def scores_of_acts(mine, other, core, proj, tokens=()):
    nq, count, _ = proj.shape
    return call(finish_kernel, [core], [mine, other, proj], [((nq, count), jnp.float32)], 1024, tokens)[0]


def on_device(activations, out_grads, queries):
    count, spread = lax.axis_size("dp"), lax.axis_size("din")
    me, column, core = lax.axis_index("dp"), lax.axis_index("din"), lax.axis_index("dout")
    tokens, rows = activations.shape[0], queries.shape[2]
    part, half = tokens // spread, tokens // 2

    def to_columns(arrived):
        return [arrived] + [trade(arrived, {"din": r}) for r in range(1, spread)]

    def acts_of(block):
        return [block, trade(block, {"dout": 1})]

    far, late = count - 1, count - 2
    early = list(range(1, late))

    mine = lax.dynamic_slice_in_dim(activations, core * half, half, 0)
    hops = [(mine, mine)]
    hops.append(pass_on(hops[0], 1, count))

    def grads_for(device, first, size):
        return lax.dynamic_slice(out_grads, (first, device * rows), (size, rows))

    sent = turned([grads_for(me ^ d, column * part, part) for d in early + [late]])
    sent = [*sent, grads_for(me ^ far, column * part, part)]
    arrived = {d: trade(block, {"dp": d}) for d, block in zip(early + [late, far], sent)}

    queries = loaded(queries)
    zero = jnp.zeros((), jnp.int32)
    mix, token = mixed([activations], zero, queries, SHORT, sent)
    own, = turned([grads_for(me, 0, tokens)])
    scores = scores_of_grads([own], zero, mix)
    hops[1] = hold(list(hops[1]), [token])
    for step in range(2, count - 1):
        hops.append(pass_on(hops[-1], step, count))

    mixes, token = {}, scores
    for d in early:
        mixes[d], token = mixed(acts_of(from_partner(hops, me, d, count)), core, queries, SHORT, [token])
    sides = to_columns(hold([arrived[far]], hops[1])[0])
    block = from_partner(hops, me, late, count, [token] + sides)
    end = lax.ppermute(block, "dp", [(1, 0), (count - 2, count - 1)])
    hops.append((end, end))

    proj, token = projected(sides, column, queries, SHORT, [token])
    for d in early:
        sides = to_columns(hold([arrived[d]], hops[1])[0])
        token = scores_of_grads(sides, column, mixes[d], [token])
        scores = scores + trade(token, {"dp": d})

    sides = to_columns(hold([arrived[late]], [token])[0])
    mix, token = mixed(acts_of(block), core, queries, SHORT, [token])
    sides = sides[:1] + list(hold(sides[1:], [token]))
    near = trade(scores_of_grads(sides, column, mix, (), LONG), {"dp": late})
    block = from_partner(hops, me, far, count, [token])
    scores = scores + near + trade(scores_of_acts(*acts_of(block), core, proj), {"dp": far})
    return over_chips(scores, spread)


def over_chips(scores, spread):
    scores = scores + trade(scores, {"dout": 1})
    return scores + sum(trade(scores, {"din": r}) for r in range(1, spread))


def solution(mesh):
    placed = (P(("groups", "dp"), "din"), P(("groups", "dp"), "dout"), P(None, "dout", "dp", "din"))
    return jax.shard_map(
        on_device, mesh=mesh, in_specs=placed, out_specs=P(None, ("groups", "dp")), check_vma=False
    )
```

```python
import functools
import math

import jax
import jax.numpy as jnp
from jax import lax
from jax.experimental import pallas as pl
from jax.experimental.pallas import tpu as pltpu
from jax.sharding import PartitionSpec as P


LONG, SHORT = 14_000_000_000, 1_000_000


def trade(block, steps, backwards=False):
    axes = tuple(steps)
    sizes = [lax.axis_size(axis) for axis in axes]
    mask = 0
    for axis, size in zip(axes, sizes):
        mask = mask * size + steps[axis]
    route = [(i, i ^ mask) for i in range(math.prod(sizes))]
    return lax.ppermute(block, axes, route[::-1] if backwards else route)


def pass_on(block, step, count):
    up = lax.ppermute(block[0], "dp", [(i, i + 1) for i in range(step - 1, count - 1)])
    down = lax.ppermute(block[1], "dp", [(i, i - 1) for i in range(1, count - step + 1)])
    return up, down


ANYWHERE = pl.BlockSpec(memory_space=pl.ANY)
NEAR = pl.BlockSpec(memory_space=pltpu.VMEM)


def call(kernel, arrays, outs, flops=1024, tokens=(), scratch=()):
    skip = len(tokens)

    def body(*refs):
        kernel(*refs[: len(arrays)], *refs[len(arrays) + skip :])

    return pl.pallas_call(
        body,
        in_specs=[NEAR] * len(arrays) + [ANYWHERE] * skip,
        out_specs=[NEAR] * len(outs),
        out_shape=[pltpu.VMEM(shape, dtype) for shape, dtype in outs],
        scratch_shapes=list(scratch),
        compiler_params=pltpu.CompilerParams(vmem_limit_bytes=12 * 1024 * 1024),
        cost_estimate=pl.CostEstimate(flops=flops, bytes_accessed=1024, transcendentals=0),
    )(*[pltpu.with_memory_space_constraint(array, pltpu.VMEM) for array in arrays], *tokens)


def fetch(kernel, arrays, outs, scratch, copies):
    return pl.pallas_call(
        kernel,
        in_specs=[ANYWHERE] * len(arrays),
        out_specs=[NEAR] * len(outs),
        out_shape=[pltpu.VMEM(shape, dtype) for shape, dtype in outs],
        scratch_shapes=[*scratch, pltpu.SemaphoreType.DMA((copies,))],
        compiler_params=pltpu.CompilerParams(vmem_limit_bytes=12 * 1024 * 1024),
        cost_estimate=pl.CostEstimate(flops=1024, bytes_accessed=1024, transcendentals=0),
    )(*[pltpu.with_memory_space_constraint(array, pltpu.HBM) for array in arrays])


def grads_block(grads_ref, device, part, rows):
    first = pl.multiple_of(lax.axis_index("din") * part, part)
    return grads_ref.at[pl.ds(first, part), pl.ds(pl.multiple_of(device * rows, rows), rows)]


def first_kernel(far, acts_ref, grads_ref, mine_ref, far_ref, arrived):
    half = mine_ref.shape[0]
    rows = pl.ds(pl.multiple_of(lax.axis_index("dout") * half, half), half)
    block = grads_block(grads_ref, lax.axis_index("dp") ^ far, *far_ref.shape)
    copies = [
        pltpu.make_async_copy(acts_ref.at[rows, :], mine_ref, arrived.at[0]),
        pltpu.make_async_copy(block, far_ref, arrived.at[1]),
    ]
    for copy in copies:
        copy.start()
    for copy in copies:
        copy.wait()


def rest_kernel(steps, acts_ref, grads_ref, query_ref, near_query, near_acts, own_out, *refs):
    outs, own, blocks, arrived = refs[: len(steps)], refs[-3], refs[-2], refs[-1]
    me = lax.axis_index("dp")
    tokens, rows = own.shape
    copies = [pltpu.make_async_copy(grads_ref.at[:, pl.ds(pl.multiple_of(me * rows, rows), rows)], own, arrived.at[0])]
    for k, d in enumerate(steps):
        block = grads_block(grads_ref, me ^ d, *blocks.shape[1:])
        copies.append(pltpu.make_async_copy(block, blocks.at[k], arrived.at[1 + k]))
    copies.append(pltpu.make_async_copy(acts_ref, near_acts, arrived.at[len(steps) + 1]))
    copies.append(pltpu.make_async_copy(query_ref, near_query, arrived.at[len(steps) + 2]))
    for copy in copies:
        copy.start()
    for k, out in enumerate(outs):
        copies[1 + k].wait()
        out[...] = blocks[k].astype(jnp.float32).T.astype(out.dtype)
    copies[0].wait()
    own_out[...] = own[...].astype(jnp.float32).T.astype(own_out.dtype)
    for copy in copies[-2:]:
        copy.wait()


def hold(blocks, tokens):
    count = len(blocks)
    return pl.pallas_call(
        lambda *refs: None,
        in_specs=[ANYWHERE] * (count + len(tokens)),
        out_specs=[ANYWHERE] * count,
        out_shape=[jax.ShapeDtypeStruct(block.shape, block.dtype) for block in blocks],
        input_output_aliases={i: i for i in range(count)},
        compiler_params=pltpu.CompilerParams(vmem_limit_bytes=1024 * 1024),
        cost_estimate=pl.CostEstimate(flops=1024, bytes_accessed=1024, transcendentals=0),
    )(*blocks, *tokens)


def pick_kernel(choice, *refs):
    *blocks, out_ref = refs
    me = lax.axis_index("dp")
    where = functools.reduce(lambda found, z: jnp.where(me == z, choice[z], found), range(len(choice)), 0)
    for k, block in enumerate(blocks):

        @pl.when(where == k)
        def _():
            out_ref[...] = block[...]


def from_partner(hops, d, count, tokens=()):
    sources, choice = [], []
    for z in range(count):
        away = z - (z ^ d)
        source = (abs(away), int(away < 0 and abs(away) < count - 1))
        if source not in sources:
            sources.append(source)
        choice.append(sources.index(source))
    blocks = [hops[step][way] for step, way in sources]
    outs = [(blocks[0].shape, blocks[0].dtype)]
    return call(functools.partial(pick_kernel, choice), blocks, outs, tokens=tokens)[0]


def joined(parts, axis):
    if len(parts) == 1:
        return parts[0][...]
    column, found = lax.axis_index("din"), []
    for p in range(len(parts)):
        chosen = parts[0][...]
        for r in range(1, len(parts)):
            chosen = jnp.where(column == p ^ r, parts[r][...], chosen)
        found.append(chosen)
    return jnp.concatenate(found, axis=axis)


MARK = (8, 128), jnp.float32


def mix_kernel(*refs):
    *parts, query_ref, out_ref, mark_ref, acts = refs
    mark_ref[...] = jnp.zeros_like(mark_ref)
    half = parts[0].shape[0]
    first = lax.axis_index("dout") * half if len(parts) > 1 else 0
    for part, at in zip(parts, (first, half - first)):
        acts[pl.ds(pl.multiple_of(at, half), half), :] = part[...]
    nq, _, depth, _ = query_ref.shape
    tile = depth // 2

    def step(at, _):
        q, rows = at // 2, pl.ds(pl.multiple_of(at % 2 * tile, tile), tile)
        out_ref[q, rows, :] = lax.dot_general(
            query_ref[q, 0, rows, :], acts[...], (((1,), (1,)), ((), ())), preferred_element_type=jnp.float32
        )
        return 0

    lax.fori_loop(0, 2 * nq, step, 0)


def mixed(parts, queries, flops, tokens=()):
    nq, _, depth, width = queries.shape
    tokens_here = sum(part.shape[0] for part in parts)
    outs = [((nq, depth, tokens_here), jnp.float32), MARK]
    scratch = [pltpu.VMEM((tokens_here, width), queries.dtype)]
    return call(mix_kernel, [*parts, queries], outs, flops, tokens, scratch)


def score_kernel(*refs):
    *parts, mix_ref, out_ref = refs
    grads = joined(parts, 1).astype(jnp.float32)
    for q in range(mix_ref.shape[0]):
        out_ref[q : q + 1, :] = jnp.sum(grads * mix_ref[q], axis=0, keepdims=True)


def scores_of_grads(parts, mix, tokens=(), flops=1024):
    nq, _, count = mix.shape
    return call(score_kernel, [*parts, mix], [((nq, count), jnp.float32)], flops, tokens)[0]


def project_kernel(*refs):
    *parts, query_ref, out_ref, mark_ref, grads = refs
    mark_ref[...] = jnp.zeros_like(mark_ref)
    grads[...] = joined(parts, 0)
    nq, _, _, width = query_ref.shape
    tile = width // 2

    def step(at, _):
        q, columns = at // 2, pl.ds(pl.multiple_of(at % 2 * tile, tile), tile)
        out_ref[q, :, columns] = jnp.dot(
            grads[...], query_ref[q, 0, :, columns], preferred_element_type=jnp.float32
        )
        return 0

    lax.fori_loop(0, 2 * nq, step, 0)


def projected(parts, queries, flops, tokens=()):
    nq, _, depth, width = queries.shape
    count = sum(part.shape[0] for part in parts)
    outs = [((nq, count, width), jnp.float32), MARK]
    scratch = [pltpu.VMEM((count, depth), queries.dtype)]
    return call(project_kernel, [*parts, queries], outs, flops, tokens, scratch)


def finish_kernel(mine_ref, other_ref, proj_ref, out_ref):
    half, width = mine_ref.shape
    swapped = lax.axis_index("dout") == 1
    for h, (first, second) in enumerate(((mine_ref, other_ref), (other_ref, mine_ref))):
        acts = jnp.where(swapped, second[...], first[...]).astype(jnp.float32)
        for q in range(proj_ref.shape[0]):
            terms = acts * proj_ref[q, h * half : (h + 1) * half, :]
            lanes = terms[:, :128]
            for at in range(128, width, 128):
                lanes = lanes + terms[:, at : at + 128]
            out_ref[q : q + 1, h * half : (h + 1) * half] = jnp.sum(lanes.T, axis=0, keepdims=True)


def scores_of_acts(mine, other, proj, tokens=()):
    nq, count, _ = proj.shape
    return call(finish_kernel, [mine, other, proj], [((nq, count), jnp.float32)], tokens=tokens)[0]


def cut(activations, out_grads, queries, far, others):
    count, part = lax.axis_size("dp"), out_grads.shape[0] // lax.axis_size("din")
    rows, (tokens, width), dtype = queries.shape[2], activations.shape, out_grads.dtype
    half = tokens // 2
    if part % 128 or rows % 128:
        me, column = lax.axis_index("dp"), lax.axis_index("din")
        mine = lax.dynamic_slice_in_dim(activations, lax.axis_index("dout") * half, half, 0)
        share = lax.dynamic_slice_in_dim(out_grads, column * part, part, 0)
        away = [lax.dynamic_slice_in_dim(share, (me ^ d) * rows, rows, 1) for d in [far, *others]]
        own = lax.dynamic_slice_in_dim(out_grads, me * rows, rows, 1).T
        return (mine, away[0]), (queries, activations, own, *[block.T for block in away[1:]])
    outs = [((half, width), activations.dtype), ((part, rows), dtype)]
    first = fetch(functools.partial(first_kernel, far), [activations, out_grads], outs, [], 2)
    outs = [(queries.shape, queries.dtype), (activations.shape, activations.dtype), ((rows, tokens), dtype)]
    outs += [((rows, part), dtype)] * len(others)
    scratch = [pltpu.VMEM((tokens, rows), dtype), pltpu.VMEM((len(others), part, rows), dtype)]
    arrays = [activations, out_grads, queries]
    return first, fetch(functools.partial(rest_kernel, others), arrays, outs, scratch, len(others) + 3)


def on_device(activations, out_grads, queries):
    count, spread = lax.axis_size("dp"), lax.axis_size("din")

    def to_columns(arrived):
        return [arrived] + [trade(arrived, {"din": r}) for r in range(1, spread)]

    def acts_of(block):
        return [block, trade(block, {"dout": 1})]

    far, late = count - 1, count - 2
    early = list(range(1, late))
    (mine, far_grads), (queries, own_acts, own, *sent) = cut(activations, out_grads, queries, far, early + [late])
    hops = [(mine, mine)]
    hops.append(pass_on(hops[0], 1, count))
    arrived = {d: trade(block, {"dp": d}) for d, block in zip([far, *early, late], [far_grads, *sent])}

    mix, token = mixed([own_acts], queries, SHORT)
    scores = scores_of_grads([own], mix)
    hops[1] = hold(list(hops[1]), [token])
    for step in range(2, count - 1):
        hops.append(pass_on(hops[-1], step, count))

    mixes, token = {}, scores
    for d in early:
        mixes[d], token = mixed(acts_of(from_partner(hops, d, count)), queries, SHORT, [token])
    sides = to_columns(hold([arrived[far]], hops[1])[0])
    block = from_partner(hops, late, count, [token] + sides)
    end = lax.ppermute(block, "dp", [(1, 0), (count - 2, count - 1)])
    hops.append((end, end))

    proj, token = projected(sides, queries, SHORT, [token])
    terms = []
    for d in early:
        sides = to_columns(hold([arrived[d]], hops[1])[0])
        token = scores_of_grads(sides, mixes[d], [token])
        terms.append(trade(token, {"dp": d}))

    sides = to_columns(hold([arrived[late]], [token])[0])
    mix, token = mixed(acts_of(block), queries, SHORT, [token])
    sides = sides[:1] + list(hold(sides[1:], [token]))
    terms.append(trade(scores_of_grads(sides, mix, (), LONG), {"dp": late}))
    block = from_partner(hops, far, count, [token])
    terms.append(trade(scores_of_acts(*acts_of(block), proj), {"dp": far}))
    return over_chips(sum(terms, scores), spread)


def over_chips(scores, spread):
    scores = scores + trade(scores, {"dout": 1})
    return scores + sum(trade(scores, {"din": r}) for r in range(1, spread))


def solution(mesh):
    placed = (P(("groups", "dp"), "din"), P(("groups", "dp"), "dout"), P(None, "dout", "dp", "din"))
    return jax.shard_map(
        on_device, mesh=mesh, in_specs=placed, out_specs=P(None, ("groups", "dp")), check_vma=False
    )
```

```python
import functools
import math

import jax
import jax.numpy as jnp
from jax import lax
from jax.experimental import pallas as pl
from jax.experimental.pallas import tpu as pltpu
from jax.sharding import PartitionSpec as P


LONG, SHORT = 14_000_000_000, 1_000_000


def trade(block, steps, backwards=False):
    axes = tuple(steps)
    sizes = [lax.axis_size(axis) for axis in axes]
    mask = 0
    for axis, size in zip(axes, sizes):
        mask = mask * size + steps[axis]
    route = [(i, i ^ mask) for i in range(math.prod(sizes))]
    return lax.ppermute(block, axes, route[::-1] if backwards else route)


def pass_on(block, step, count):
    up = lax.ppermute(block[0], "dp", [(i, i + 1) for i in range(step - 1, count - 1)])
    down = lax.ppermute(block[1], "dp", [(i, i - 1) for i in range(1, count - step + 1)])
    return up, down


ANYWHERE = pl.BlockSpec(memory_space=pl.ANY)
NEAR = pl.BlockSpec(memory_space=pltpu.VMEM)


def call(kernel, arrays, outs, flops=1024, tokens=(), scratch=()):
    skip = len(tokens)

    def body(*refs):
        kernel(*refs[: len(arrays)], *refs[len(arrays) + skip :])

    return pl.pallas_call(
        body,
        in_specs=[NEAR] * len(arrays) + [ANYWHERE] * skip,
        out_specs=[NEAR] * len(outs),
        out_shape=[pltpu.VMEM(shape, dtype) for shape, dtype in outs],
        scratch_shapes=list(scratch),
        compiler_params=pltpu.CompilerParams(vmem_limit_bytes=12 * 1024 * 1024),
        cost_estimate=pl.CostEstimate(flops=flops, bytes_accessed=1024, transcendentals=0),
    )(*[pltpu.with_memory_space_constraint(array, pltpu.VMEM) for array in arrays], *tokens)


def fetch(kernel, arrays, outs, scratch, copies):
    return pl.pallas_call(
        kernel,
        in_specs=[ANYWHERE] * len(arrays),
        out_specs=[NEAR] * len(outs),
        out_shape=[pltpu.VMEM(shape, dtype) for shape, dtype in outs],
        scratch_shapes=[*scratch, pltpu.SemaphoreType.DMA((copies,))],
        compiler_params=pltpu.CompilerParams(vmem_limit_bytes=12 * 1024 * 1024),
        cost_estimate=pl.CostEstimate(flops=1024, bytes_accessed=1024, transcendentals=0),
    )(*[pltpu.with_memory_space_constraint(array, pltpu.HBM) for array in arrays])


def grads_block(grads_ref, device, part, rows):
    first = pl.multiple_of(lax.axis_index("din") * part, part)
    return grads_ref.at[pl.ds(first, part), pl.ds(pl.multiple_of(device * rows, rows), rows)]


def first_kernel(far, acts_ref, grads_ref, mine_ref, far_ref, arrived):
    half = mine_ref.shape[0]
    rows = pl.ds(pl.multiple_of(lax.axis_index("dout") * half, half), half)
    block = grads_block(grads_ref, lax.axis_index("dp") ^ far, *far_ref.shape)
    copies = [
        pltpu.make_async_copy(acts_ref.at[rows, :], mine_ref, arrived.at[0]),
        pltpu.make_async_copy(block, far_ref, arrived.at[1]),
    ]
    for copy in copies:
        copy.start()
    for copy in copies:
        copy.wait()


def rest_kernel(steps, acts_ref, grads_ref, query_ref, near_query, near_acts, own_out, *refs):
    outs, own, blocks, arrived = list(refs[:-3]), refs[-3], refs[-2], refs[-1]
    me = lax.axis_index("dp")
    tokens, rows = own.shape
    copies = [pltpu.make_async_copy(grads_ref.at[:, pl.ds(pl.multiple_of(me * rows, rows), rows)], own, arrived.at[0])]
    for k, d in enumerate(steps):
        block = grads_block(grads_ref, me ^ d, *blocks.shape[1:])
        copies.append(pltpu.make_async_copy(block, blocks.at[k], arrived.at[1 + k]))
    copies.append(pltpu.make_async_copy(acts_ref, near_acts, arrived.at[len(steps) + 1]))
    copies.append(pltpu.make_async_copy(query_ref, near_query, arrived.at[len(steps) + 2]))
    for copy in copies:
        copy.start()
    for k in range(len(steps)):
        copies[1 + k].wait()
        turned, at = blocks[k].astype(jnp.float32).T.astype(blocks.dtype), 0
        while at < rows:
            out = outs.pop(0)
            out[...] = turned[at : at + out.shape[0]]
            at += out.shape[0]
    copies[0].wait()
    own_out[...] = own[...].astype(jnp.float32).T.astype(own_out.dtype)
    for copy in copies[-2:]:
        copy.wait()


def hold(blocks, tokens, flops=1024):
    count = len(blocks)
    return pl.pallas_call(
        lambda *refs: None,
        in_specs=[ANYWHERE] * (count + len(tokens)),
        out_specs=[ANYWHERE] * count,
        out_shape=[jax.ShapeDtypeStruct(block.shape, block.dtype) for block in blocks],
        input_output_aliases={i: i for i in range(count)},
        compiler_params=pltpu.CompilerParams(vmem_limit_bytes=1024 * 1024),
        cost_estimate=pl.CostEstimate(flops=flops, bytes_accessed=1024, transcendentals=0),
    )(*blocks, *tokens)


def pick_kernel(choice, *refs):
    *blocks, out_ref = refs
    me = lax.axis_index("dp")
    where = functools.reduce(lambda found, z: jnp.where(me == z, choice[z], found), range(len(choice)), 0)
    for k, block in enumerate(blocks):

        @pl.when(where == k)
        def _():
            out_ref[...] = block[...]


def from_partner(hops, d, count, tokens=()):
    sources, choice = [], []
    for z in range(count):
        away = z - (z ^ d)
        source = (abs(away), int(away < 0 and abs(away) < count - 1))
        if source not in sources:
            sources.append(source)
        choice.append(sources.index(source))
    blocks = [hops[step][way] for step, way in sources]
    outs = [(blocks[0].shape, blocks[0].dtype)]
    return call(functools.partial(pick_kernel, choice), blocks, outs, tokens=tokens)[0]


def joined(parts, axis):
    parts = [part[...] for part in parts]
    if len(parts) == 1:
        return parts[0]
    column, found = lax.axis_index("din"), []
    for p in range(len(parts)):
        chosen = parts[0]
        for r in range(1, len(parts)):
            chosen = jnp.where(column == p ^ r, parts[r], chosen)
        found.append(chosen)
    return jnp.concatenate(found, axis=axis)


MARK = (8, 128), jnp.float32


def mix_kernel(*refs):
    *parts, query_ref, out_ref, mark_ref, acts = refs
    mark_ref[...] = jnp.zeros_like(mark_ref)
    half = parts[0].shape[0]
    first = lax.axis_index("dout") * half if len(parts) > 1 else 0
    for part, at in zip(parts, (first, half - first)):
        acts[pl.ds(pl.multiple_of(at, half), half), :] = part[...]
    nq, _, depth, _ = query_ref.shape
    tile = depth // 2

    def step(at, _):
        q, rows = at // 2, pl.ds(pl.multiple_of(at % 2 * tile, tile), tile)
        out_ref[q, rows, :] = lax.dot_general(
            query_ref[q, 0, rows, :], acts[...], (((1,), (1,)), ((), ())), preferred_element_type=jnp.float32
        )
        return 0

    lax.fori_loop(0, 2 * nq, step, 0)


def mixed(parts, queries, flops, tokens=()):
    nq, _, depth, width = queries.shape
    tokens_here = sum(part.shape[0] for part in parts)
    outs = [((nq, depth, tokens_here), jnp.float32), MARK]
    scratch = [pltpu.VMEM((tokens_here, width), queries.dtype)]
    return call(mix_kernel, [*parts, queries], outs, flops, tokens, scratch)


def score_kernel(pieces, *refs):
    *parts, mix_ref, out_ref = refs
    size = mix_ref.shape[1] // pieces
    for p in range(pieces):
        grads = joined(parts[p::pieces], 1).astype(jnp.float32)
        for q in range(mix_ref.shape[0]):
            term = jnp.sum(grads * mix_ref[q, p * size : (p + 1) * size], axis=0, keepdims=True)
            out_ref[q : q + 1, :] = term if p == 0 else out_ref[q : q + 1, :] + term


def scores_of_grads(parts, mix, tokens=(), flops=1024):
    nq, _, count = mix.shape
    parts = [part if isinstance(part, list) else [part] for part in parts]
    kernel = functools.partial(score_kernel, len(parts[0]))
    return call(kernel, [*sum(parts, []), mix], [((nq, count), jnp.float32)], flops, tokens)[0]


def project_kernel(*refs):
    *parts, query_ref, out_ref, mark_ref, grads = refs
    mark_ref[...] = jnp.zeros_like(mark_ref)
    grads[...] = joined(parts, 0)
    nq, _, _, width = query_ref.shape
    tile = width // 2

    def step(at, _):
        q, columns = at // 2, pl.ds(pl.multiple_of(at % 2 * tile, tile), tile)
        out_ref[q, :, columns] = jnp.dot(
            grads[...], query_ref[q, 0, :, columns], preferred_element_type=jnp.float32
        )
        return 0

    lax.fori_loop(0, 2 * nq, step, 0)


def projected(parts, queries, flops, tokens=()):
    nq, _, depth, width = queries.shape
    count = sum(part.shape[0] for part in parts)
    outs = [((nq, count, width), jnp.float32), MARK]
    scratch = [pltpu.VMEM((count, depth), queries.dtype)]
    return call(project_kernel, [*parts, queries], outs, flops, tokens, scratch)


def finish_kernel(mine_ref, other_ref, proj_ref, out_ref):
    half, width = mine_ref.shape
    swapped = lax.axis_index("dout") == 1
    for h, (first, second) in enumerate(((mine_ref, other_ref), (other_ref, mine_ref))):
        acts = jnp.where(swapped, second[...], first[...]).astype(jnp.float32)
        for q in range(proj_ref.shape[0]):
            terms = acts * proj_ref[q, h * half : (h + 1) * half, :]
            lanes = terms[:, :128]
            for at in range(128, width, 128):
                lanes = lanes + terms[:, at : at + 128]
            out_ref[q : q + 1, h * half : (h + 1) * half] = jnp.sum(lanes.T, axis=0, keepdims=True)


def scores_of_acts(mine, other, proj, tokens=()):
    nq, count, _ = proj.shape
    return call(finish_kernel, [mine, other, proj], [((nq, count), jnp.float32)], tokens=tokens)[0]


def cut(activations, out_grads, queries, far, others, pieces):
    count, part = lax.axis_size("dp"), out_grads.shape[0] // lax.axis_size("din")
    rows, (tokens, width), dtype = queries.shape[2], activations.shape, out_grads.dtype
    half = tokens // 2
    if part % 128 or rows % 128:
        me, column = lax.axis_index("dp"), lax.axis_index("din")
        mine = lax.dynamic_slice_in_dim(activations, lax.axis_index("dout") * half, half, 0)
        share = lax.dynamic_slice_in_dim(out_grads, column * part, part, 0)
        away = [lax.dynamic_slice_in_dim(share, (me ^ d) * rows, rows, 1) for d in [far, *others]]
        own = lax.dynamic_slice_in_dim(out_grads, me * rows, rows, 1).T
        turned = [block.T for block in away[1:]]
        return (mine, away[0]), (queries, activations, own, *turned[:-1], *jnp.split(turned[-1], pieces))
    outs = [((half, width), activations.dtype), ((part, rows), dtype)]
    first = fetch(functools.partial(first_kernel, far), [activations, out_grads], outs, [], 2)
    outs = [(queries.shape, queries.dtype), (activations.shape, activations.dtype), ((rows, tokens), dtype)]
    outs += [((rows, part), dtype)] * (len(others) - 1) + [((rows // pieces, part), dtype)] * pieces
    scratch = [pltpu.VMEM((tokens, rows), dtype), pltpu.VMEM((len(others), part, rows), dtype)]
    arrays = [activations, out_grads, queries]
    return first, fetch(functools.partial(rest_kernel, others), arrays, outs, scratch, len(others) + 3)


def on_device(activations, out_grads, queries):
    count, spread = lax.axis_size("dp"), lax.axis_size("din")

    def to_columns(arrived):
        return [arrived] + [trade(arrived, {"din": r}) for r in range(1, spread)]

    def acts_of(block):
        return [block, trade(block, {"dout": 1})]

    far, late = count - 1, count - 2
    early = list(range(1, late))
    pieces = 2
    (mine, far_grads), (queries, own_acts, own, *sent) = cut(
        activations, out_grads, queries, far, early + [late], pieces
    )
    hops = [(mine, mine)]
    hops.append(pass_on(hops[0], 1, count))
    arrived = {d: trade(block, {"dp": d}) for d, block in zip([far, *early], [far_grads, *sent])}
    tail = [trade(block, {"dp": late}) for block in sent[len(early) :]]

    mix, token = mixed([own_acts], queries, SHORT)
    scores = scores_of_grads([own], mix)
    hops[1] = hold(list(hops[1]), [token])
    for step in range(2, count - 1):
        hops.append(pass_on(hops[-1], step, count))

    mixes, token = {}, scores
    for d in early:
        mixes[d], token = mixed(acts_of(from_partner(hops, d, count)), queries, SHORT, [token])
    sides = to_columns(hold([arrived[far]], [*hops[1], *[arrived[d] for d in early]])[0])
    block = from_partner(hops, late, count, [token] + sides)
    end = lax.ppermute(block, "dp", [(1, 0), (count - 2, count - 1)])
    hops.append((end, end))

    proj, token = projected(sides, queries, SHORT, [token])
    terms = []
    for d in early:
        sides = to_columns(hold([arrived[d]], hops[1])[0])
        token = scores_of_grads(sides, mixes[d], [token])
        terms.append(trade(token, {"dp": d}))

    tail = [to_columns(hold([piece], [token], LONG)[0]) for piece in tail]
    mix, done = mixed(acts_of(block), queries, SHORT, [token])
    block = from_partner(hops, far, count, [done])
    terms.append(trade(scores_of_acts(*acts_of(block), proj), {"dp": far}))
    sides = [list(hold(sides, [done])) for sides in zip(*tail)]
    terms.append(trade(scores_of_grads(sides, mix, (), LONG), {"dp": late}))
    return over_chips(sum(terms, scores), spread)


def over_chips(scores, spread):
    scores = scores + trade(scores, {"dout": 1})
    return scores + sum(trade(scores, {"din": r}) for r in range(1, spread))


def solution(mesh):
    placed = (P(("groups", "dp"), "din"), P(("groups", "dp"), "dout"), P(None, "dout", "dp", "din"))
    return jax.shard_map(
        on_device, mesh=mesh, in_specs=placed, out_specs=P(None, ("groups", "dp")), check_vma=False
    )
```

```python
import functools
import math

import jax
import jax.numpy as jnp
from jax import lax
from jax.experimental import pallas as pl
from jax.experimental.pallas import tpu as pltpu
from jax.sharding import PartitionSpec as P


LONG, SHORT = 14_000_000_000, 1_000_000


def trade(block, steps, backwards=False):
    axes = tuple(steps)
    sizes = [lax.axis_size(axis) for axis in axes]
    mask = 0
    for axis, size in zip(axes, sizes):
        mask = mask * size + steps[axis]
    route = [(i, i ^ mask) for i in range(math.prod(sizes))]
    return lax.ppermute(block, axes, route[::-1] if backwards else route)


def pass_on(block, step, count):
    up = lax.ppermute(block[0], "dp", [(i, i + 1) for i in range(step - 1, count - 1)])
    down = lax.ppermute(block[1], "dp", [(i, i - 1) for i in range(1, count - step + 1)])
    return up, down


ANYWHERE = pl.BlockSpec(memory_space=pl.ANY)
NEAR = pl.BlockSpec(memory_space=pltpu.VMEM)


def call(kernel, arrays, outs, flops=1024, tokens=(), scratch=()):
    skip = len(tokens)

    def body(*refs):
        kernel(*refs[: len(arrays)], *refs[len(arrays) + skip :])

    return pl.pallas_call(
        body,
        in_specs=[NEAR] * len(arrays) + [ANYWHERE] * skip,
        out_specs=[NEAR] * len(outs),
        out_shape=[pltpu.VMEM(shape, dtype) for shape, dtype in outs],
        scratch_shapes=list(scratch),
        compiler_params=pltpu.CompilerParams(vmem_limit_bytes=12 * 1024 * 1024),
        cost_estimate=pl.CostEstimate(flops=flops, bytes_accessed=1024, transcendentals=0),
    )(*[pltpu.with_memory_space_constraint(array, pltpu.VMEM) for array in arrays], *tokens)


def fetch(kernel, arrays, outs, scratch, copies):
    return pl.pallas_call(
        kernel,
        in_specs=[ANYWHERE] * len(arrays),
        out_specs=[NEAR] * len(outs),
        out_shape=[pltpu.VMEM(shape, dtype) for shape, dtype in outs],
        scratch_shapes=[*scratch, pltpu.SemaphoreType.DMA((copies,))],
        compiler_params=pltpu.CompilerParams(vmem_limit_bytes=12 * 1024 * 1024),
        cost_estimate=pl.CostEstimate(flops=1024, bytes_accessed=1024, transcendentals=0),
    )(*[pltpu.with_memory_space_constraint(array, pltpu.HBM) for array in arrays])


def grads_block(grads_ref, device, part, rows):
    first = pl.multiple_of(lax.axis_index("din") * part, part)
    return grads_ref.at[pl.ds(first, part), pl.ds(pl.multiple_of(device * rows, rows), rows)]


def first_kernel(far, acts_ref, grads_ref, mine_ref, far_ref, arrived):
    half = mine_ref.shape[0]
    rows = pl.ds(pl.multiple_of(lax.axis_index("dout") * half, half), half)
    block = grads_block(grads_ref, lax.axis_index("dp") ^ far, *far_ref.shape)
    copies = [
        pltpu.make_async_copy(acts_ref.at[rows, :], mine_ref, arrived.at[0]),
        pltpu.make_async_copy(block, far_ref, arrived.at[1]),
    ]
    for copy in copies:
        copy.start()
    for copy in copies:
        copy.wait()


def rest_kernel(steps, acts_ref, grads_ref, query_ref, near_query, near_acts, own_out, *refs):
    outs, own, blocks, arrived = list(refs[:-3]), refs[-3], refs[-2], refs[-1]
    me = lax.axis_index("dp")
    tokens, rows = own.shape
    copies = [pltpu.make_async_copy(grads_ref.at[:, pl.ds(pl.multiple_of(me * rows, rows), rows)], own, arrived.at[0])]
    for k, d in enumerate(steps):
        block = grads_block(grads_ref, me ^ d, *blocks.shape[1:])
        copies.append(pltpu.make_async_copy(block, blocks.at[k], arrived.at[1 + k]))
    copies.append(pltpu.make_async_copy(acts_ref, near_acts, arrived.at[len(steps) + 1]))
    copies.append(pltpu.make_async_copy(query_ref, near_query, arrived.at[len(steps) + 2]))
    for copy in copies:
        copy.start()
    for k in range(len(steps)):
        copies[1 + k].wait()
        turned, at = blocks[k].astype(jnp.float32).T.astype(blocks.dtype), 0
        while at < rows:
            out = outs.pop(0)
            out[...] = turned[at : at + out.shape[0]]
            at += out.shape[0]
    copies[0].wait()
    own_out[...] = own[...].astype(jnp.float32).T.astype(own_out.dtype)
    for copy in copies[-2:]:
        copy.wait()


def hold(blocks, tokens, flops=1024):
    count = len(blocks)
    return pl.pallas_call(
        lambda *refs: None,
        in_specs=[ANYWHERE] * (count + len(tokens)),
        out_specs=[ANYWHERE] * count,
        out_shape=[jax.ShapeDtypeStruct(block.shape, block.dtype) for block in blocks],
        input_output_aliases={i: i for i in range(count)},
        compiler_params=pltpu.CompilerParams(vmem_limit_bytes=1024 * 1024),
        cost_estimate=pl.CostEstimate(flops=flops, bytes_accessed=1024, transcendentals=0),
    )(*blocks, *tokens)


def pick_kernel(choice, *refs):
    *blocks, out_ref = refs
    me = lax.axis_index("dp")
    where = functools.reduce(lambda found, z: jnp.where(me == z, choice[z], found), range(len(choice)), 0)
    for k, block in enumerate(blocks):

        @pl.when(where == k)
        def _():
            out_ref[...] = block[...]


def from_partner(hops, d, count, tokens=()):
    sources, choice = [], []
    for z in range(count):
        away = z - (z ^ d)
        source = (abs(away), int(away < 0 and abs(away) < count - 1))
        if source not in sources:
            sources.append(source)
        choice.append(sources.index(source))
    blocks = [hops[step][way] for step, way in sources]
    outs = [(blocks[0].shape, blocks[0].dtype)]
    return call(functools.partial(pick_kernel, choice), blocks, outs, tokens=tokens)[0]


def joined(parts, axis):
    parts = [part[...] for part in parts]
    if len(parts) == 1:
        return parts[0]
    column, found = lax.axis_index("din"), []
    for p in range(len(parts)):
        chosen = parts[0]
        for r in range(1, len(parts)):
            chosen = jnp.where(column == p ^ r, parts[r], chosen)
        found.append(chosen)
    return jnp.concatenate(found, axis=axis)


MARK = (8, 128), jnp.float32


def mix_kernel(*refs):
    *parts, query_ref, out_ref, mark_ref, acts = refs
    mark_ref[...] = jnp.zeros_like(mark_ref)
    half = parts[0].shape[0]
    first = lax.axis_index("dout") * half if len(parts) > 1 else 0
    for part, at in zip(parts, (first, half - first)):
        acts[pl.ds(pl.multiple_of(at, half), half), :] = part[...]
    nq, _, depth, _ = query_ref.shape
    tile = depth // 2

    def step(at, _):
        q, rows = at // 2, pl.ds(pl.multiple_of(at % 2 * tile, tile), tile)
        out_ref[q, rows, :] = lax.dot_general(
            query_ref[q, 0, rows, :], acts[...], (((1,), (1,)), ((), ())), preferred_element_type=jnp.float32
        )
        return 0

    lax.fori_loop(0, 2 * nq, step, 0)


def mixed(parts, queries, flops, tokens=()):
    nq, _, depth, width = queries.shape
    tokens_here = sum(part.shape[0] for part in parts)
    outs = [((nq, depth, tokens_here), jnp.float32), MARK]
    scratch = [pltpu.VMEM((tokens_here, width), queries.dtype)]
    return call(mix_kernel, [*parts, queries], outs, flops, tokens, scratch)


def score_kernel(pieces, *refs):
    *parts, mix_ref, out_ref = refs
    size = mix_ref.shape[1] // pieces
    for p in range(pieces):
        grads = joined(parts[p::pieces], 1).astype(jnp.float32)
        for q in range(mix_ref.shape[0]):
            term = jnp.sum(grads * mix_ref[q, p * size : (p + 1) * size], axis=0, keepdims=True)
            out_ref[q : q + 1, :] = term if p == 0 else out_ref[q : q + 1, :] + term


def scores_of_grads(parts, mix, tokens=(), flops=1024):
    nq, _, count = mix.shape
    parts = [part if isinstance(part, list) else [part] for part in parts]
    kernel = functools.partial(score_kernel, len(parts[0]))
    return call(kernel, [*sum(parts, []), mix], [((nq, count), jnp.float32)], flops, tokens)[0]


def project_kernel(*refs):
    *parts, query_ref, out_ref, mark_ref, grads = refs
    mark_ref[...] = jnp.zeros_like(mark_ref)
    grads[...] = joined(parts, 0)
    nq, _, _, width = query_ref.shape
    tile = width // 2

    def step(at, _):
        q, columns = at // 2, pl.ds(pl.multiple_of(at % 2 * tile, tile), tile)
        out_ref[q, :, columns] = jnp.dot(
            grads[...], query_ref[q, 0, :, columns], preferred_element_type=jnp.float32
        )
        return 0

    lax.fori_loop(0, 2 * nq, step, 0)


def projected(parts, queries, flops, tokens=()):
    nq, _, depth, width = queries.shape
    count = sum(part.shape[0] for part in parts)
    outs = [((nq, count, width), jnp.float32), MARK]
    scratch = [pltpu.VMEM((count, depth), queries.dtype)]
    return call(project_kernel, [*parts, queries], outs, flops, tokens, scratch)


def finish_kernel(mine_ref, other_ref, proj_ref, out_ref):
    half, width = mine_ref.shape
    swapped = lax.axis_index("dout") == 1
    for h, (first, second) in enumerate(((mine_ref, other_ref), (other_ref, mine_ref))):
        acts = jnp.where(swapped, second[...], first[...]).astype(jnp.float32)
        for q in range(proj_ref.shape[0]):
            terms = acts * proj_ref[q, h * half : (h + 1) * half, :]
            lanes = terms[:, :128]
            for at in range(128, width, 128):
                lanes = lanes + terms[:, at : at + 128]
            out_ref[q : q + 1, h * half : (h + 1) * half] = jnp.sum(lanes.T, axis=0, keepdims=True)


def scores_of_acts(mine, other, proj, tokens=()):
    nq, count, _ = proj.shape
    return call(finish_kernel, [mine, other, proj], [((nq, count), jnp.float32)], tokens=tokens)[0]


def cut(activations, out_grads, queries, far, others, pieces):
    count, part = lax.axis_size("dp"), out_grads.shape[0] // lax.axis_size("din")
    rows, (tokens, width), dtype = queries.shape[2], activations.shape, out_grads.dtype
    half = tokens // 2
    if part % 128 or rows % 128:
        me, column = lax.axis_index("dp"), lax.axis_index("din")
        mine = lax.dynamic_slice_in_dim(activations, lax.axis_index("dout") * half, half, 0)
        share = lax.dynamic_slice_in_dim(out_grads, column * part, part, 0)
        away = [lax.dynamic_slice_in_dim(share, (me ^ d) * rows, rows, 1) for d in [far, *others]]
        own = lax.dynamic_slice_in_dim(out_grads, me * rows, rows, 1).T
        turned = [block.T for block in away[1:]]
        return (mine, away[0]), (queries, activations, own, *turned[:-1], *jnp.split(turned[-1], pieces))
    outs = [((half, width), activations.dtype), ((part, rows), dtype)]
    first = fetch(functools.partial(first_kernel, far), [activations, out_grads], outs, [], 2)
    outs = [(queries.shape, queries.dtype), (activations.shape, activations.dtype), ((rows, tokens), dtype)]
    outs += [((rows, part), dtype)] * (len(others) - 1) + [((rows // pieces, part), dtype)] * pieces
    scratch = [pltpu.VMEM((tokens, rows), dtype), pltpu.VMEM((len(others), part, rows), dtype)]
    arrays = [activations, out_grads, queries]
    return first, fetch(functools.partial(rest_kernel, others), arrays, outs, scratch, len(others) + 3)


def on_device(activations, out_grads, queries):
    count, spread = lax.axis_size("dp"), lax.axis_size("din")

    def to_columns(arrived):
        return [arrived] + [trade(arrived, {"din": r}) for r in range(1, spread)]

    def acts_of(block):
        return [block, trade(block, {"dout": 1})]

    far, late = count - 1, count - 2
    early = list(range(1, late))
    pieces = 2
    (mine, far_grads), (queries, own_acts, own, *sent) = cut(
        activations, out_grads, queries, far, early + [late], pieces
    )
    hops = [(mine, mine)]
    hops.append(pass_on(hops[0], 1, count))
    arrived = {d: trade(block, {"dp": d}) for d, block in zip([far, *early], [far_grads, *sent])}

    mix, token = mixed([own_acts], queries, SHORT)
    scores = scores_of_grads([own], mix)
    hops[1] = hold(list(hops[1]), [token])
    for step in range(2, count - 1):
        hops.append(pass_on(hops[-1], step, count))

    mixes, token = {}, scores
    for d in early:
        mixes[d], token = mixed(acts_of(from_partner(hops, d, count)), queries, SHORT, [token])
    tail = [trade(hold([block], [token])[0], {"dp": late}) for block in sent[len(early) :]]
    sides = to_columns(hold([arrived[far]], [*hops[1], *[arrived[d] for d in early]])[0])
    block = from_partner(hops, late, count, [token] + sides)
    end = lax.ppermute(block, "dp", [(1, 0), (count - 2, count - 1)])
    hops.append((end, end))

    proj, token = projected(sides, queries, SHORT, [token])
    terms = []
    for d in early:
        sides = to_columns(hold([arrived[d]], hops[1])[0])
        token = scores_of_grads(sides, mixes[d], [token])
        terms.append(trade(token, {"dp": d}))

    tail = [to_columns(hold([piece], [token], LONG)[0]) for piece in tail]
    mix, done = mixed(acts_of(block), queries, SHORT, [token])
    block = from_partner(hops, far, count, [done])
    terms.append(trade(scores_of_acts(*acts_of(block), proj), {"dp": far}))
    sides = [list(hold(sides, [done])) for sides in zip(*tail)]
    terms.append(trade(scores_of_grads(sides, mix, (), LONG), {"dp": late}))
    return over_chips(sum(terms, scores), spread)


def over_chips(scores, spread):
    scores = scores + trade(scores, {"dout": 1})
    return scores + sum(trade(scores, {"din": r}) for r in range(1, spread))


def solution(mesh):
    placed = (P(("groups", "dp"), "din"), P(("groups", "dp"), "dout"), P(None, "dout", "dp", "din"))
    return jax.shard_map(
        on_device, mesh=mesh, in_specs=placed, out_specs=P(None, ("groups", "dp")), check_vma=False
    )
```

```python
import functools
import math

import jax
import jax.numpy as jnp
from jax import lax
from jax.experimental import pallas as pl
from jax.experimental.pallas import tpu as pltpu
from jax.sharding import PartitionSpec as P


LONG, SHORT = 14_000_000_000, 1_000_000


def trade(block, steps, backwards=False):
    axes = tuple(steps)
    sizes = [lax.axis_size(axis) for axis in axes]
    mask = 0
    for axis, size in zip(axes, sizes):
        mask = mask * size + steps[axis]
    route = [(i, i ^ mask) for i in range(math.prod(sizes))]
    return lax.ppermute(block, axes, route[::-1] if backwards else route)


def pass_on(block, step, count):
    up = lax.ppermute(block[0], "dp", [(i, i + 1) for i in range(step - 1, count - 1)])
    down = lax.ppermute(block[1], "dp", [(i, i - 1) for i in range(1, count - step + 1)])
    return up, down


ANYWHERE = pl.BlockSpec(memory_space=pl.ANY)
NEAR = pl.BlockSpec(memory_space=pltpu.VMEM)


def call(kernel, arrays, outs, flops=1024, tokens=(), scratch=()):
    skip = len(tokens)

    def body(*refs):
        kernel(*refs[: len(arrays)], *refs[len(arrays) + skip :])

    return pl.pallas_call(
        body,
        in_specs=[NEAR] * len(arrays) + [ANYWHERE] * skip,
        out_specs=[NEAR] * len(outs),
        out_shape=[pltpu.VMEM(shape, dtype) for shape, dtype in outs],
        scratch_shapes=list(scratch),
        compiler_params=pltpu.CompilerParams(vmem_limit_bytes=12 * 1024 * 1024),
        cost_estimate=pl.CostEstimate(flops=flops, bytes_accessed=1024, transcendentals=0),
    )(*[pltpu.with_memory_space_constraint(array, pltpu.VMEM) for array in arrays], *tokens)


def fetch(kernel, arrays, outs, scratch, copies):
    return pl.pallas_call(
        kernel,
        in_specs=[ANYWHERE] * len(arrays),
        out_specs=[NEAR] * len(outs),
        out_shape=[pltpu.VMEM(shape, dtype) for shape, dtype in outs],
        scratch_shapes=[*scratch, pltpu.SemaphoreType.DMA((copies,))],
        compiler_params=pltpu.CompilerParams(vmem_limit_bytes=12 * 1024 * 1024),
        cost_estimate=pl.CostEstimate(flops=1024, bytes_accessed=1024, transcendentals=0),
    )(*[pltpu.with_memory_space_constraint(array, pltpu.HBM) for array in arrays])


def grads_block(grads_ref, device, part, rows):
    first = pl.multiple_of(lax.axis_index("din") * part, part)
    return grads_ref.at[pl.ds(first, part), pl.ds(pl.multiple_of(device * rows, rows), rows)]


def first_kernel(acts_ref, mine_ref, arrived):
    half = mine_ref.shape[0]
    rows = pl.ds(pl.multiple_of(lax.axis_index("dout") * half, half), half)
    copy = pltpu.make_async_copy(acts_ref.at[rows, :], mine_ref, arrived.at[0])
    copy.start()
    copy.wait()


def rest_kernel(far, steps, acts_ref, grads_ref, query_ref, near_query, near_acts, far_out, own_out, *refs):
    outs, own, blocks, arrived = list(refs[:-3]), refs[-3], refs[-2], refs[-1]
    me = lax.axis_index("dp")
    tokens, rows = own.shape
    copies = [pltpu.make_async_copy(grads_ref.at[:, pl.ds(pl.multiple_of(me * rows, rows), rows)], own, arrived.at[0])]
    for k, d in enumerate(steps):
        block = grads_block(grads_ref, me ^ d, *blocks.shape[1:])
        copies.append(pltpu.make_async_copy(block, blocks.at[k], arrived.at[1 + k]))
    block = grads_block(grads_ref, me ^ far, *far_out.shape)
    copies.append(pltpu.make_async_copy(block, far_out, arrived.at[len(steps) + 1]))
    copies.append(pltpu.make_async_copy(acts_ref, near_acts, arrived.at[len(steps) + 2]))
    copies.append(pltpu.make_async_copy(query_ref, near_query, arrived.at[len(steps) + 3]))
    for copy in copies:
        copy.start()
    for k in range(len(steps)):
        copies[1 + k].wait()
        turned, at = blocks[k].astype(jnp.float32).T.astype(blocks.dtype), 0
        while at < rows:
            out = outs.pop(0)
            out[...] = turned[at : at + out.shape[0]]
            at += out.shape[0]
    copies[0].wait()
    own_out[...] = own[...].astype(jnp.float32).T.astype(own_out.dtype)
    for copy in copies[-3:]:
        copy.wait()


def hold(blocks, tokens, flops=1024):
    count = len(blocks)
    return pl.pallas_call(
        lambda *refs: None,
        in_specs=[ANYWHERE] * (count + len(tokens)),
        out_specs=[ANYWHERE] * count,
        out_shape=[jax.ShapeDtypeStruct(block.shape, block.dtype) for block in blocks],
        input_output_aliases={i: i for i in range(count)},
        compiler_params=pltpu.CompilerParams(vmem_limit_bytes=1024 * 1024),
        cost_estimate=pl.CostEstimate(flops=flops, bytes_accessed=1024, transcendentals=0),
    )(*blocks, *tokens)


def pick_kernel(choice, *refs):
    *blocks, out_ref = refs
    me = lax.axis_index("dp")
    where = functools.reduce(lambda found, z: jnp.where(me == z, choice[z], found), range(len(choice)), 0)
    for k, block in enumerate(blocks):

        @pl.when(where == k)
        def _():
            out_ref[...] = block[...]


def from_partner(hops, d, count, tokens=()):
    sources, choice = [], []
    for z in range(count):
        away = z - (z ^ d)
        source = (abs(away), int(away < 0 and abs(away) < count - 1))
        if source not in sources:
            sources.append(source)
        choice.append(sources.index(source))
    blocks = [hops[step][way] for step, way in sources]
    outs = [(blocks[0].shape, blocks[0].dtype)]
    return call(functools.partial(pick_kernel, choice), blocks, outs, tokens=tokens)[0]


def joined(parts, axis):
    parts = [part[...] for part in parts]
    if len(parts) == 1:
        return parts[0]
    column, found = lax.axis_index("din"), []
    for p in range(len(parts)):
        chosen = parts[0]
        for r in range(1, len(parts)):
            chosen = jnp.where(column == p ^ r, parts[r], chosen)
        found.append(chosen)
    return jnp.concatenate(found, axis=axis)


MARK = (8, 128), jnp.float32


def mix_kernel(*refs):
    *parts, query_ref, out_ref, mark_ref, acts = refs
    mark_ref[...] = jnp.zeros_like(mark_ref)
    half = parts[0].shape[0]
    first = lax.axis_index("dout") * half if len(parts) > 1 else 0
    for part, at in zip(parts, (first, half - first)):
        acts[pl.ds(pl.multiple_of(at, half), half), :] = part[...]
    nq, _, depth, _ = query_ref.shape
    tile = depth // 2

    def step(at, _):
        q, rows = at // 2, pl.ds(pl.multiple_of(at % 2 * tile, tile), tile)
        out_ref[q, rows, :] = lax.dot_general(
            query_ref[q, 0, rows, :], acts[...], (((1,), (1,)), ((), ())), preferred_element_type=jnp.float32
        )
        return 0

    lax.fori_loop(0, 2 * nq, step, 0)


def mixed(parts, queries, flops, tokens=()):
    nq, _, depth, width = queries.shape
    tokens_here = sum(part.shape[0] for part in parts)
    outs = [((nq, depth, tokens_here), jnp.float32), MARK]
    scratch = [pltpu.VMEM((tokens_here, width), queries.dtype)]
    return call(mix_kernel, [*parts, queries], outs, flops, tokens, scratch)


def score_kernel(pieces, *refs):
    *parts, mix_ref, out_ref = refs
    size = mix_ref.shape[1] // pieces
    for p in range(pieces):
        grads = joined(parts[p::pieces], 1).astype(jnp.float32)
        for q in range(mix_ref.shape[0]):
            term = jnp.sum(grads * mix_ref[q, p * size : (p + 1) * size], axis=0, keepdims=True)
            out_ref[q : q + 1, :] = term if p == 0 else out_ref[q : q + 1, :] + term


def scores_of_grads(parts, mix, tokens=(), flops=1024):
    nq, _, count = mix.shape
    parts = [part if isinstance(part, list) else [part] for part in parts]
    kernel = functools.partial(score_kernel, len(parts[0]))
    return call(kernel, [*sum(parts, []), mix], [((nq, count), jnp.float32)], flops, tokens)[0]


def project_kernel(*refs):
    *parts, query_ref, out_ref, mark_ref, grads = refs
    mark_ref[...] = jnp.zeros_like(mark_ref)
    grads[...] = joined(parts, 0)
    nq, _, _, width = query_ref.shape
    tile = width // 2

    def step(at, _):
        q, columns = at // 2, pl.ds(pl.multiple_of(at % 2 * tile, tile), tile)
        out_ref[q, :, columns] = jnp.dot(
            grads[...], query_ref[q, 0, :, columns], preferred_element_type=jnp.float32
        )
        return 0

    lax.fori_loop(0, 2 * nq, step, 0)


def projected(parts, queries, flops, tokens=()):
    nq, _, depth, width = queries.shape
    count = sum(part.shape[0] for part in parts)
    outs = [((nq, count, width), jnp.float32), MARK]
    scratch = [pltpu.VMEM((count, depth), queries.dtype)]
    return call(project_kernel, [*parts, queries], outs, flops, tokens, scratch)


def finish_kernel(mine_ref, other_ref, proj_ref, out_ref):
    half, width = mine_ref.shape
    swapped = lax.axis_index("dout") == 1
    for h, (first, second) in enumerate(((mine_ref, other_ref), (other_ref, mine_ref))):
        acts = jnp.where(swapped, second[...], first[...]).astype(jnp.float32)
        for q in range(proj_ref.shape[0]):
            terms = acts * proj_ref[q, h * half : (h + 1) * half, :]
            lanes = terms[:, :128]
            for at in range(128, width, 128):
                lanes = lanes + terms[:, at : at + 128]
            out_ref[q : q + 1, h * half : (h + 1) * half] = jnp.sum(lanes.T, axis=0, keepdims=True)


def scores_of_acts(mine, other, proj, tokens=()):
    nq, count, _ = proj.shape
    return call(finish_kernel, [mine, other, proj], [((nq, count), jnp.float32)], tokens=tokens)[0]


def cut(activations, out_grads, queries, far, others, pieces):
    count, part = lax.axis_size("dp"), out_grads.shape[0] // lax.axis_size("din")
    rows, (tokens, width), dtype = queries.shape[2], activations.shape, out_grads.dtype
    half = tokens // 2
    if part % 128 or rows % 128:
        me, column = lax.axis_index("dp"), lax.axis_index("din")
        mine = lax.dynamic_slice_in_dim(activations, lax.axis_index("dout") * half, half, 0)
        share = lax.dynamic_slice_in_dim(out_grads, column * part, part, 0)
        away = [lax.dynamic_slice_in_dim(share, (me ^ d) * rows, rows, 1) for d in [far, *others]]
        own = lax.dynamic_slice_in_dim(out_grads, me * rows, rows, 1).T
        turned = [block.T for block in away[1:]]
        return mine, (queries, activations, away[0], own, *turned[:-1], *jnp.split(turned[-1], pieces))
    first, = fetch(first_kernel, [activations], [((half, width), activations.dtype)], [], 1)
    outs = [(queries.shape, queries.dtype), (activations.shape, activations.dtype)]
    outs += [((part, rows), dtype), ((rows, tokens), dtype)]
    outs += [((rows, part), dtype)] * (len(others) - 1) + [((rows // pieces, part), dtype)] * pieces
    scratch = [pltpu.VMEM((tokens, rows), dtype), pltpu.VMEM((len(others), part, rows), dtype)]
    arrays = [activations, out_grads, queries]
    return first, fetch(functools.partial(rest_kernel, far, others), arrays, outs, scratch, len(others) + 4)


def on_device(activations, out_grads, queries):
    count, spread = lax.axis_size("dp"), lax.axis_size("din")

    def to_columns(arrived):
        return [arrived] + [trade(arrived, {"din": r}) for r in range(1, spread)]

    def acts_of(block):
        return [block, trade(block, {"dout": 1})]

    far, late = count - 1, count - 2
    early = list(range(1, late))
    pieces = 2
    mine, (queries, own_acts, far_grads, own, *sent) = cut(
        activations, out_grads, queries, far, early + [late], pieces
    )
    hops = [(mine, mine)]
    hops.append(pass_on(hops[0], 1, count))
    arrived = {d: trade(block, {"dp": d}) for d, block in zip([far, *early], [far_grads, *sent])}

    mix, token = mixed([own_acts], queries, SHORT)
    scores = scores_of_grads([own], mix)
    hops[1] = hold(list(hops[1]), [token])
    for step in range(2, count - 1):
        hops.append(pass_on(hops[-1], step, count))

    mixes, token = {}, scores
    for d in early:
        mixes[d], token = mixed(acts_of(from_partner(hops, d, count)), queries, SHORT, [token])
    tail = [trade(hold([block], [token])[0], {"dp": late}) for block in sent[len(early) :]]
    sides = to_columns(hold([arrived[far]], [*hops[1], *[arrived[d] for d in early]])[0])
    block = from_partner(hops, late, count, [token] + sides)
    end = lax.ppermute(block, "dp", [(1, 0), (count - 2, count - 1)])
    hops.append((end, end))

    proj, token = projected(sides, queries, SHORT, [token])
    terms = []
    for d in early:
        sides = to_columns(hold([arrived[d]], hops[1])[0])
        token = scores_of_grads(sides, mixes[d], [token])
        terms.append(trade(token, {"dp": d}))

    mix, done = mixed(acts_of(block), queries, SHORT, [token])
    tail = [to_columns(hold([piece], [done if p else token], LONG)[0]) for p, piece in enumerate(tail)]
    token = scores_of_acts(*acts_of(from_partner(hops, far, count, [done])), proj)
    terms.append(trade(token, {"dp": far}))
    terms.append(trade(scores_of_grads([list(sides) for sides in zip(*tail)], mix, [token], LONG), {"dp": late}))
    return over_chips(sum(terms, scores), spread)


def over_chips(scores, spread):
    scores = scores + trade(scores, {"dout": 1})
    return scores + sum(trade(scores, {"din": r}) for r in range(1, spread))


def solution(mesh):
    placed = (P(("groups", "dp"), "din"), P(("groups", "dp"), "dout"), P(None, "dout", "dp", "din"))
    return jax.shard_map(
        on_device, mesh=mesh, in_specs=placed, out_specs=P(None, ("groups", "dp")), check_vma=False
    )
```

```python
import functools
import math

import jax
import jax.numpy as jnp
from jax import lax
from jax.experimental import pallas as pl
from jax.experimental.pallas import tpu as pltpu
from jax.sharding import PartitionSpec as P


LONG, SHORT = 14_000_000_000, 1_000_000


def trade(block, steps, backwards=False):
    axes = tuple(steps)
    sizes = [lax.axis_size(axis) for axis in axes]
    mask = 0
    for axis, size in zip(axes, sizes):
        mask = mask * size + steps[axis]
    route = [(i, i ^ mask) for i in range(math.prod(sizes))]
    return lax.ppermute(block, axes, route[::-1] if backwards else route)


def pass_on(block, step, count):
    up = lax.ppermute(block[0], "dp", [(i, i + 1) for i in range(step - 1, count - 1)])
    down = lax.ppermute(block[1], "dp", [(i, i - 1) for i in range(1, count - step + 1)])
    return up, down


ANYWHERE = pl.BlockSpec(memory_space=pl.ANY)
NEAR = pl.BlockSpec(memory_space=pltpu.VMEM)


def call(kernel, arrays, outs, flops=1024, tokens=(), scratch=()):
    skip = len(tokens)

    def body(*refs):
        kernel(*refs[: len(arrays)], *refs[len(arrays) + skip :])

    return pl.pallas_call(
        body,
        in_specs=[NEAR] * len(arrays) + [ANYWHERE] * skip,
        out_specs=[NEAR] * len(outs),
        out_shape=[pltpu.VMEM(shape, dtype) for shape, dtype in outs],
        scratch_shapes=list(scratch),
        compiler_params=pltpu.CompilerParams(vmem_limit_bytes=12 * 1024 * 1024),
        cost_estimate=pl.CostEstimate(flops=flops, bytes_accessed=1024, transcendentals=0),
    )(*[pltpu.with_memory_space_constraint(array, pltpu.VMEM) for array in arrays], *tokens)


def fetch(kernel, arrays, outs, scratch, copies):
    return pl.pallas_call(
        kernel,
        in_specs=[ANYWHERE] * len(arrays),
        out_specs=[NEAR] * len(outs),
        out_shape=[pltpu.VMEM(shape, dtype) for shape, dtype in outs],
        scratch_shapes=[*scratch, pltpu.SemaphoreType.DMA((copies,))],
        compiler_params=pltpu.CompilerParams(vmem_limit_bytes=12 * 1024 * 1024),
        cost_estimate=pl.CostEstimate(flops=1024, bytes_accessed=1024, transcendentals=0),
    )(*[pltpu.with_memory_space_constraint(array, pltpu.HBM) for array in arrays])


def grads_block(grads_ref, device, part, rows):
    first = pl.multiple_of(lax.axis_index("din") * part, part)
    return grads_ref.at[pl.ds(first, part), pl.ds(pl.multiple_of(device * rows, rows), rows)]


def first_kernel(acts_ref, mine_ref, arrived):
    half = mine_ref.shape[0]
    rows = pl.ds(pl.multiple_of(lax.axis_index("dout") * half, half), half)
    copy = pltpu.make_async_copy(acts_ref.at[rows, :], mine_ref, arrived.at[0])
    copy.start()
    copy.wait()


def rest_kernel(far, steps, acts_ref, grads_ref, query_ref, near_query, near_acts, far_out, own_out, *refs):
    outs, own, blocks, arrived = list(refs[:-3]), refs[-3], refs[-2], refs[-1]
    me = lax.axis_index("dp")
    tokens, rows = own.shape
    copies = [pltpu.make_async_copy(grads_ref.at[:, pl.ds(pl.multiple_of(me * rows, rows), rows)], own, arrived.at[0])]
    for k, d in enumerate(steps):
        block = grads_block(grads_ref, me ^ d, *blocks.shape[1:])
        copies.append(pltpu.make_async_copy(block, blocks.at[k], arrived.at[1 + k]))
    block = grads_block(grads_ref, me ^ far, *far_out.shape)
    copies.append(pltpu.make_async_copy(block, far_out, arrived.at[len(steps) + 1]))
    copies.append(pltpu.make_async_copy(acts_ref, near_acts, arrived.at[len(steps) + 2]))
    copies.append(pltpu.make_async_copy(query_ref, near_query, arrived.at[len(steps) + 3]))
    for copy in copies:
        copy.start()
    for k in range(len(steps)):
        copies[1 + k].wait()
        turned, at = blocks[k].astype(jnp.float32).T.astype(blocks.dtype), 0
        while at < rows:
            out = outs.pop(0)
            out[...] = turned[at : at + out.shape[0]]
            at += out.shape[0]
    copies[0].wait()
    own_out[...] = own[...].astype(jnp.float32).T.astype(own_out.dtype)
    for copy in copies[-3:]:
        copy.wait()


def hold(blocks, tokens, flops=1024):
    count = len(blocks)
    return pl.pallas_call(
        lambda *refs: None,
        in_specs=[ANYWHERE] * (count + len(tokens)),
        out_specs=[ANYWHERE] * count,
        out_shape=[jax.ShapeDtypeStruct(block.shape, block.dtype) for block in blocks],
        input_output_aliases={i: i for i in range(count)},
        compiler_params=pltpu.CompilerParams(vmem_limit_bytes=1024 * 1024),
        cost_estimate=pl.CostEstimate(flops=flops, bytes_accessed=1024, transcendentals=0),
    )(*blocks, *tokens)


def pick_kernel(choice, *refs):
    *blocks, out_ref = refs
    me = lax.axis_index("dp")
    where = functools.reduce(lambda found, z: jnp.where(me == z, choice[z], found), range(len(choice)), 0)
    for k, block in enumerate(blocks):

        @pl.when(where == k)
        def _():
            out_ref[...] = block[...]


def from_partner(hops, d, count, tokens=()):
    sources, choice = [], []
    for z in range(count):
        away = z - (z ^ d)
        source = (abs(away), int(away < 0 and abs(away) < count - 1))
        if source not in sources:
            sources.append(source)
        choice.append(sources.index(source))
    blocks = [hops[step][way] for step, way in sources]
    outs = [(blocks[0].shape, blocks[0].dtype)]
    return call(functools.partial(pick_kernel, choice), blocks, outs, tokens=tokens)[0]


def joined(parts, axis):
    parts = [part[...] for part in parts]
    if len(parts) == 1:
        return parts[0]
    column, found = lax.axis_index("din"), []
    for p in range(len(parts)):
        chosen = parts[0]
        for r in range(1, len(parts)):
            chosen = jnp.where(column == p ^ r, parts[r], chosen)
        found.append(chosen)
    return jnp.concatenate(found, axis=axis)


MARK = (8, 128), jnp.float32


def mix_kernel(*refs):
    *parts, query_ref, out_ref, mark_ref, acts = refs
    mark_ref[...] = jnp.zeros_like(mark_ref)
    half = parts[0].shape[0]
    first = lax.axis_index("dout") * half if len(parts) > 1 else 0
    for part, at in zip(parts, (first, half - first)):
        acts[pl.ds(pl.multiple_of(at, half), half), :] = part[...]
    nq, _, depth, _ = query_ref.shape
    tile = depth // 2

    def step(at, _):
        q, rows = at // 2, pl.ds(pl.multiple_of(at % 2 * tile, tile), tile)
        out_ref[q, rows, :] = lax.dot_general(
            query_ref[q, 0, rows, :], acts[...], (((1,), (1,)), ((), ())), preferred_element_type=jnp.float32
        )
        return 0

    lax.fori_loop(0, 2 * nq, step, 0)


def mixed(parts, queries, flops, tokens=()):
    nq, _, depth, width = queries.shape
    tokens_here = sum(part.shape[0] for part in parts)
    outs = [((nq, depth, tokens_here), jnp.float32), MARK]
    scratch = [pltpu.VMEM((tokens_here, width), queries.dtype)]
    return call(mix_kernel, [*parts, queries], outs, flops, tokens, scratch)


def score_kernel(pieces, *refs):
    *parts, mix_ref, out_ref = refs
    size = mix_ref.shape[1] // pieces
    for p in range(pieces):
        grads = joined(parts[p::pieces], 1).astype(jnp.float32)
        for q in range(mix_ref.shape[0]):
            term = jnp.sum(grads * mix_ref[q, p * size : (p + 1) * size], axis=0, keepdims=True)
            out_ref[q : q + 1, :] = term if p == 0 else out_ref[q : q + 1, :] + term


def scores_of_grads(parts, mix, tokens=(), flops=1024):
    nq, _, count = mix.shape
    parts = [part if isinstance(part, list) else [part] for part in parts]
    kernel = functools.partial(score_kernel, len(parts[0]))
    return call(kernel, [*sum(parts, []), mix], [((nq, count), jnp.float32)], flops, tokens)[0]


def project_kernel(*refs):
    *parts, query_ref, out_ref, mark_ref, grads = refs
    mark_ref[...] = jnp.zeros_like(mark_ref)
    grads[...] = joined(parts, 0)
    nq, _, _, width = query_ref.shape
    tile = width // 2

    def step(at, _):
        q, columns = at // 2, pl.ds(pl.multiple_of(at % 2 * tile, tile), tile)
        out_ref[q, :, columns] = jnp.dot(
            grads[...], query_ref[q, 0, :, columns], preferred_element_type=jnp.float32
        )
        return 0

    lax.fori_loop(0, 2 * nq, step, 0)


def projected(parts, queries, flops, tokens=()):
    nq, _, depth, width = queries.shape
    count = sum(part.shape[0] for part in parts)
    outs = [((nq, count, width), jnp.float32), MARK]
    scratch = [pltpu.VMEM((count, depth), queries.dtype)]
    return call(project_kernel, [*parts, queries], outs, flops, tokens, scratch)


def finish_kernel(mine_ref, other_ref, proj_ref, out_ref):
    half, width = mine_ref.shape
    swapped = lax.axis_index("dout") == 1
    for h, (first, second) in enumerate(((mine_ref, other_ref), (other_ref, mine_ref))):
        acts = jnp.where(swapped, second[...], first[...]).astype(jnp.float32)
        for q in range(proj_ref.shape[0]):
            terms = acts * proj_ref[q, h * half : (h + 1) * half, :]
            lanes = terms[:, :128]
            for at in range(128, width, 128):
                lanes = lanes + terms[:, at : at + 128]
            out_ref[q : q + 1, h * half : (h + 1) * half] = jnp.sum(lanes.T, axis=0, keepdims=True)


def scores_of_acts(mine, other, proj, tokens=()):
    nq, count, _ = proj.shape
    return call(finish_kernel, [mine, other, proj], [((nq, count), jnp.float32)], tokens=tokens)[0]


def cut(activations, out_grads, queries, far, others, pieces):
    count, part = lax.axis_size("dp"), out_grads.shape[0] // lax.axis_size("din")
    rows, (tokens, width), dtype = queries.shape[2], activations.shape, out_grads.dtype
    half = tokens // 2
    if part % 128 or rows % 128:
        me, column = lax.axis_index("dp"), lax.axis_index("din")
        mine = lax.dynamic_slice_in_dim(activations, lax.axis_index("dout") * half, half, 0)
        share = lax.dynamic_slice_in_dim(out_grads, column * part, part, 0)
        away = [lax.dynamic_slice_in_dim(share, (me ^ d) * rows, rows, 1) for d in [far, *others]]
        own = lax.dynamic_slice_in_dim(out_grads, me * rows, rows, 1).T
        turned = [block.T for block in away[1:]]
        return mine, (queries, activations, away[0], own, *turned[:-1], *jnp.split(turned[-1], pieces))
    first, = fetch(first_kernel, [activations], [((half, width), activations.dtype)], [], 1)
    outs = [(queries.shape, queries.dtype), (activations.shape, activations.dtype)]
    outs += [((part, rows), dtype), ((rows, tokens), dtype)]
    outs += [((rows, part), dtype)] * (len(others) - 1) + [((rows // pieces, part), dtype)] * pieces
    scratch = [pltpu.VMEM((tokens, rows), dtype), pltpu.VMEM((len(others), part, rows), dtype)]
    arrays = [activations, out_grads, queries]
    return first, fetch(functools.partial(rest_kernel, far, others), arrays, outs, scratch, len(others) + 4)


def on_device(activations, out_grads, queries):
    count, spread = lax.axis_size("dp"), lax.axis_size("din")

    def to_columns(arrived):
        return [arrived] + [trade(arrived, {"din": r}) for r in range(1, spread)]

    def acts_of(block):
        return [block, trade(block, {"dout": 1})]

    far, late = count - 1, count - 2
    early = list(range(1, late))
    pieces = 2
    mine, (queries, own_acts, far_grads, own, *sent) = cut(
        activations, out_grads, queries, far, early + [late], pieces
    )
    hops = [(mine, mine)]
    hops.append(pass_on(hops[0], 1, count))
    arrived = {d: trade(block, {"dp": d}) for d, block in zip(early, sent)}

    mix, token = mixed([own_acts], queries, SHORT)
    arrived[far] = trade(hold([far_grads], [token])[0], {"dp": far})
    scores = scores_of_grads([own], mix)
    hops[1] = hold(list(hops[1]), [token])
    for step in range(2, count - 1):
        hops.append(pass_on(hops[-1], step, count))

    mixes, token = {}, scores
    for d in early:
        mixes[d], token = mixed(acts_of(from_partner(hops, d, count)), queries, SHORT, [token])
    tail = [trade(hold([block], [token])[0], {"dp": late}) for block in sent[len(early) :]]
    sides = to_columns(hold([arrived[far]], [token])[0])
    block = from_partner(hops, late, count, [token])
    end = lax.ppermute(block, "dp", [(1, 0), (count - 2, count - 1)])
    hops.append((end, end))

    proj, token = projected(sides, queries, SHORT, [token])
    terms = []
    for d in early:
        sides = to_columns(hold([arrived[d]], hops[1])[0])
        token = scores_of_grads(sides, mixes[d], [token])
        terms.append(trade(token, {"dp": d}))

    mix, done = mixed(acts_of(block), queries, SHORT, [token])
    tail = [to_columns(hold([piece], [done if p else token], LONG)[0]) for p, piece in enumerate(tail)]
    block = from_partner(hops, far, count, [done])
    terms.append(trade(scores_of_acts(*acts_of(block), proj), {"dp": far}))
    terms.append(trade(scores_of_grads([list(sides) for sides in zip(*tail)], mix, (), LONG), {"dp": late}))
    return over_chips(sum(terms, scores), spread)


def over_chips(scores, spread):
    scores = scores + trade(scores, {"dout": 1})
    return scores + sum(trade(scores, {"din": r}) for r in range(1, spread))


def solution(mesh):
    placed = (P(("groups", "dp"), "din"), P(("groups", "dp"), "dout"), P(None, "dout", "dp", "din"))
    return jax.shard_map(
        on_device, mesh=mesh, in_specs=placed, out_specs=P(None, ("groups", "dp")), check_vma=False
    )
```

```python
import functools
import math

import jax
import jax.numpy as jnp
from jax import lax
from jax.experimental import pallas as pl
from jax.experimental.pallas import tpu as pltpu
from jax.sharding import PartitionSpec as P


LONG, MIDDLE, SHORT = 14_000_000_000, 8_000_000_000, 1_000_000


def trade(block, steps, backwards=False):
    axes = tuple(steps)
    sizes = [lax.axis_size(axis) for axis in axes]
    mask = 0
    for axis, size in zip(axes, sizes):
        mask = mask * size + steps[axis]
    route = [(i, i ^ mask) for i in range(math.prod(sizes))]
    return lax.ppermute(block, axes, route[::-1] if backwards else route)


def pass_on(block, step, count):
    up = lax.ppermute(block[0], "dp", [(i, i + 1) for i in range(step - 1, count - 1)])
    down = lax.ppermute(block[1], "dp", [(i, i - 1) for i in range(1, count - step + 1)])
    return up, down


ANYWHERE = pl.BlockSpec(memory_space=pl.ANY)
NEAR = pl.BlockSpec(memory_space=pltpu.VMEM)


def call(kernel, arrays, outs, flops=1024, tokens=(), scratch=()):
    skip = len(tokens)

    def body(*refs):
        kernel(*refs[: len(arrays)], *refs[len(arrays) + skip :])

    return pl.pallas_call(
        body,
        in_specs=[NEAR] * len(arrays) + [ANYWHERE] * skip,
        out_specs=[NEAR] * len(outs),
        out_shape=[pltpu.VMEM(shape, dtype) for shape, dtype in outs],
        scratch_shapes=list(scratch),
        compiler_params=pltpu.CompilerParams(vmem_limit_bytes=12 * 1024 * 1024),
        cost_estimate=pl.CostEstimate(flops=flops, bytes_accessed=1024, transcendentals=0),
    )(*[pltpu.with_memory_space_constraint(array, pltpu.VMEM) for array in arrays], *tokens)


def fetch(kernel, arrays, outs, scratch, copies):
    return pl.pallas_call(
        kernel,
        in_specs=[ANYWHERE] * len(arrays),
        out_specs=[NEAR] * len(outs),
        out_shape=[pltpu.VMEM(shape, dtype) for shape, dtype in outs],
        scratch_shapes=[*scratch, pltpu.SemaphoreType.DMA((copies,))],
        compiler_params=pltpu.CompilerParams(vmem_limit_bytes=12 * 1024 * 1024),
        cost_estimate=pl.CostEstimate(flops=1024, bytes_accessed=1024, transcendentals=0),
    )(*[pltpu.with_memory_space_constraint(array, pltpu.HBM) for array in arrays])


def grads_block(grads_ref, device, part, rows):
    first = pl.multiple_of(lax.axis_index("din") * part, part)
    return grads_ref.at[pl.ds(first, part), pl.ds(pl.multiple_of(device * rows, rows), rows)]


def first_kernel(acts_ref, mine_ref, arrived):
    half = mine_ref.shape[0]
    rows = pl.ds(pl.multiple_of(lax.axis_index("dout") * half, half), half)
    copy = pltpu.make_async_copy(acts_ref.at[rows, :], mine_ref, arrived.at[0])
    copy.start()
    copy.wait()


def rest_kernel(far, steps, acts_ref, grads_ref, query_ref, near_query, near_acts, far_out, own_out, *refs):
    outs, own, blocks, arrived = list(refs[:-3]), refs[-3], refs[-2], refs[-1]
    me = lax.axis_index("dp")
    tokens, rows = own.shape
    copies = [pltpu.make_async_copy(grads_ref.at[:, pl.ds(pl.multiple_of(me * rows, rows), rows)], own, arrived.at[0])]
    for k, d in enumerate(steps):
        block = grads_block(grads_ref, me ^ d, *blocks.shape[1:])
        copies.append(pltpu.make_async_copy(block, blocks.at[k], arrived.at[1 + k]))
    block = grads_block(grads_ref, me ^ far, *far_out.shape)
    copies.append(pltpu.make_async_copy(block, far_out, arrived.at[len(steps) + 1]))
    copies.append(pltpu.make_async_copy(acts_ref, near_acts, arrived.at[len(steps) + 2]))
    copies.append(pltpu.make_async_copy(query_ref, near_query, arrived.at[len(steps) + 3]))
    for copy in copies:
        copy.start()
    for k in range(len(steps)):
        copies[1 + k].wait()
        turned, at = blocks[k].astype(jnp.float32).T.astype(blocks.dtype), 0
        while at < rows:
            out = outs.pop(0)
            out[...] = turned[at : at + out.shape[0]]
            at += out.shape[0]
    copies[0].wait()
    own_out[...] = own[...].astype(jnp.float32).T.astype(own_out.dtype)
    for copy in copies[-3:]:
        copy.wait()


def hold(blocks, tokens, flops=1024):
    count = len(blocks)
    return pl.pallas_call(
        lambda *refs: None,
        in_specs=[ANYWHERE] * (count + len(tokens)),
        out_specs=[ANYWHERE] * count,
        out_shape=[jax.ShapeDtypeStruct(block.shape, block.dtype) for block in blocks],
        input_output_aliases={i: i for i in range(count)},
        compiler_params=pltpu.CompilerParams(vmem_limit_bytes=1024 * 1024),
        cost_estimate=pl.CostEstimate(flops=flops, bytes_accessed=1024, transcendentals=0),
    )(*blocks, *tokens)


def pick_kernel(choice, *refs):
    *blocks, out_ref = refs
    me = lax.axis_index("dp")
    where = functools.reduce(lambda found, z: jnp.where(me == z, choice[z], found), range(len(choice)), 0)
    for k, block in enumerate(blocks):

        @pl.when(where == k)
        def _():
            out_ref[...] = block[...]


def from_partner(hops, d, count, tokens=(), flops=1024):
    sources, choice = [], []
    for z in range(count):
        away = z - (z ^ d)
        source = (abs(away), int(away < 0 and abs(away) < count - 1))
        if source not in sources:
            sources.append(source)
        choice.append(sources.index(source))
    blocks = [hops[step][way] for step, way in sources]
    outs = [(blocks[0].shape, blocks[0].dtype)]
    return call(functools.partial(pick_kernel, choice), blocks, outs, flops, tokens)[0]


def joined(parts, axis):
    parts = [part[...] for part in parts]
    if len(parts) == 1:
        return parts[0]
    column, found = lax.axis_index("din"), []
    for p in range(len(parts)):
        chosen = parts[0]
        for r in range(1, len(parts)):
            chosen = jnp.where(column == p ^ r, parts[r], chosen)
        found.append(chosen)
    return jnp.concatenate(found, axis=axis)


MARK = (8, 128), jnp.float32


def mix_kernel(*refs):
    *parts, query_ref, out_ref, mark_ref, acts = refs
    mark_ref[...] = jnp.zeros_like(mark_ref)
    half = parts[0].shape[0]
    first = lax.axis_index("dout") * half if len(parts) > 1 else 0
    for part, at in zip(parts, (first, half - first)):
        acts[pl.ds(pl.multiple_of(at, half), half), :] = part[...]
    nq, _, depth, _ = query_ref.shape
    tile = depth // 2

    def step(at, _):
        q, rows = at // 2, pl.ds(pl.multiple_of(at % 2 * tile, tile), tile)
        out_ref[q, rows, :] = lax.dot_general(
            query_ref[q, 0, rows, :], acts[...], (((1,), (1,)), ((), ())), preferred_element_type=jnp.float32
        )
        return 0

    lax.fori_loop(0, 2 * nq, step, 0)


def mixed(parts, queries, flops, tokens=()):
    nq, _, depth, width = queries.shape
    tokens_here = sum(part.shape[0] for part in parts)
    outs = [((nq, depth, tokens_here), jnp.float32), MARK]
    scratch = [pltpu.VMEM((tokens_here, width), queries.dtype)]
    return call(mix_kernel, [*parts, queries], outs, flops, tokens, scratch)


def score_kernel(pieces, *refs):
    *parts, mix_ref, out_ref = refs
    size = mix_ref.shape[1] // pieces
    for p in range(pieces):
        grads = joined(parts[p::pieces], 1).astype(jnp.float32)
        for q in range(mix_ref.shape[0]):
            term = jnp.sum(grads * mix_ref[q, p * size : (p + 1) * size], axis=0, keepdims=True)
            out_ref[q : q + 1, :] = term if p == 0 else out_ref[q : q + 1, :] + term


def scores_of_grads(parts, mix, tokens=(), flops=1024):
    nq, _, count = mix.shape
    parts = [part if isinstance(part, list) else [part] for part in parts]
    kernel = functools.partial(score_kernel, len(parts[0]))
    return call(kernel, [*sum(parts, []), mix], [((nq, count), jnp.float32)], flops, tokens)[0]


def project_kernel(*refs):
    *parts, query_ref, out_ref, mark_ref, grads = refs
    mark_ref[...] = jnp.zeros_like(mark_ref)
    grads[...] = joined(parts, 0)
    nq, _, _, width = query_ref.shape
    tile = width // 2

    def step(at, _):
        q, columns = at // 2, pl.ds(pl.multiple_of(at % 2 * tile, tile), tile)
        out_ref[q, :, columns] = jnp.dot(
            grads[...], query_ref[q, 0, :, columns], preferred_element_type=jnp.float32
        )
        return 0

    lax.fori_loop(0, 2 * nq, step, 0)


def projected(parts, queries, flops, tokens=()):
    nq, _, depth, width = queries.shape
    count = sum(part.shape[0] for part in parts)
    outs = [((nq, count, width), jnp.float32), MARK]
    scratch = [pltpu.VMEM((count, depth), queries.dtype)]
    return call(project_kernel, [*parts, queries], outs, flops, tokens, scratch)


def finish_kernel(mine_ref, other_ref, proj_ref, out_ref):
    half, width = mine_ref.shape
    swapped = lax.axis_index("dout") == 1
    for h, (first, second) in enumerate(((mine_ref, other_ref), (other_ref, mine_ref))):
        acts = jnp.where(swapped, second[...], first[...]).astype(jnp.float32)
        for q in range(proj_ref.shape[0]):
            terms = acts * proj_ref[q, h * half : (h + 1) * half, :]
            lanes = terms[:, :128]
            for at in range(128, width, 128):
                lanes = lanes + terms[:, at : at + 128]
            out_ref[q : q + 1, h * half : (h + 1) * half] = jnp.sum(lanes.T, axis=0, keepdims=True)


def scores_of_acts(mine, other, proj, tokens=()):
    nq, count, _ = proj.shape
    return call(finish_kernel, [mine, other, proj], [((nq, count), jnp.float32)], tokens=tokens)[0]


def cut(activations, out_grads, queries, far, others, pieces):
    count, part = lax.axis_size("dp"), out_grads.shape[0] // lax.axis_size("din")
    rows, (tokens, width), dtype = queries.shape[2], activations.shape, out_grads.dtype
    half = tokens // 2
    if part % 128 or rows % 128:
        me, column = lax.axis_index("dp"), lax.axis_index("din")
        mine = lax.dynamic_slice_in_dim(activations, lax.axis_index("dout") * half, half, 0)
        share = lax.dynamic_slice_in_dim(out_grads, column * part, part, 0)
        away = [lax.dynamic_slice_in_dim(share, (me ^ d) * rows, rows, 1) for d in [far, *others]]
        own = lax.dynamic_slice_in_dim(out_grads, me * rows, rows, 1).T
        turned = [block.T for block in away[1:]]
        return mine, (queries, activations, away[0], own, *turned[:-1], *jnp.split(turned[-1], pieces))
    first, = fetch(first_kernel, [activations], [((half, width), activations.dtype)], [], 1)
    outs = [(queries.shape, queries.dtype), (activations.shape, activations.dtype)]
    outs += [((part, rows), dtype), ((rows, tokens), dtype)]
    outs += [((rows, part), dtype)] * (len(others) - 1) + [((rows // pieces, part), dtype)] * pieces
    scratch = [pltpu.VMEM((tokens, rows), dtype), pltpu.VMEM((len(others), part, rows), dtype)]
    arrays = [activations, out_grads, queries]
    return first, fetch(functools.partial(rest_kernel, far, others), arrays, outs, scratch, len(others) + 4)


def on_device(activations, out_grads, queries):
    count, spread = lax.axis_size("dp"), lax.axis_size("din")

    def to_columns(arrived):
        return [arrived] + [trade(arrived, {"din": r}) for r in range(1, spread)]

    def acts_of(block):
        return [block, trade(block, {"dout": 1})]

    far, late = count - 1, count - 2
    early = list(range(1, late))
    pieces = 2
    mine, (queries, own_acts, far_grads, own, *sent) = cut(
        activations, out_grads, queries, far, early + [late], pieces
    )
    hops = [(mine, mine)]
    hops.append(pass_on(hops[0], 1, count))
    arrived = {d: trade(block, {"dp": d}) for d, block in zip(early, sent)}

    mix, token = mixed([own_acts], queries, SHORT)
    scores = scores_of_grads([own], mix)
    hops[1] = hold(list(hops[1]), [token])
    for step in range(2, count - 1):
        hops.append(pass_on(hops[-1], step, count))
    arrived[far] = trade(hold([far_grads], hops[1])[0], {"dp": far})

    mixes, token = {}, scores
    for d in early:
        mixes[d], token = mixed(acts_of(from_partner(hops, d, count)), queries, SHORT, [token])
    tail = [trade(hold([block], [token])[0], {"dp": late}) for block in sent[len(early) :]]
    sides = to_columns(hold([arrived[far]], [token])[0])
    block = from_partner(hops, late, count, [token], MIDDLE)
    end = lax.ppermute(block, "dp", [(1, 0), (count - 2, count - 1)])
    hops.append((end, end))

    proj, token = projected(sides, queries, SHORT, [token])
    terms = []
    for d in early:
        sides = to_columns(hold([arrived[d]], hops[1])[0])
        token = scores_of_grads(sides, mixes[d], [token])
        terms.append(trade(token, {"dp": d}))

    mix, done = mixed(acts_of(block), queries, SHORT, [token])
    tail = [to_columns(hold([piece], [done if p else token], LONG)[0]) for p, piece in enumerate(tail)]
    block = from_partner(hops, far, count, [done], MIDDLE)
    terms.append(trade(scores_of_acts(*acts_of(block), proj), {"dp": far}))
    terms.append(trade(scores_of_grads([list(sides) for sides in zip(*tail)], mix, (), LONG), {"dp": late}))
    return over_chips(sum(terms, scores), spread)


def over_chips(scores, spread):
    scores = scores + trade(scores, {"dout": 1})
    return scores + sum(trade(scores, {"din": r}) for r in range(1, spread))


def solution(mesh):
    placed = (P(("groups", "dp"), "din"), P(("groups", "dp"), "dout"), P(None, "dout", "dp", "din"))
    return jax.shard_map(
        on_device, mesh=mesh, in_specs=placed, out_specs=P(None, ("groups", "dp")), check_vma=False
    )
```

```python
import functools
import math

import jax
import jax.numpy as jnp
from jax import lax
from jax.experimental import pallas as pl
from jax.experimental.pallas import tpu as pltpu
from jax.sharding import PartitionSpec as P


LONG, SHORT = 14_000_000_000, 1_000_000


def trade(block, steps, backwards=False):
    axes = tuple(steps)
    sizes = [lax.axis_size(axis) for axis in axes]
    mask = 0
    for axis, size in zip(axes, sizes):
        mask = mask * size + steps[axis]
    route = [(i, i ^ mask) for i in range(math.prod(sizes))]
    return lax.ppermute(block, axes, route[::-1] if backwards else route)


def pass_on(block, step, count):
    up = lax.ppermute(block[0], "dp", [(i, i + 1) for i in range(step - 1, count - 1)])
    down = lax.ppermute(block[1], "dp", [(i, i - 1) for i in range(1, count - step + 1)])
    return up, down


ANYWHERE = pl.BlockSpec(memory_space=pl.ANY)
NEAR = pl.BlockSpec(memory_space=pltpu.VMEM)


def call(kernel, arrays, outs, flops=1024, tokens=(), scratch=()):
    skip = len(tokens)

    def body(*refs):
        kernel(*refs[: len(arrays)], *refs[len(arrays) + skip :])

    return pl.pallas_call(
        body,
        in_specs=[NEAR] * len(arrays) + [ANYWHERE] * skip,
        out_specs=[NEAR] * len(outs),
        out_shape=[pltpu.VMEM(shape, dtype) for shape, dtype in outs],
        scratch_shapes=list(scratch),
        compiler_params=pltpu.CompilerParams(vmem_limit_bytes=12 * 1024 * 1024),
        cost_estimate=pl.CostEstimate(flops=flops, bytes_accessed=1024, transcendentals=0),
    )(*[pltpu.with_memory_space_constraint(array, pltpu.VMEM) for array in arrays], *tokens)


def fetch(kernel, arrays, outs, scratch, copies):
    return pl.pallas_call(
        kernel,
        in_specs=[ANYWHERE] * len(arrays),
        out_specs=[NEAR] * len(outs),
        out_shape=[pltpu.VMEM(shape, dtype) for shape, dtype in outs],
        scratch_shapes=[*scratch, pltpu.SemaphoreType.DMA((copies,))],
        compiler_params=pltpu.CompilerParams(vmem_limit_bytes=12 * 1024 * 1024),
        cost_estimate=pl.CostEstimate(flops=1024, bytes_accessed=1024, transcendentals=0),
    )(*[pltpu.with_memory_space_constraint(array, pltpu.HBM) for array in arrays])


def grads_block(grads_ref, device, part, rows):
    first = pl.multiple_of(lax.axis_index("din") * part, part)
    return grads_ref.at[pl.ds(first, part), pl.ds(pl.multiple_of(device * rows, rows), rows)]


def first_kernel(far, acts_ref, grads_ref, mine_ref, far_ref, arrived):
    half = mine_ref.shape[0]
    rows = pl.ds(pl.multiple_of(lax.axis_index("dout") * half, half), half)
    block = grads_block(grads_ref, lax.axis_index("dp") ^ far, *far_ref.shape)
    copies = [
        pltpu.make_async_copy(acts_ref.at[rows, :], mine_ref, arrived.at[0]),
        pltpu.make_async_copy(block, far_ref, arrived.at[1]),
    ]
    for copy in copies:
        copy.start()
    for copy in copies:
        copy.wait()


def rest_kernel(steps, acts_ref, grads_ref, query_ref, near_query, near_acts, own_out, *refs):
    outs, own, blocks, arrived = list(refs[:-3]), refs[-3], refs[-2], refs[-1]
    me = lax.axis_index("dp")
    tokens, rows = own.shape
    copies = [pltpu.make_async_copy(grads_ref.at[:, pl.ds(pl.multiple_of(me * rows, rows), rows)], own, arrived.at[0])]
    for k, d in enumerate(steps):
        block = grads_block(grads_ref, me ^ d, *blocks.shape[1:])
        copies.append(pltpu.make_async_copy(block, blocks.at[k], arrived.at[1 + k]))
    copies.append(pltpu.make_async_copy(acts_ref, near_acts, arrived.at[len(steps) + 1]))
    copies.append(pltpu.make_async_copy(query_ref, near_query, arrived.at[len(steps) + 2]))
    for copy in copies:
        copy.start()
    for k in range(len(steps)):
        copies[1 + k].wait()
        turned, at = blocks[k].astype(jnp.float32).T.astype(blocks.dtype), 0
        while at < rows:
            out = outs.pop(0)
            out[...] = turned[at : at + out.shape[0]]
            at += out.shape[0]
    copies[0].wait()
    own_out[...] = own[...].astype(jnp.float32).T.astype(own_out.dtype)
    for copy in copies[-2:]:
        copy.wait()


def hold(blocks, tokens, flops=1024):
    count = len(blocks)
    return pl.pallas_call(
        lambda *refs: None,
        in_specs=[ANYWHERE] * (count + len(tokens)),
        out_specs=[ANYWHERE] * count,
        out_shape=[jax.ShapeDtypeStruct(block.shape, block.dtype) for block in blocks],
        input_output_aliases={i: i for i in range(count)},
        compiler_params=pltpu.CompilerParams(vmem_limit_bytes=1024 * 1024),
        cost_estimate=pl.CostEstimate(flops=flops, bytes_accessed=1024, transcendentals=0),
    )(*blocks, *tokens)


def pick_kernel(choice, *refs):
    *blocks, out_ref = refs
    me = lax.axis_index("dp")
    where = functools.reduce(lambda found, z: jnp.where(me == z, choice[z], found), range(len(choice)), 0)
    for k, block in enumerate(blocks):

        @pl.when(where == k)
        def _():
            out_ref[...] = block[...]


def from_partner(hops, d, count, tokens=()):
    sources, choice = [], []
    for z in range(count):
        away = z - (z ^ d)
        source = (abs(away), int(away < 0 and abs(away) < count - 1))
        if source not in sources:
            sources.append(source)
        choice.append(sources.index(source))
    blocks = [hops[step][way] for step, way in sources]
    outs = [(blocks[0].shape, blocks[0].dtype)]
    return call(functools.partial(pick_kernel, choice), blocks, outs, tokens=tokens)[0]


def joined(parts, axis):
    parts = [part[...] for part in parts]
    if len(parts) == 1:
        return parts[0]
    column, found = lax.axis_index("din"), []
    for p in range(len(parts)):
        chosen = parts[0]
        for r in range(1, len(parts)):
            chosen = jnp.where(column == p ^ r, parts[r], chosen)
        found.append(chosen)
    return jnp.concatenate(found, axis=axis)


MARK = (8, 128), jnp.float32


def mix_kernel(*refs):
    *parts, query_ref, out_ref, mark_ref, acts = refs
    mark_ref[...] = jnp.zeros_like(mark_ref)
    half = parts[0].shape[0]
    first = lax.axis_index("dout") * half if len(parts) > 1 else 0
    for part, at in zip(parts, (first, half - first)):
        acts[pl.ds(pl.multiple_of(at, half), half), :] = part[...]
    nq, _, depth, _ = query_ref.shape
    tile = depth // 2

    def step(at, _):
        q, rows = at // 2, pl.ds(pl.multiple_of(at % 2 * tile, tile), tile)
        out_ref[q, rows, :] = lax.dot_general(
            query_ref[q, 0, rows, :], acts[...], (((1,), (1,)), ((), ())), preferred_element_type=jnp.float32
        )
        return 0

    lax.fori_loop(0, 2 * nq, step, 0)


def mixed(parts, queries, flops, tokens=()):
    nq, _, depth, width = queries.shape
    tokens_here = sum(part.shape[0] for part in parts)
    outs = [((nq, depth, tokens_here), jnp.float32), MARK]
    scratch = [pltpu.VMEM((tokens_here, width), queries.dtype)]
    return call(mix_kernel, [*parts, queries], outs, flops, tokens, scratch)


def score_kernel(pieces, *refs):
    *parts, mix_ref, out_ref = refs
    size = mix_ref.shape[1] // pieces
    for p in range(pieces):
        grads = joined(parts[p::pieces], 1).astype(jnp.float32)
        for q in range(mix_ref.shape[0]):
            term = jnp.sum(grads * mix_ref[q, p * size : (p + 1) * size], axis=0, keepdims=True)
            out_ref[q : q + 1, :] = term if p == 0 else out_ref[q : q + 1, :] + term


def scores_of_grads(parts, mix, tokens=(), flops=1024):
    nq, _, count = mix.shape
    parts = [part if isinstance(part, list) else [part] for part in parts]
    kernel = functools.partial(score_kernel, len(parts[0]))
    return call(kernel, [*sum(parts, []), mix], [((nq, count), jnp.float32)], flops, tokens)[0]


def project_kernel(*refs):
    *parts, query_ref, out_ref, mark_ref, grads = refs
    mark_ref[...] = jnp.zeros_like(mark_ref)
    grads[...] = joined(parts, 0)
    nq, _, _, width = query_ref.shape
    tile = width // 2

    def step(at, _):
        q, columns = at // 2, pl.ds(pl.multiple_of(at % 2 * tile, tile), tile)
        out_ref[q, :, columns] = jnp.dot(
            grads[...], query_ref[q, 0, :, columns], preferred_element_type=jnp.float32
        )
        return 0

    lax.fori_loop(0, 2 * nq, step, 0)


def projected(parts, queries, flops, tokens=()):
    nq, _, depth, width = queries.shape
    count = sum(part.shape[0] for part in parts)
    outs = [((nq, count, width), jnp.float32), MARK]
    scratch = [pltpu.VMEM((count, depth), queries.dtype)]
    return call(project_kernel, [*parts, queries], outs, flops, tokens, scratch)


def finish_kernel(mine_ref, other_ref, proj_ref, out_ref):
    half, width = mine_ref.shape
    swapped = lax.axis_index("dout") == 1
    for h, (first, second) in enumerate(((mine_ref, other_ref), (other_ref, mine_ref))):
        acts = jnp.where(swapped, second[...], first[...]).astype(jnp.float32)
        for q in range(proj_ref.shape[0]):
            terms = acts * proj_ref[q, h * half : (h + 1) * half, :]
            lanes = terms[:, :128]
            for at in range(128, width, 128):
                lanes = lanes + terms[:, at : at + 128]
            out_ref[q : q + 1, h * half : (h + 1) * half] = jnp.sum(lanes.T, axis=0, keepdims=True)


def scores_of_acts(mine, other, proj, tokens=()):
    nq, count, _ = proj.shape
    return call(finish_kernel, [mine, other, proj], [((nq, count), jnp.float32)], tokens=tokens)[0]


def cut(activations, out_grads, queries, far, others, pieces):
    count, part = lax.axis_size("dp"), out_grads.shape[0] // lax.axis_size("din")
    rows, (tokens, width), dtype = queries.shape[2], activations.shape, out_grads.dtype
    half = tokens // 2
    if part % 128 or rows % 128:
        me, column = lax.axis_index("dp"), lax.axis_index("din")
        mine = lax.dynamic_slice_in_dim(activations, lax.axis_index("dout") * half, half, 0)
        share = lax.dynamic_slice_in_dim(out_grads, column * part, part, 0)
        away = [lax.dynamic_slice_in_dim(share, (me ^ d) * rows, rows, 1) for d in [far, *others]]
        own = lax.dynamic_slice_in_dim(out_grads, me * rows, rows, 1).T
        turned = [block.T for block in away[1:]]
        return (mine, away[0]), (queries, activations, own, *turned[:-1], *jnp.split(turned[-1], pieces))
    outs = [((half, width), activations.dtype), ((part, rows), dtype)]
    first = fetch(functools.partial(first_kernel, far), [activations, out_grads], outs, [], 2)
    outs = [(queries.shape, queries.dtype), (activations.shape, activations.dtype), ((rows, tokens), dtype)]
    outs += [((rows, part), dtype)] * (len(others) - 1) + [((rows // pieces, part), dtype)] * pieces
    scratch = [pltpu.VMEM((tokens, rows), dtype), pltpu.VMEM((len(others), part, rows), dtype)]
    arrays = [activations, out_grads, queries]
    return first, fetch(functools.partial(rest_kernel, others), arrays, outs, scratch, len(others) + 3)


def on_device(activations, out_grads, queries):
    count, spread = lax.axis_size("dp"), lax.axis_size("din")

    def to_columns(arrived):
        return [arrived] + [trade(arrived, {"din": r}) for r in range(1, spread)]

    def acts_of(block):
        return [block, trade(block, {"dout": 1})]

    far, late = count - 1, count - 2
    early = list(range(1, late))
    pieces = 2
    (mine, far_grads), (queries, own_acts, own, *sent) = cut(
        activations, out_grads, queries, far, early + [late], pieces
    )
    hops = [(mine, mine)]
    hops.append(pass_on(hops[0], 1, count))
    arrived = {d: trade(block, {"dp": d}) for d, block in zip([far, *early], [far_grads, *sent])}

    mix, token = mixed([own_acts], queries, SHORT)
    scores = scores_of_grads([own], mix)
    hops[1] = hold(list(hops[1]), [token])
    for step in range(2, count - 1):
        hops.append(pass_on(hops[-1], step, count))

    mixes, token = {}, scores
    for d in early:
        mixes[d], token = mixed(acts_of(from_partner(hops, d, count)), queries, SHORT, [token])
    tail = [trade(hold([block], [token])[0], {"dp": late}) for block in sent[len(early) :]]
    sides = to_columns(hold([arrived[far]], [*hops[1], *[arrived[d] for d in early]])[0])
    block = from_partner(hops, late, count, [token] + sides)
    end = lax.ppermute(block, "dp", [(1, 0), (count - 2, count - 1)])
    hops.append((end, end))

    proj, token = projected(sides, queries, SHORT, [token])
    terms = []
    for d in early:
        sides = to_columns(hold([arrived[d]], hops[1])[0])
        token = scores_of_grads(sides, mixes[d], [token])
        terms.append(trade(token, {"dp": d}))

    mix, done = mixed(acts_of(block), queries, SHORT, [token])
    tail = [to_columns(hold([piece], [done if p else token], LONG)[0]) for p, piece in enumerate(tail)]
    block = from_partner(hops, far, count, [done])
    terms.append(trade(scores_of_acts(*acts_of(block), proj), {"dp": far}))
    terms.append(trade(scores_of_grads([list(sides) for sides in zip(*tail)], mix, (), LONG), {"dp": late}))
    return over_chips(sum(terms, scores), spread)


def over_chips(scores, spread):
    scores = scores + trade(scores, {"dout": 1})
    return scores + sum(trade(scores, {"din": r}) for r in range(1, spread))


def solution(mesh):
    placed = (P(("groups", "dp"), "din"), P(("groups", "dp"), "dout"), P(None, "dout", "dp", "din"))
    return jax.shard_map(
        on_device, mesh=mesh, in_specs=placed, out_specs=P(None, ("groups", "dp")), check_vma=False
    )
```

```python
import functools
import math

import jax
import jax.numpy as jnp
from jax import lax
from jax.experimental import pallas as pl
from jax.experimental.pallas import tpu as pltpu
from jax.sharding import PartitionSpec as P


LONG, MIDDLE, SHORT = 14_000_000_000, 14_000_000_000, 1_000_000


def trade(block, steps, backwards=False):
    axes = tuple(steps)
    sizes = [lax.axis_size(axis) for axis in axes]
    mask = 0
    for axis, size in zip(axes, sizes):
        mask = mask * size + steps[axis]
    route = [(i, i ^ mask) for i in range(math.prod(sizes))]
    return lax.ppermute(block, axes, route[::-1] if backwards else route)


def pass_on(block, step, count):
    up = lax.ppermute(block[0], "dp", [(i, i + 1) for i in range(step - 1, count - 1)])
    down = lax.ppermute(block[1], "dp", [(i, i - 1) for i in range(1, count - step + 1)])
    return up, down


ANYWHERE = pl.BlockSpec(memory_space=pl.ANY)
NEAR = pl.BlockSpec(memory_space=pltpu.VMEM)


def call(kernel, arrays, outs, flops=1024, tokens=(), scratch=()):
    skip = len(tokens)

    def body(*refs):
        kernel(*refs[: len(arrays)], *refs[len(arrays) + skip :])

    return pl.pallas_call(
        body,
        in_specs=[NEAR] * len(arrays) + [ANYWHERE] * skip,
        out_specs=[NEAR] * len(outs),
        out_shape=[pltpu.VMEM(shape, dtype) for shape, dtype in outs],
        scratch_shapes=list(scratch),
        compiler_params=pltpu.CompilerParams(vmem_limit_bytes=12 * 1024 * 1024),
        cost_estimate=pl.CostEstimate(flops=flops, bytes_accessed=1024, transcendentals=0),
    )(*[pltpu.with_memory_space_constraint(array, pltpu.VMEM) for array in arrays], *tokens)


def fetch(kernel, arrays, outs, scratch, copies):
    return pl.pallas_call(
        kernel,
        in_specs=[ANYWHERE] * len(arrays),
        out_specs=[NEAR] * len(outs),
        out_shape=[pltpu.VMEM(shape, dtype) for shape, dtype in outs],
        scratch_shapes=[*scratch, pltpu.SemaphoreType.DMA((copies,))],
        compiler_params=pltpu.CompilerParams(vmem_limit_bytes=12 * 1024 * 1024),
        cost_estimate=pl.CostEstimate(flops=1024, bytes_accessed=1024, transcendentals=0),
    )(*[pltpu.with_memory_space_constraint(array, pltpu.HBM) for array in arrays])


def grads_block(grads_ref, device, part, rows):
    first = pl.multiple_of(lax.axis_index("din") * part, part)
    return grads_ref.at[pl.ds(first, part), pl.ds(pl.multiple_of(device * rows, rows), rows)]


def first_kernel(acts_ref, mine_ref, arrived):
    half = mine_ref.shape[0]
    rows = pl.ds(pl.multiple_of(lax.axis_index("dout") * half, half), half)
    copy = pltpu.make_async_copy(acts_ref.at[rows, :], mine_ref, arrived.at[0])
    copy.start()
    copy.wait()


def rest_kernel(far, steps, acts_ref, grads_ref, query_ref, near_query, near_acts, far_out, own_out, *refs):
    outs, own, blocks, arrived = list(refs[:-3]), refs[-3], refs[-2], refs[-1]
    me = lax.axis_index("dp")
    tokens, rows = own.shape
    copies = [pltpu.make_async_copy(grads_ref.at[:, pl.ds(pl.multiple_of(me * rows, rows), rows)], own, arrived.at[0])]
    for k, d in enumerate(steps):
        block = grads_block(grads_ref, me ^ d, *blocks.shape[1:])
        copies.append(pltpu.make_async_copy(block, blocks.at[k], arrived.at[1 + k]))
    block = grads_block(grads_ref, me ^ far, *far_out.shape)
    copies.append(pltpu.make_async_copy(block, far_out, arrived.at[len(steps) + 1]))
    copies.append(pltpu.make_async_copy(acts_ref, near_acts, arrived.at[len(steps) + 2]))
    copies.append(pltpu.make_async_copy(query_ref, near_query, arrived.at[len(steps) + 3]))
    for copy in copies:
        copy.start()
    for k in range(len(steps)):
        copies[1 + k].wait()
        turned, at = blocks[k].astype(jnp.float32).T.astype(blocks.dtype), 0
        while at < rows:
            out = outs.pop(0)
            out[...] = turned[at : at + out.shape[0]]
            at += out.shape[0]
    copies[0].wait()
    own_out[...] = own[...].astype(jnp.float32).T.astype(own_out.dtype)
    for copy in copies[-3:]:
        copy.wait()


def hold(blocks, tokens, flops=1024):
    count = len(blocks)
    return pl.pallas_call(
        lambda *refs: None,
        in_specs=[ANYWHERE] * (count + len(tokens)),
        out_specs=[ANYWHERE] * count,
        out_shape=[jax.ShapeDtypeStruct(block.shape, block.dtype) for block in blocks],
        input_output_aliases={i: i for i in range(count)},
        compiler_params=pltpu.CompilerParams(vmem_limit_bytes=1024 * 1024),
        cost_estimate=pl.CostEstimate(flops=flops, bytes_accessed=1024, transcendentals=0),
    )(*blocks, *tokens)


def pick_kernel(choice, *refs):
    *blocks, out_ref = refs
    me = lax.axis_index("dp")
    where = functools.reduce(lambda found, z: jnp.where(me == z, choice[z], found), range(len(choice)), 0)
    for k, block in enumerate(blocks):

        @pl.when(where == k)
        def _():
            out_ref[...] = block[...]


def from_partner(hops, d, count, tokens=(), flops=1024):
    sources, choice = [], []
    for z in range(count):
        away = z - (z ^ d)
        source = (abs(away), int(away < 0 and abs(away) < count - 1))
        if source not in sources:
            sources.append(source)
        choice.append(sources.index(source))
    blocks = [hops[step][way] for step, way in sources]
    outs = [(blocks[0].shape, blocks[0].dtype)]
    return call(functools.partial(pick_kernel, choice), blocks, outs, flops, tokens)[0]


def joined(parts, axis):
    parts = [part[...] for part in parts]
    if len(parts) == 1:
        return parts[0]
    column, found = lax.axis_index("din"), []
    for p in range(len(parts)):
        chosen = parts[0]
        for r in range(1, len(parts)):
            chosen = jnp.where(column == p ^ r, parts[r], chosen)
        found.append(chosen)
    return jnp.concatenate(found, axis=axis)


MARK = (8, 128), jnp.float32


def mix_kernel(*refs):
    *parts, query_ref, out_ref, mark_ref, acts = refs
    mark_ref[...] = jnp.zeros_like(mark_ref)
    half = parts[0].shape[0]
    first = lax.axis_index("dout") * half if len(parts) > 1 else 0
    for part, at in zip(parts, (first, half - first)):
        acts[pl.ds(pl.multiple_of(at, half), half), :] = part[...]
    nq, _, depth, _ = query_ref.shape
    tile = depth // 2

    def step(at, _):
        q, rows = at // 2, pl.ds(pl.multiple_of(at % 2 * tile, tile), tile)
        out_ref[q, rows, :] = lax.dot_general(
            query_ref[q, 0, rows, :], acts[...], (((1,), (1,)), ((), ())), preferred_element_type=jnp.float32
        )
        return 0

    lax.fori_loop(0, 2 * nq, step, 0)


def mixed(parts, queries, flops, tokens=()):
    nq, _, depth, width = queries.shape
    tokens_here = sum(part.shape[0] for part in parts)
    outs = [((nq, depth, tokens_here), jnp.float32), MARK]
    scratch = [pltpu.VMEM((tokens_here, width), queries.dtype)]
    return call(mix_kernel, [*parts, queries], outs, flops, tokens, scratch)


def score_kernel(pieces, *refs):
    *parts, mix_ref, out_ref = refs
    size = mix_ref.shape[1] // pieces
    for p in range(pieces):
        grads = joined(parts[p::pieces], 1).astype(jnp.float32)
        for q in range(mix_ref.shape[0]):
            term = jnp.sum(grads * mix_ref[q, p * size : (p + 1) * size], axis=0, keepdims=True)
            out_ref[q : q + 1, :] = term if p == 0 else out_ref[q : q + 1, :] + term


def scores_of_grads(parts, mix, tokens=(), flops=1024):
    nq, _, count = mix.shape
    parts = [part if isinstance(part, list) else [part] for part in parts]
    kernel = functools.partial(score_kernel, len(parts[0]))
    return call(kernel, [*sum(parts, []), mix], [((nq, count), jnp.float32)], flops, tokens)[0]


def project_kernel(*refs):
    *parts, query_ref, out_ref, mark_ref, grads = refs
    mark_ref[...] = jnp.zeros_like(mark_ref)
    grads[...] = joined(parts, 0)
    nq, _, _, width = query_ref.shape
    tile = width // 2

    def step(at, _):
        q, columns = at // 2, pl.ds(pl.multiple_of(at % 2 * tile, tile), tile)
        out_ref[q, :, columns] = jnp.dot(
            grads[...], query_ref[q, 0, :, columns], preferred_element_type=jnp.float32
        )
        return 0

    lax.fori_loop(0, 2 * nq, step, 0)


def projected(parts, queries, flops, tokens=()):
    nq, _, depth, width = queries.shape
    count = sum(part.shape[0] for part in parts)
    outs = [((nq, count, width), jnp.float32), MARK]
    scratch = [pltpu.VMEM((count, depth), queries.dtype)]
    return call(project_kernel, [*parts, queries], outs, flops, tokens, scratch)


def finish_kernel(mine_ref, other_ref, proj_ref, out_ref):
    half, width = mine_ref.shape
    swapped = lax.axis_index("dout") == 1
    for h, (first, second) in enumerate(((mine_ref, other_ref), (other_ref, mine_ref))):
        acts = jnp.where(swapped, second[...], first[...]).astype(jnp.float32)
        for q in range(proj_ref.shape[0]):
            terms = acts * proj_ref[q, h * half : (h + 1) * half, :]
            lanes = terms[:, :128]
            for at in range(128, width, 128):
                lanes = lanes + terms[:, at : at + 128]
            out_ref[q : q + 1, h * half : (h + 1) * half] = jnp.sum(lanes.T, axis=0, keepdims=True)


def scores_of_acts(mine, other, proj, tokens=()):
    nq, count, _ = proj.shape
    return call(finish_kernel, [mine, other, proj], [((nq, count), jnp.float32)], tokens=tokens)[0]


def cut(activations, out_grads, queries, far, others, pieces):
    count, part = lax.axis_size("dp"), out_grads.shape[0] // lax.axis_size("din")
    rows, (tokens, width), dtype = queries.shape[2], activations.shape, out_grads.dtype
    half = tokens // 2
    if part % 128 or rows % 128:
        me, column = lax.axis_index("dp"), lax.axis_index("din")
        mine = lax.dynamic_slice_in_dim(activations, lax.axis_index("dout") * half, half, 0)
        share = lax.dynamic_slice_in_dim(out_grads, column * part, part, 0)
        away = [lax.dynamic_slice_in_dim(share, (me ^ d) * rows, rows, 1) for d in [far, *others]]
        own = lax.dynamic_slice_in_dim(out_grads, me * rows, rows, 1).T
        turned = [block.T for block in away[1:]]
        return mine, (queries, activations, away[0], own, *turned[:-1], *jnp.split(turned[-1], pieces))
    first, = fetch(first_kernel, [activations], [((half, width), activations.dtype)], [], 1)
    outs = [(queries.shape, queries.dtype), (activations.shape, activations.dtype)]
    outs += [((part, rows), dtype), ((rows, tokens), dtype)]
    outs += [((rows, part), dtype)] * (len(others) - 1) + [((rows // pieces, part), dtype)] * pieces
    scratch = [pltpu.VMEM((tokens, rows), dtype), pltpu.VMEM((len(others), part, rows), dtype)]
    arrays = [activations, out_grads, queries]
    return first, fetch(functools.partial(rest_kernel, far, others), arrays, outs, scratch, len(others) + 4)


def on_device(activations, out_grads, queries):
    count, spread = lax.axis_size("dp"), lax.axis_size("din")

    def to_columns(arrived):
        return [arrived] + [trade(arrived, {"din": r}) for r in range(1, spread)]

    def acts_of(block):
        return [block, trade(block, {"dout": 1})]

    far, late = count - 1, count - 2
    early = list(range(1, late))
    pieces = 2
    mine, (queries, own_acts, far_grads, own, *sent) = cut(
        activations, out_grads, queries, far, early + [late], pieces
    )
    hops = [(mine, mine)]
    hops.append(pass_on(hops[0], 1, count))
    arrived = {d: trade(block, {"dp": d}) for d, block in zip(early, sent)}

    mix, token = mixed([own_acts], queries, SHORT)
    scores = scores_of_grads([own], mix)
    hops[1] = hold(list(hops[1]), [token])
    for step in range(2, count - 1):
        hops.append(pass_on(hops[-1], step, count))
    arrived[far] = trade(hold([far_grads], hops[1])[0], {"dp": far})

    mixes, token = {}, scores
    for d in early:
        mixes[d], token = mixed(acts_of(from_partner(hops, d, count)), queries, SHORT, [token])
    near = {d: to_columns(hold([arrived[d]], hops[1], LONG)[0]) for d in early}
    block = from_partner(hops, late, count, [token], MIDDLE)
    end = lax.ppermute(block, "dp", [(1, 0), (count - 2, count - 1)])
    hops.append((end, end))
    tail = [trade(hold([piece], [block])[0], {"dp": late}) for piece in sent[len(early) :]]
    sides = to_columns(hold([arrived[far]], [block])[0])

    terms = []
    for d in early:
        token = scores_of_grads(near[d], mixes[d], [token], LONG)
        terms.append(trade(token, {"dp": d}))
    mix, done = mixed(acts_of(block), queries, SHORT, [token])
    proj, token = projected(sides, queries, SHORT, [done])
    tail[0], = hold(tail[:1], [done], LONG)
    tail = [to_columns(hold([piece], [token if p else done], LONG)[0]) for p, piece in enumerate(tail)]
    block = from_partner(hops, far, count, [done], LONG)
    block, = hold([block], [], LONG)
    terms.append(trade(scores_of_acts(*acts_of(block), proj), {"dp": far}))
    terms.append(trade(scores_of_grads([list(sides) for sides in zip(*tail)], mix, (), LONG), {"dp": late}))
    return over_chips(sum(terms, scores), spread)


def over_chips(scores, spread):
    scores = scores + trade(scores, {"dout": 1})
    return scores + sum(trade(scores, {"din": r}) for r in range(1, spread))


def solution(mesh):
    placed = (P(("groups", "dp"), "din"), P(("groups", "dp"), "dout"), P(None, "dout", "dp", "din"))
    return jax.shard_map(
        on_device, mesh=mesh, in_specs=placed, out_specs=P(None, ("groups", "dp")), check_vma=False
    )
```

```python
import functools
import math

import jax
import jax.numpy as jnp
from jax import lax
from jax.experimental import pallas as pl
from jax.experimental.pallas import tpu as pltpu
from jax.sharding import PartitionSpec as P


LONG, SHORT = 14_000_000_000, 1_000_000


def trade(block, steps, backwards=False):
    axes = tuple(steps)
    sizes = [lax.axis_size(axis) for axis in axes]
    mask = 0
    for axis, size in zip(axes, sizes):
        mask = mask * size + steps[axis]
    route = [(i, i ^ mask) for i in range(math.prod(sizes))]
    return lax.ppermute(block, axes, route[::-1] if backwards else route)


def pass_on(block, step, count):
    up = lax.ppermute(block[0], "dp", [(i, i + 1) for i in range(step - 1, count - 1)])
    down = lax.ppermute(block[1], "dp", [(i, i - 1) for i in range(1, count - step + 1)])
    return up, down


ANYWHERE = pl.BlockSpec(memory_space=pl.ANY)
NEAR = pl.BlockSpec(memory_space=pltpu.VMEM)


def call(kernel, arrays, outs, flops=1024, tokens=(), scratch=()):
    skip = len(tokens)

    def body(*refs):
        kernel(*refs[: len(arrays)], *refs[len(arrays) + skip :])

    return pl.pallas_call(
        body,
        in_specs=[NEAR] * len(arrays) + [ANYWHERE] * skip,
        out_specs=[NEAR] * len(outs),
        out_shape=[pltpu.VMEM(shape, dtype) for shape, dtype in outs],
        scratch_shapes=list(scratch),
        compiler_params=pltpu.CompilerParams(vmem_limit_bytes=12 * 1024 * 1024),
        cost_estimate=pl.CostEstimate(flops=flops, bytes_accessed=1024, transcendentals=0),
    )(*[pltpu.with_memory_space_constraint(array, pltpu.VMEM) for array in arrays], *tokens)


def fetch(kernel, arrays, outs, scratch, copies):
    return pl.pallas_call(
        kernel,
        in_specs=[ANYWHERE] * len(arrays),
        out_specs=[NEAR] * len(outs),
        out_shape=[pltpu.VMEM(shape, dtype) for shape, dtype in outs],
        scratch_shapes=[*scratch, pltpu.SemaphoreType.DMA((copies,))],
        compiler_params=pltpu.CompilerParams(vmem_limit_bytes=12 * 1024 * 1024),
        cost_estimate=pl.CostEstimate(flops=1024, bytes_accessed=1024, transcendentals=0),
    )(*[pltpu.with_memory_space_constraint(array, pltpu.HBM) for array in arrays])


def grads_block(grads_ref, device, part, rows):
    first = pl.multiple_of(lax.axis_index("din") * part, part)
    return grads_ref.at[pl.ds(first, part), pl.ds(pl.multiple_of(device * rows, rows), rows)]


def first_kernel(far, acts_ref, grads_ref, mine_ref, far_ref, arrived):
    half = mine_ref.shape[0]
    rows = pl.ds(pl.multiple_of(lax.axis_index("dout") * half, half), half)
    block = grads_block(grads_ref, lax.axis_index("dp") ^ far, *far_ref.shape)
    copies = [
        pltpu.make_async_copy(acts_ref.at[rows, :], mine_ref, arrived.at[0]),
        pltpu.make_async_copy(block, far_ref, arrived.at[1]),
    ]
    for copy in copies:
        copy.start()
    for copy in copies:
        copy.wait()


def rest_kernel(steps, acts_ref, grads_ref, query_ref, near_query, near_acts, own_out, *refs):
    outs, own, blocks, arrived = list(refs[:-3]), refs[-3], refs[-2], refs[-1]
    me = lax.axis_index("dp")
    tokens, rows = own.shape
    copies = [pltpu.make_async_copy(grads_ref.at[:, pl.ds(pl.multiple_of(me * rows, rows), rows)], own, arrived.at[0])]
    for k, d in enumerate(steps):
        block = grads_block(grads_ref, me ^ d, *blocks.shape[1:])
        copies.append(pltpu.make_async_copy(block, blocks.at[k], arrived.at[1 + k]))
    copies.append(pltpu.make_async_copy(acts_ref, near_acts, arrived.at[len(steps) + 1]))
    copies.append(pltpu.make_async_copy(query_ref, near_query, arrived.at[len(steps) + 2]))
    for copy in copies:
        copy.start()
    for k in range(len(steps)):
        copies[1 + k].wait()
        turned, at = blocks[k].astype(jnp.float32).T.astype(blocks.dtype), 0
        while at < rows:
            out = outs.pop(0)
            out[...] = turned[at : at + out.shape[0]]
            at += out.shape[0]
    copies[0].wait()
    own_out[...] = own[...].astype(jnp.float32).T.astype(own_out.dtype)
    for copy in copies[-2:]:
        copy.wait()


def hold(blocks, tokens, flops=1024):
    count = len(blocks)
    return pl.pallas_call(
        lambda *refs: None,
        in_specs=[ANYWHERE] * (count + len(tokens)),
        out_specs=[ANYWHERE] * count,
        out_shape=[jax.ShapeDtypeStruct(block.shape, block.dtype) for block in blocks],
        input_output_aliases={i: i for i in range(count)},
        compiler_params=pltpu.CompilerParams(vmem_limit_bytes=1024 * 1024),
        cost_estimate=pl.CostEstimate(flops=flops, bytes_accessed=1024, transcendentals=0),
    )(*blocks, *tokens)


def pick_kernel(choice, *refs):
    *blocks, out_ref = refs
    me = lax.axis_index("dp")
    where = functools.reduce(lambda found, z: jnp.where(me == z, choice[z], found), range(len(choice)), 0)
    for k, block in enumerate(blocks):

        @pl.when(where == k)
        def _():
            out_ref[...] = block[...]


def from_partner(hops, d, count, tokens=()):
    sources, choice = [], []
    for z in range(count):
        away = z - (z ^ d)
        source = (abs(away), int(away < 0 and abs(away) < count - 1))
        if source not in sources:
            sources.append(source)
        choice.append(sources.index(source))
    blocks = [hops[step][way] for step, way in sources]
    outs = [(blocks[0].shape, blocks[0].dtype)]
    return call(functools.partial(pick_kernel, choice), blocks, outs, tokens=tokens)[0]


def joined(parts, axis):
    parts = [part[...] for part in parts]
    if len(parts) == 1:
        return parts[0]
    column, found = lax.axis_index("din"), []
    for p in range(len(parts)):
        chosen = parts[0]
        for r in range(1, len(parts)):
            chosen = jnp.where(column == p ^ r, parts[r], chosen)
        found.append(chosen)
    return jnp.concatenate(found, axis=axis)


MARK = (8, 128), jnp.float32


def mix_kernel(*refs):
    *parts, query_ref, out_ref, mark_ref, acts = refs
    mark_ref[...] = jnp.zeros_like(mark_ref)
    half = parts[0].shape[0]
    first = lax.axis_index("dout") * half if len(parts) > 1 else 0
    for part, at in zip(parts, (first, half - first)):
        acts[pl.ds(pl.multiple_of(at, half), half), :] = part[...]
    nq, _, depth, _ = query_ref.shape
    tile = depth // 2

    def step(at, _):
        q, rows = at // 2, pl.ds(pl.multiple_of(at % 2 * tile, tile), tile)
        out_ref[q, rows, :] = lax.dot_general(
            query_ref[q, 0, rows, :], acts[...], (((1,), (1,)), ((), ())), preferred_element_type=jnp.float32
        )
        return 0

    lax.fori_loop(0, 2 * nq, step, 0)


def mixed(parts, queries, flops, tokens=()):
    nq, _, depth, width = queries.shape
    tokens_here = sum(part.shape[0] for part in parts)
    outs = [((nq, depth, tokens_here), jnp.float32), MARK]
    scratch = [pltpu.VMEM((tokens_here, width), queries.dtype)]
    return call(mix_kernel, [*parts, queries], outs, flops, tokens, scratch)


def score_kernel(first, number, *refs):
    parts, (mix_ref, *before, out_ref) = refs[:number], refs[number:]
    grads = joined(parts, 1).astype(jnp.float32)
    for q in range(mix_ref.shape[0]):
        mix = mix_ref[q, first : first + grads.shape[0]]
        term = jnp.sum(grads * mix, axis=0, keepdims=True)
        out_ref[q : q + 1, :] = before[0][q : q + 1, :] + term if before else term


def scores_of_grads(parts, mix, tokens=(), flops=1024, first=0, before=()):
    nq, _, count = mix.shape
    kernel = functools.partial(score_kernel, first, len(parts))
    return call(kernel, [*parts, mix, *before], [((nq, count), jnp.float32)], flops, tokens)[0]


def project_kernel(*refs):
    *parts, query_ref, out_ref, mark_ref, grads = refs
    mark_ref[...] = jnp.zeros_like(mark_ref)
    grads[...] = joined(parts, 0)
    nq, _, _, width = query_ref.shape
    tile = width // 2

    def step(at, _):
        q, columns = at // 2, pl.ds(pl.multiple_of(at % 2 * tile, tile), tile)
        out_ref[q, :, columns] = jnp.dot(
            grads[...], query_ref[q, 0, :, columns], preferred_element_type=jnp.float32
        )
        return 0

    lax.fori_loop(0, 2 * nq, step, 0)


def projected(parts, queries, flops, tokens=()):
    nq, _, depth, width = queries.shape
    count = sum(part.shape[0] for part in parts)
    outs = [((nq, count, width), jnp.float32), MARK]
    scratch = [pltpu.VMEM((count, depth), queries.dtype)]
    return call(project_kernel, [*parts, queries], outs, flops, tokens, scratch)


def finish_kernel(mine_ref, other_ref, proj_ref, out_ref):
    half, width = mine_ref.shape
    swapped = lax.axis_index("dout") == 1
    for h, (first, second) in enumerate(((mine_ref, other_ref), (other_ref, mine_ref))):
        acts = jnp.where(swapped, second[...], first[...]).astype(jnp.float32)
        for q in range(proj_ref.shape[0]):
            terms = acts * proj_ref[q, h * half : (h + 1) * half, :]
            lanes = terms[:, :128]
            for at in range(128, width, 128):
                lanes = lanes + terms[:, at : at + 128]
            out_ref[q : q + 1, h * half : (h + 1) * half] = jnp.sum(lanes.T, axis=0, keepdims=True)


def scores_of_acts(mine, other, proj, tokens=()):
    nq, count, _ = proj.shape
    return call(finish_kernel, [mine, other, proj], [((nq, count), jnp.float32)], tokens=tokens)[0]


def cut(activations, out_grads, queries, far, others, sizes):
    count, part = lax.axis_size("dp"), out_grads.shape[0] // lax.axis_size("din")
    rows, (tokens, width), dtype = queries.shape[2], activations.shape, out_grads.dtype
    half = tokens // 2
    if part % 128 or rows % 128:
        me, column = lax.axis_index("dp"), lax.axis_index("din")
        mine = lax.dynamic_slice_in_dim(activations, lax.axis_index("dout") * half, half, 0)
        share = lax.dynamic_slice_in_dim(out_grads, column * part, part, 0)
        away = [lax.dynamic_slice_in_dim(share, (me ^ d) * rows, rows, 1) for d in [far, *others]]
        own = lax.dynamic_slice_in_dim(out_grads, me * rows, rows, 1).T
        turned = [block.T for block in away[1:]]
        return (mine, away[0]), (queries, activations, own, *turned[:-1], *jnp.split(turned[-1], [sizes[0]]))
    outs = [((half, width), activations.dtype), ((part, rows), dtype)]
    first = fetch(functools.partial(first_kernel, far), [activations, out_grads], outs, [], 2)
    outs = [(queries.shape, queries.dtype), (activations.shape, activations.dtype), ((rows, tokens), dtype)]
    outs += [((rows, part), dtype)] * (len(others) - 1) + [((size, part), dtype) for size in sizes]
    scratch = [pltpu.VMEM((tokens, rows), dtype), pltpu.VMEM((len(others), part, rows), dtype)]
    arrays = [activations, out_grads, queries]
    return first, fetch(functools.partial(rest_kernel, others), arrays, outs, scratch, len(others) + 3)


def on_device(activations, out_grads, queries):
    count, spread = lax.axis_size("dp"), lax.axis_size("din")

    def to_columns(arrived):
        return [arrived] + [trade(arrived, {"din": r}) for r in range(1, spread)]

    def acts_of(block):
        return [block, trade(block, {"dout": 1})]

    far, late = count - 1, count - 2
    early = list(range(1, late))
    rows = queries.shape[2]
    sizes = [rows // 7 * 5, rows - rows // 7 * 5]
    (mine, far_grads), (queries, own_acts, own, *sent) = cut(
        activations, out_grads, queries, far, early + [late], sizes
    )
    hops = [(mine, mine)]
    hops.append(pass_on(hops[0], 1, count))
    arrived = {d: trade(block, {"dp": d}) for d, block in zip([far, *early], [far_grads, *sent])}

    mix, token = mixed([own_acts], queries, SHORT)
    scores = scores_of_grads([own], mix)
    hops[1] = hold(list(hops[1]), [token])
    for step in range(2, count - 1):
        hops.append(pass_on(hops[-1], step, count))

    mixes, token = {}, scores
    for d in early:
        mixes[d], token = mixed(acts_of(from_partner(hops, d, count)), queries, SHORT, [token])
    tail = [trade(hold([block], [token])[0], {"dp": late}) for block in sent[len(early) :]]
    sides = to_columns(hold([arrived[far]], [*hops[1], *[arrived[d] for d in early]])[0])
    block = from_partner(hops, late, count, [token] + sides)
    end = lax.ppermute(block, "dp", [(1, 0), (count - 2, count - 1)])
    hops.append((end, end))

    proj, token = projected(sides, queries, SHORT, [token])
    terms = []
    for d in early:
        sides = to_columns(hold([arrived[d]], hops[1])[0])
        token = scores_of_grads(sides, mixes[d], [token])
        terms.append(trade(token, {"dp": d}))

    mix, done = mixed(acts_of(block), queries, SHORT, [token])
    tail = [to_columns(hold([piece], [done if p else token], LONG)[0]) for p, piece in enumerate(tail)]
    block = from_partner(hops, far, count, [done])
    terms.append(trade(scores_of_acts(*acts_of(block), proj), {"dp": far}))
    term = scores_of_grads(tail[0], mix)
    term = scores_of_grads(tail[1], mix, (), LONG, sizes[0], [term])
    terms.append(trade(term, {"dp": late}))
    return over_chips(sum(terms, scores), spread)


def over_chips(scores, spread):
    scores = scores + trade(scores, {"dout": 1})
    return scores + sum(trade(scores, {"din": r}) for r in range(1, spread))


def solution(mesh):
    placed = (P(("groups", "dp"), "din"), P(("groups", "dp"), "dout"), P(None, "dout", "dp", "din"))
    return jax.shard_map(
        on_device, mesh=mesh, in_specs=placed, out_specs=P(None, ("groups", "dp")), check_vma=False
    )
```

```python
import functools
import math

import jax
import jax.numpy as jnp
from jax import lax
from jax.experimental import pallas as pl
from jax.experimental.pallas import tpu as pltpu
from jax.sharding import PartitionSpec as P


LONG, SHORT = 14_000_000_000, 1_000_000


def trade(block, steps, backwards=False):
    axes = tuple(steps)
    sizes = [lax.axis_size(axis) for axis in axes]
    mask = 0
    for axis, size in zip(axes, sizes):
        mask = mask * size + steps[axis]
    route = [(i, i ^ mask) for i in range(math.prod(sizes))]
    return lax.ppermute(block, axes, route[::-1] if backwards else route)


def pass_on(block, step, count):
    up = lax.ppermute(block[0], "dp", [(i, i + 1) for i in range(step - 1, count - 1)])
    down = lax.ppermute(block[1], "dp", [(i, i - 1) for i in range(1, count - step + 1)])
    return up, down


ANYWHERE = pl.BlockSpec(memory_space=pl.ANY)
NEAR = pl.BlockSpec(memory_space=pltpu.VMEM)


def call(kernel, arrays, outs, flops=1024, tokens=(), scratch=()):
    skip = len(tokens)

    def body(*refs):
        kernel(*refs[: len(arrays)], *refs[len(arrays) + skip :])

    return pl.pallas_call(
        body,
        in_specs=[NEAR] * len(arrays) + [ANYWHERE] * skip,
        out_specs=[NEAR] * len(outs),
        out_shape=[pltpu.VMEM(shape, dtype) for shape, dtype in outs],
        scratch_shapes=list(scratch),
        compiler_params=pltpu.CompilerParams(vmem_limit_bytes=12 * 1024 * 1024),
        cost_estimate=pl.CostEstimate(flops=flops, bytes_accessed=1024, transcendentals=0),
    )(*[pltpu.with_memory_space_constraint(array, pltpu.VMEM) for array in arrays], *tokens)


def fetch(kernel, arrays, outs, scratch, copies):
    return pl.pallas_call(
        kernel,
        in_specs=[ANYWHERE] * len(arrays),
        out_specs=[NEAR] * len(outs),
        out_shape=[pltpu.VMEM(shape, dtype) for shape, dtype in outs],
        scratch_shapes=[*scratch, pltpu.SemaphoreType.DMA((copies,))],
        compiler_params=pltpu.CompilerParams(vmem_limit_bytes=12 * 1024 * 1024),
        cost_estimate=pl.CostEstimate(flops=1024, bytes_accessed=1024, transcendentals=0),
    )(*[pltpu.with_memory_space_constraint(array, pltpu.HBM) for array in arrays])


def grads_block(grads_ref, device, part, rows):
    first = pl.multiple_of(lax.axis_index("din") * part, part)
    return grads_ref.at[pl.ds(first, part), pl.ds(pl.multiple_of(device * rows, rows), rows)]


def first_kernel(far, acts_ref, grads_ref, mine_ref, far_ref, arrived):
    half = mine_ref.shape[0]
    rows = pl.ds(pl.multiple_of(lax.axis_index("dout") * half, half), half)
    block = grads_block(grads_ref, lax.axis_index("dp") ^ far, *far_ref.shape)
    copies = [
        pltpu.make_async_copy(acts_ref.at[rows, :], mine_ref, arrived.at[0]),
        pltpu.make_async_copy(block, far_ref, arrived.at[1]),
    ]
    for copy in copies:
        copy.start()
    for copy in copies:
        copy.wait()


def rest_kernel(steps, acts_ref, grads_ref, query_ref, near_query, near_acts, own_out, *refs):
    outs, own, blocks, arrived = list(refs[:-3]), refs[-3], refs[-2], refs[-1]
    me = lax.axis_index("dp")
    tokens, rows = own.shape
    copies = [pltpu.make_async_copy(grads_ref.at[:, pl.ds(pl.multiple_of(me * rows, rows), rows)], own, arrived.at[0])]
    for k, d in enumerate(steps):
        block = grads_block(grads_ref, me ^ d, *blocks.shape[1:])
        copies.append(pltpu.make_async_copy(block, blocks.at[k], arrived.at[1 + k]))
    copies.append(pltpu.make_async_copy(acts_ref, near_acts, arrived.at[len(steps) + 1]))
    copies.append(pltpu.make_async_copy(query_ref, near_query, arrived.at[len(steps) + 2]))
    for copy in copies:
        copy.start()
    for k in range(len(steps)):
        copies[1 + k].wait()
        turned, at = blocks[k].astype(jnp.float32).T.astype(blocks.dtype), 0
        while at < rows:
            out = outs.pop(0)
            out[...] = turned[at : at + out.shape[0]]
            at += out.shape[0]
    copies[0].wait()
    own_out[...] = own[...].astype(jnp.float32).T.astype(own_out.dtype)
    for copy in copies[-2:]:
        copy.wait()


def hold(blocks, tokens, flops=1024):
    count = len(blocks)
    return pl.pallas_call(
        lambda *refs: None,
        in_specs=[ANYWHERE] * (count + len(tokens)),
        out_specs=[ANYWHERE] * count,
        out_shape=[jax.ShapeDtypeStruct(block.shape, block.dtype) for block in blocks],
        input_output_aliases={i: i for i in range(count)},
        compiler_params=pltpu.CompilerParams(vmem_limit_bytes=1024 * 1024),
        cost_estimate=pl.CostEstimate(flops=flops, bytes_accessed=1024, transcendentals=0),
    )(*blocks, *tokens)


def pick_kernel(choice, *refs):
    *blocks, out_ref = refs
    me = lax.axis_index("dp")
    where = functools.reduce(lambda found, z: jnp.where(me == z, choice[z], found), range(len(choice)), 0)
    for k, block in enumerate(blocks):

        @pl.when(where == k)
        def _():
            out_ref[...] = block[...]


def from_partner(hops, d, count, tokens=()):
    sources, choice = [], []
    for z in range(count):
        away = z - (z ^ d)
        source = (abs(away), int(away < 0 and abs(away) < count - 1))
        if source not in sources:
            sources.append(source)
        choice.append(sources.index(source))
    blocks = [hops[step][way] for step, way in sources]
    outs = [(blocks[0].shape, blocks[0].dtype)]
    return call(functools.partial(pick_kernel, choice), blocks, outs, tokens=tokens)[0]


def joined(parts, axis):
    parts = [part[...] for part in parts]
    if len(parts) == 1:
        return parts[0]
    column, found = lax.axis_index("din"), []
    for p in range(len(parts)):
        chosen = parts[0]
        for r in range(1, len(parts)):
            chosen = jnp.where(column == p ^ r, parts[r], chosen)
        found.append(chosen)
    return jnp.concatenate(found, axis=axis)


MARK = (8, 128), jnp.float32


def mix_kernel(*refs):
    *parts, query_ref, out_ref, mark_ref, acts = refs
    mark_ref[...] = jnp.zeros_like(mark_ref)
    half = parts[0].shape[0]
    first = lax.axis_index("dout") * half if len(parts) > 1 else 0
    for part, at in zip(parts, (first, half - first)):
        acts[pl.ds(pl.multiple_of(at, half), half), :] = part[...]

    def step(q, _):
        out_ref[q] = lax.dot_general(
            query_ref[q, 0], acts[...], (((1,), (1,)), ((), ())), preferred_element_type=jnp.float32
        )
        return 0

    lax.fori_loop(0, query_ref.shape[0], step, 0)


def mixed(parts, queries, flops, tokens=()):
    nq, _, depth, width = queries.shape
    tokens_here = sum(part.shape[0] for part in parts)
    outs = [((nq, depth, tokens_here), jnp.float32), MARK]
    scratch = [pltpu.VMEM((tokens_here, width), queries.dtype)]
    return call(mix_kernel, [*parts, queries], outs, flops, tokens, scratch)


def score_kernel(pieces, *refs):
    *parts, mix_ref, out_ref = refs
    size = mix_ref.shape[1] // pieces
    for p in range(pieces):
        grads = joined(parts[p::pieces], 1).astype(jnp.float32)
        for q in range(mix_ref.shape[0]):
            term = jnp.sum(grads * mix_ref[q, p * size : (p + 1) * size], axis=0, keepdims=True)
            out_ref[q : q + 1, :] = term if p == 0 else out_ref[q : q + 1, :] + term


def scores_of_grads(parts, mix, tokens=(), flops=1024):
    nq, _, count = mix.shape
    parts = [part if isinstance(part, list) else [part] for part in parts]
    kernel = functools.partial(score_kernel, len(parts[0]))
    return call(kernel, [*sum(parts, []), mix], [((nq, count), jnp.float32)], flops, tokens)[0]


def project_kernel(*refs):
    *parts, query_ref, out_ref, mark_ref, grads = refs
    mark_ref[...] = jnp.zeros_like(mark_ref)
    grads[...] = joined(parts, 0)

    def step(q, _):
        out_ref[q] = jnp.dot(grads[...], query_ref[q, 0], preferred_element_type=jnp.float32)
        return 0

    lax.fori_loop(0, query_ref.shape[0], step, 0)


def projected(parts, queries, flops, tokens=()):
    nq, _, depth, width = queries.shape
    count = sum(part.shape[0] for part in parts)
    outs = [((nq, count, width), jnp.float32), MARK]
    scratch = [pltpu.VMEM((count, depth), queries.dtype)]
    return call(project_kernel, [*parts, queries], outs, flops, tokens, scratch)


def finish_kernel(mine_ref, other_ref, proj_ref, out_ref):
    half, width = mine_ref.shape
    swapped = lax.axis_index("dout") == 1
    for h, (first, second) in enumerate(((mine_ref, other_ref), (other_ref, mine_ref))):
        acts = jnp.where(swapped, second[...], first[...]).astype(jnp.float32)
        for q in range(proj_ref.shape[0]):
            terms = acts * proj_ref[q, h * half : (h + 1) * half, :]
            lanes = terms[:, :128]
            for at in range(128, width, 128):
                lanes = lanes + terms[:, at : at + 128]
            out_ref[q : q + 1, h * half : (h + 1) * half] = jnp.sum(lanes.T, axis=0, keepdims=True)


def scores_of_acts(mine, other, proj, tokens=()):
    nq, count, _ = proj.shape
    return call(finish_kernel, [mine, other, proj], [((nq, count), jnp.float32)], tokens=tokens)[0]


def cut(activations, out_grads, queries, far, others, pieces):
    count, part = lax.axis_size("dp"), out_grads.shape[0] // lax.axis_size("din")
    rows, (tokens, width), dtype = queries.shape[2], activations.shape, out_grads.dtype
    half = tokens // 2
    if part % 128 or rows % 128:
        me, column = lax.axis_index("dp"), lax.axis_index("din")
        mine = lax.dynamic_slice_in_dim(activations, lax.axis_index("dout") * half, half, 0)
        share = lax.dynamic_slice_in_dim(out_grads, column * part, part, 0)
        away = [lax.dynamic_slice_in_dim(share, (me ^ d) * rows, rows, 1) for d in [far, *others]]
        own = lax.dynamic_slice_in_dim(out_grads, me * rows, rows, 1).T
        turned = [block.T for block in away[1:]]
        return (mine, away[0]), (queries, activations, own, *turned[:-1], *jnp.split(turned[-1], pieces))
    outs = [((half, width), activations.dtype), ((part, rows), dtype)]
    first = fetch(functools.partial(first_kernel, far), [activations, out_grads], outs, [], 2)
    outs = [(queries.shape, queries.dtype), (activations.shape, activations.dtype), ((rows, tokens), dtype)]
    outs += [((rows, part), dtype)] * (len(others) - 1) + [((rows // pieces, part), dtype)] * pieces
    scratch = [pltpu.VMEM((tokens, rows), dtype), pltpu.VMEM((len(others), part, rows), dtype)]
    arrays = [activations, out_grads, queries]
    return first, fetch(functools.partial(rest_kernel, others), arrays, outs, scratch, len(others) + 3)


def on_device(activations, out_grads, queries):
    count, spread = lax.axis_size("dp"), lax.axis_size("din")

    def to_columns(arrived):
        return [arrived] + [trade(arrived, {"din": r}) for r in range(1, spread)]

    def acts_of(block):
        return [block, trade(block, {"dout": 1})]

    far, late = count - 1, count - 2
    early = list(range(1, late))
    pieces = 2
    (mine, far_grads), (queries, own_acts, own, *sent) = cut(
        activations, out_grads, queries, far, early + [late], pieces
    )
    hops = [(mine, mine)]
    hops.append(pass_on(hops[0], 1, count))
    arrived = {d: trade(block, {"dp": d}) for d, block in zip([far, *early], [far_grads, *sent])}

    mix, token = mixed([own_acts], queries, SHORT)
    scores = scores_of_grads([own], mix)
    hops[1] = hold(list(hops[1]), [token])
    for step in range(2, count - 1):
        hops.append(pass_on(hops[-1], step, count))

    mixes, token = {}, scores
    for d in early:
        mixes[d], token = mixed(acts_of(from_partner(hops, d, count)), queries, SHORT, [token])
    tail = [trade(hold([block], [token])[0], {"dp": late}) for block in sent[len(early) :]]
    sides = to_columns(hold([arrived[far]], [*hops[1], *[arrived[d] for d in early]])[0])
    block = from_partner(hops, late, count, [token] + sides)
    end = lax.ppermute(block, "dp", [(1, 0), (count - 2, count - 1)])
    hops.append((end, end))

    proj, token = projected(sides, queries, SHORT, [token])
    terms = []
    for d in early:
        sides = to_columns(hold([arrived[d]], hops[1])[0])
        token = scores_of_grads(sides, mixes[d], [token])
        terms.append(trade(token, {"dp": d}))

    mix, done = mixed(acts_of(block), queries, SHORT, [token])
    tail = [to_columns(hold([piece], [done if p else token], LONG)[0]) for p, piece in enumerate(tail)]
    block = from_partner(hops, far, count, [done])
    terms.append(trade(scores_of_acts(*acts_of(block), proj), {"dp": far}))
    terms.append(trade(scores_of_grads([list(sides) for sides in zip(*tail)], mix, (), LONG), {"dp": late}))
    return over_chips(sum(terms, scores), spread)


def over_chips(scores, spread):
    scores = scores + trade(scores, {"dout": 1})
    return scores + sum(trade(scores, {"din": r}) for r in range(1, spread))


def solution(mesh):
    placed = (P(("groups", "dp"), "din"), P(("groups", "dp"), "dout"), P(None, "dout", "dp", "din"))
    return jax.shard_map(
        on_device, mesh=mesh, in_specs=placed, out_specs=P(None, ("groups", "dp")), check_vma=False
    )
```

```python
import functools
import math

import jax
import jax.numpy as jnp
from jax import lax
from jax.experimental import pallas as pl
from jax.experimental.pallas import tpu as pltpu
from jax.sharding import PartitionSpec as P


LONG, SHORT = 14_000_000_000, 1_000_000


def trade(block, steps, backwards=False):
    axes = tuple(steps)
    sizes = [lax.axis_size(axis) for axis in axes]
    mask = 0
    for axis, size in zip(axes, sizes):
        mask = mask * size + steps[axis]
    route = [(i, i ^ mask) for i in range(math.prod(sizes))]
    return lax.ppermute(block, axes, route[::-1] if backwards else route)


def pass_on(block, step, count):
    up = lax.ppermute(block[0], "dp", [(i, i + 1) for i in range(step - 1, count - 1)])
    down = lax.ppermute(block[1], "dp", [(i, i - 1) for i in range(1, count - step + 1)])
    return up, down


ANYWHERE = pl.BlockSpec(memory_space=pl.ANY)
NEAR = pl.BlockSpec(memory_space=pltpu.VMEM)


def call(kernel, arrays, outs, flops=1024, tokens=(), scratch=()):
    skip = len(tokens)

    def body(*refs):
        kernel(*refs[: len(arrays)], *refs[len(arrays) + skip :])

    return pl.pallas_call(
        body,
        in_specs=[NEAR] * len(arrays) + [ANYWHERE] * skip,
        out_specs=[NEAR] * len(outs),
        out_shape=[pltpu.VMEM(shape, dtype) for shape, dtype in outs],
        scratch_shapes=list(scratch),
        compiler_params=pltpu.CompilerParams(vmem_limit_bytes=12 * 1024 * 1024),
        cost_estimate=pl.CostEstimate(flops=flops, bytes_accessed=1024, transcendentals=0),
    )(*[pltpu.with_memory_space_constraint(array, pltpu.VMEM) for array in arrays], *tokens)


def fetch(kernel, arrays, outs, scratch, copies):
    return pl.pallas_call(
        kernel,
        in_specs=[ANYWHERE] * len(arrays),
        out_specs=[NEAR] * len(outs),
        out_shape=[pltpu.VMEM(shape, dtype) for shape, dtype in outs],
        scratch_shapes=[*scratch, pltpu.SemaphoreType.DMA((copies,))],
        compiler_params=pltpu.CompilerParams(vmem_limit_bytes=12 * 1024 * 1024),
        cost_estimate=pl.CostEstimate(flops=1024, bytes_accessed=1024, transcendentals=0),
    )(*[pltpu.with_memory_space_constraint(array, pltpu.HBM) for array in arrays])


def grads_block(grads_ref, device, part, rows):
    first = pl.multiple_of(lax.axis_index("din") * part, part)
    return grads_ref.at[pl.ds(first, part), pl.ds(pl.multiple_of(device * rows, rows), rows)]


def first_kernel(far, acts_ref, grads_ref, mine_ref, far_ref, arrived):
    half = mine_ref.shape[0]
    rows = pl.ds(pl.multiple_of(lax.axis_index("dout") * half, half), half)
    block = grads_block(grads_ref, lax.axis_index("dp") ^ far, *far_ref.shape)
    copies = [
        pltpu.make_async_copy(acts_ref.at[rows, :], mine_ref, arrived.at[0]),
        pltpu.make_async_copy(block, far_ref, arrived.at[1]),
    ]
    for copy in copies:
        copy.start()
    for copy in copies:
        copy.wait()


def rest_kernel(steps, acts_ref, grads_ref, query_ref, near_query, near_acts, own_out, *refs):
    outs, own, blocks, arrived = list(refs[:-3]), refs[-3], refs[-2], refs[-1]
    me = lax.axis_index("dp")
    tokens, rows = own.shape
    copies = [pltpu.make_async_copy(grads_ref.at[:, pl.ds(pl.multiple_of(me * rows, rows), rows)], own, arrived.at[0])]
    for k, d in enumerate(steps):
        block = grads_block(grads_ref, me ^ d, *blocks.shape[1:])
        copies.append(pltpu.make_async_copy(block, blocks.at[k], arrived.at[1 + k]))
    copies.append(pltpu.make_async_copy(acts_ref, near_acts, arrived.at[len(steps) + 1]))
    copies.append(pltpu.make_async_copy(query_ref, near_query, arrived.at[len(steps) + 2]))
    for copy in copies:
        copy.start()
    for k in range(len(steps)):
        copies[1 + k].wait()
        turned, at = blocks[k].astype(jnp.float32).T.astype(blocks.dtype), 0
        while at < rows:
            out = outs.pop(0)
            out[...] = turned[at : at + out.shape[0]]
            at += out.shape[0]
    copies[0].wait()
    own_out[...] = own[...].astype(jnp.float32).T.astype(own_out.dtype)
    for copy in copies[-2:]:
        copy.wait()


def hold(blocks, tokens, flops=1024):
    count = len(blocks)
    return pl.pallas_call(
        lambda *refs: None,
        in_specs=[ANYWHERE] * (count + len(tokens)),
        out_specs=[ANYWHERE] * count,
        out_shape=[jax.ShapeDtypeStruct(block.shape, block.dtype) for block in blocks],
        input_output_aliases={i: i for i in range(count)},
        compiler_params=pltpu.CompilerParams(vmem_limit_bytes=1024 * 1024),
        cost_estimate=pl.CostEstimate(flops=flops, bytes_accessed=1024, transcendentals=0),
    )(*blocks, *tokens)


def pick_kernel(choice, *refs):
    *blocks, out_ref = refs
    me = lax.axis_index("dp")
    where = functools.reduce(lambda found, z: jnp.where(me == z, choice[z], found), range(len(choice)), 0)
    for k, block in enumerate(blocks):

        @pl.when(where == k)
        def _():
            out_ref[...] = block[...]


def from_partner(hops, d, count, tokens=()):
    sources, choice = [], []
    for z in range(count):
        away = z - (z ^ d)
        source = (abs(away), int(away < 0 and abs(away) < count - 1))
        if source not in sources:
            sources.append(source)
        choice.append(sources.index(source))
    blocks = [hops[step][way] for step, way in sources]
    outs = [(blocks[0].shape, blocks[0].dtype)]
    return call(functools.partial(pick_kernel, choice), blocks, outs, tokens=tokens)[0]


def joined(parts, axis):
    parts = [part[...] for part in parts]
    if len(parts) == 1:
        return parts[0]
    column, found = lax.axis_index("din"), []
    for p in range(len(parts)):
        chosen = parts[0]
        for r in range(1, len(parts)):
            chosen = jnp.where(column == p ^ r, parts[r], chosen)
        found.append(chosen)
    return jnp.concatenate(found, axis=axis)


MARK = (8, 128), jnp.float32


def mix_kernel(*refs):
    *parts, query_ref, out_ref, mark_ref, acts = refs
    mark_ref[...] = jnp.zeros_like(mark_ref)
    half = parts[0].shape[0]
    first = lax.axis_index("dout") * half if len(parts) > 1 else 0
    for part, at in zip(parts, (first, half - first)):
        acts[pl.ds(pl.multiple_of(at, half), half), :] = part[...]

    def step(q, _):
        out_ref[q] = lax.dot_general(
            query_ref[q, 0], acts[...], (((1,), (1,)), ((), ())), preferred_element_type=jnp.float32
        )
        return 0

    lax.fori_loop(0, query_ref.shape[0], step, 0)


def mixed(parts, queries, flops, tokens=()):
    nq, _, depth, width = queries.shape
    tokens_here = sum(part.shape[0] for part in parts)
    outs = [((nq, depth, tokens_here), jnp.float32), MARK]
    scratch = [pltpu.VMEM((tokens_here, width), queries.dtype)]
    return call(mix_kernel, [*parts, queries], outs, flops, tokens, scratch)


def score_kernel(pieces, *refs):
    *parts, mix_ref, out_ref = refs
    size = mix_ref.shape[1] // pieces
    for p in range(pieces):
        grads = joined(parts[p::pieces], 1).astype(jnp.float32)
        for q in range(mix_ref.shape[0]):
            term = jnp.sum(grads * mix_ref[q, p * size : (p + 1) * size], axis=0, keepdims=True)
            out_ref[q : q + 1, :] = term if p == 0 else out_ref[q : q + 1, :] + term


def scores_of_grads(parts, mix, tokens=(), flops=1024):
    nq, _, count = mix.shape
    parts = [part if isinstance(part, list) else [part] for part in parts]
    kernel = functools.partial(score_kernel, len(parts[0]))
    return call(kernel, [*sum(parts, []), mix], [((nq, count), jnp.float32)], flops, tokens)[0]


def project_kernel(*refs):
    *parts, query_ref, out_ref, mark_ref, grads = refs
    mark_ref[...] = jnp.zeros_like(mark_ref)
    grads[...] = joined(parts, 0)

    def step(q, _):
        out_ref[q] = jnp.dot(grads[...], query_ref[q, 0], preferred_element_type=jnp.float32)
        return 0

    lax.fori_loop(0, query_ref.shape[0], step, 0)


def projected(parts, queries, flops, tokens=()):
    nq, _, depth, width = queries.shape
    count = sum(part.shape[0] for part in parts)
    outs = [((nq, count, width), jnp.float32), MARK]
    scratch = [pltpu.VMEM((count, depth), queries.dtype)]
    return call(project_kernel, [*parts, queries], outs, flops, tokens, scratch)


def finish_kernel(mine_ref, other_ref, proj_ref, out_ref):
    half, width = mine_ref.shape
    swapped = lax.axis_index("dout") == 1
    for h, (first, second) in enumerate(((mine_ref, other_ref), (other_ref, mine_ref))):
        acts = jnp.where(swapped, second[...], first[...]).astype(jnp.float32)
        for q in range(proj_ref.shape[0]):
            terms = acts * proj_ref[q, h * half : (h + 1) * half, :]
            lanes = terms[:, :128]
            for at in range(128, width, 128):
                lanes = lanes + terms[:, at : at + 128]
            out_ref[q : q + 1, h * half : (h + 1) * half] = jnp.sum(lanes.T, axis=0, keepdims=True)


def scores_of_acts(mine, other, proj, tokens=()):
    nq, count, _ = proj.shape
    return call(finish_kernel, [mine, other, proj], [((nq, count), jnp.float32)], tokens=tokens)[0]


def cut(activations, out_grads, queries, far, others, pieces):
    count, part = lax.axis_size("dp"), out_grads.shape[0] // lax.axis_size("din")
    rows, (tokens, width), dtype = queries.shape[2], activations.shape, out_grads.dtype
    half = tokens // 2
    if part % 128 or rows % 128:
        me, column = lax.axis_index("dp"), lax.axis_index("din")
        mine = lax.dynamic_slice_in_dim(activations, lax.axis_index("dout") * half, half, 0)
        share = lax.dynamic_slice_in_dim(out_grads, column * part, part, 0)
        away = [lax.dynamic_slice_in_dim(share, (me ^ d) * rows, rows, 1) for d in [far, *others]]
        own = lax.dynamic_slice_in_dim(out_grads, me * rows, rows, 1).T
        turned = [block.T for block in away[1:]]
        return (mine, away[0]), (queries, activations, own, *turned[:-1], *jnp.split(turned[-1], pieces))
    outs = [((half, width), activations.dtype), ((part, rows), dtype)]
    first = fetch(functools.partial(first_kernel, far), [activations, out_grads], outs, [], 2)
    outs = [(queries.shape, queries.dtype), (activations.shape, activations.dtype), ((rows, tokens), dtype)]
    outs += [((rows, part), dtype)] * (len(others) - 1) + [((rows // pieces, part), dtype)] * pieces
    scratch = [pltpu.VMEM((tokens, rows), dtype), pltpu.VMEM((len(others), part, rows), dtype)]
    arrays = [activations, out_grads, queries]
    return first, fetch(functools.partial(rest_kernel, others), arrays, outs, scratch, len(others) + 3)


def on_device(activations, out_grads, queries):
    count, spread = lax.axis_size("dp"), lax.axis_size("din")

    def to_columns(arrived):
        return [arrived] + [trade(arrived, {"din": r}) for r in range(1, spread)]

    def acts_of(block):
        return [block, trade(block, {"dout": 1})]

    far, late = count - 1, count - 2
    early = list(range(1, late))
    pieces = 2
    (mine, far_grads), (queries, own_acts, own, *sent) = cut(
        activations, out_grads, queries, far, early + [late], pieces
    )
    hops = [(mine, mine)]
    hops.append(pass_on(hops[0], 1, count))
    arrived = {d: trade(block, {"dp": d}) for d, block in zip([far, *early], [far_grads, *sent])}

    mix, token = mixed([own_acts], queries, SHORT)
    scores = scores_of_grads([own], mix)
    hops[1] = hold(list(hops[1]), [token])
    for step in range(2, count - 1):
        hops.append(pass_on(hops[-1], step, count))

    mixes, token = {}, scores
    for d in early:
        mixes[d], token = mixed(acts_of(from_partner(hops, d, count)), queries, SHORT, [token])
    tail = [trade(hold([block], [token])[0], {"dp": late}) for block in sent[len(early) :]]
    sides = to_columns(hold([arrived[far]], [*hops[1], *[arrived[d] for d in early]])[0])
    block = from_partner(hops, late, count, [token] + sides)
    end = lax.ppermute(block, "dp", [(1, 0), (count - 2, count - 1)])
    hops.append((end, end))

    proj, token = projected(sides, queries, SHORT, [token])
    terms = []
    for d in early:
        sides = to_columns(hold([arrived[d]], hops[1])[0])
        token = scores_of_grads(sides, mixes[d], [token])
        terms.append(trade(token, {"dp": d}))

    mix, done = mixed(acts_of(block), queries, SHORT, [token])
    tail = [to_columns(hold([piece], [done if p else token], LONG)[0]) for p, piece in enumerate(tail)]
    block = from_partner(hops, far, count, [done])
    terms.append(trade(scores_of_acts(*acts_of(block), proj), {"dp": far}))
    terms.append(trade(scores_of_grads([list(sides) for sides in zip(*tail)], mix, (), LONG), {"dp": late}))
    return over_chips(sum(terms, scores), spread)


def over_chips(scores, spread):
    others = [(r, c) for r in range(spread) for c in range(2)][1:]
    return scores + sum(trade(scores, {"din": r, "dout": c}) for r, c in others)


def solution(mesh):
    placed = (P(("groups", "dp"), "din"), P(("groups", "dp"), "dout"), P(None, "dout", "dp", "din"))
    return jax.shard_map(
        on_device, mesh=mesh, in_specs=placed, out_specs=P(None, ("groups", "dp")), check_vma=False
    )
```

```python
import functools
import math

import jax
import jax.numpy as jnp
from jax import lax
from jax.experimental import pallas as pl
from jax.experimental.pallas import tpu as pltpu
from jax.sharding import PartitionSpec as P


LONG, MIDDLE, SHORT = 14_000_000_000, 14_000_000_000, 1_000_000


def trade(block, steps, backwards=False):
    axes = tuple(steps)
    sizes = [lax.axis_size(axis) for axis in axes]
    mask = 0
    for axis, size in zip(axes, sizes):
        mask = mask * size + steps[axis]
    route = [(i, i ^ mask) for i in range(math.prod(sizes))]
    return lax.ppermute(block, axes, route[::-1] if backwards else route)


def pass_on(block, step, count):
    up = lax.ppermute(block[0], "dp", [(i, i + 1) for i in range(step - 1, count - 1)])
    down = lax.ppermute(block[1], "dp", [(i, i - 1) for i in range(1, count - step + 1)])
    return up, down


ANYWHERE = pl.BlockSpec(memory_space=pl.ANY)
NEAR = pl.BlockSpec(memory_space=pltpu.VMEM)


def call(kernel, arrays, outs, flops=1024, tokens=(), scratch=()):
    skip = len(tokens)

    def body(*refs):
        kernel(*refs[: len(arrays)], *refs[len(arrays) + skip :])

    return pl.pallas_call(
        body,
        in_specs=[NEAR] * len(arrays) + [ANYWHERE] * skip,
        out_specs=[NEAR] * len(outs),
        out_shape=[pltpu.VMEM(shape, dtype) for shape, dtype in outs],
        scratch_shapes=list(scratch),
        compiler_params=pltpu.CompilerParams(vmem_limit_bytes=12 * 1024 * 1024),
        cost_estimate=pl.CostEstimate(flops=flops, bytes_accessed=1024, transcendentals=0),
    )(*[pltpu.with_memory_space_constraint(array, pltpu.VMEM) for array in arrays], *tokens)


def fetch(kernel, arrays, outs, scratch, copies):
    return pl.pallas_call(
        kernel,
        in_specs=[ANYWHERE] * len(arrays),
        out_specs=[NEAR] * len(outs),
        out_shape=[pltpu.VMEM(shape, dtype) for shape, dtype in outs],
        scratch_shapes=[*scratch, pltpu.SemaphoreType.DMA((copies,))],
        compiler_params=pltpu.CompilerParams(vmem_limit_bytes=12 * 1024 * 1024),
        cost_estimate=pl.CostEstimate(flops=1024, bytes_accessed=1024, transcendentals=0),
    )(*[pltpu.with_memory_space_constraint(array, pltpu.HBM) for array in arrays])


def grads_block(grads_ref, device, part, rows):
    first = pl.multiple_of(lax.axis_index("din") * part, part)
    return grads_ref.at[pl.ds(first, part), pl.ds(pl.multiple_of(device * rows, rows), rows)]


def first_kernel(far, acts_ref, grads_ref, mine_ref, far_ref, arrived):
    half = mine_ref.shape[0]
    rows = pl.ds(pl.multiple_of(lax.axis_index("dout") * half, half), half)
    block = grads_block(grads_ref, lax.axis_index("dp") ^ far, *far_ref.shape)
    copies = [
        pltpu.make_async_copy(acts_ref.at[rows, :], mine_ref, arrived.at[0]),
        pltpu.make_async_copy(block, far_ref, arrived.at[1]),
    ]
    for copy in copies:
        copy.start()
    for copy in copies:
        copy.wait()


def rest_kernel(steps, acts_ref, grads_ref, query_ref, near_query, near_acts, own_out, *refs):
    outs, own, blocks, arrived = list(refs[:-3]), refs[-3], refs[-2], refs[-1]
    me = lax.axis_index("dp")
    tokens, rows = own.shape
    copies = [pltpu.make_async_copy(grads_ref.at[:, pl.ds(pl.multiple_of(me * rows, rows), rows)], own, arrived.at[0])]
    for k, d in enumerate(steps):
        block = grads_block(grads_ref, me ^ d, *blocks.shape[1:])
        copies.append(pltpu.make_async_copy(block, blocks.at[k], arrived.at[1 + k]))
    copies.append(pltpu.make_async_copy(acts_ref, near_acts, arrived.at[len(steps) + 1]))
    copies.append(pltpu.make_async_copy(query_ref, near_query, arrived.at[len(steps) + 2]))
    for copy in copies:
        copy.start()
    for k in range(len(steps)):
        copies[1 + k].wait()
        turned, at = blocks[k].astype(jnp.float32).T.astype(blocks.dtype), 0
        while at < rows:
            out = outs.pop(0)
            out[...] = turned[at : at + out.shape[0]]
            at += out.shape[0]
    copies[0].wait()
    own_out[...] = own[...].astype(jnp.float32).T.astype(own_out.dtype)
    for copy in copies[-2:]:
        copy.wait()


def hold(blocks, tokens, flops=1024):
    count = len(blocks)
    return pl.pallas_call(
        lambda *refs: None,
        in_specs=[ANYWHERE] * (count + len(tokens)),
        out_specs=[ANYWHERE] * count,
        out_shape=[jax.ShapeDtypeStruct(block.shape, block.dtype) for block in blocks],
        input_output_aliases={i: i for i in range(count)},
        compiler_params=pltpu.CompilerParams(vmem_limit_bytes=1024 * 1024),
        cost_estimate=pl.CostEstimate(flops=flops, bytes_accessed=1024, transcendentals=0),
    )(*blocks, *tokens)


def pick_kernel(choice, *refs):
    *blocks, out_ref = refs
    me = lax.axis_index("dp")
    where = functools.reduce(lambda found, z: jnp.where(me == z, choice[z], found), range(len(choice)), 0)
    for k, block in enumerate(blocks):

        @pl.when(where == k)
        def _():
            out_ref[...] = block[...]


def chosen(first, second, where, count, tokens=()):
    choice = [int(z in where) for z in range(count)]
    outs = [(first.shape, first.dtype)]
    return call(functools.partial(pick_kernel, choice), [first, second], outs, tokens=tokens)[0]


def from_partner(hops, d, count, tokens=()):
    sources, choice = [], []
    for z in range(count):
        away = z - (z ^ d)
        source = (abs(away), int(away < 0 and abs(away) < count - 1))
        if source not in sources:
            sources.append(source)
        choice.append(sources.index(source))
    blocks = [hops[step][way] for step, way in sources]
    outs = [(blocks[0].shape, blocks[0].dtype)]
    return call(functools.partial(pick_kernel, choice), blocks, outs, tokens=tokens)[0]


def joined(parts, axis):
    parts = [part[...] for part in parts]
    if len(parts) == 1:
        return parts[0]
    column, found = lax.axis_index("din"), []
    for p in range(len(parts)):
        chosen = parts[0]
        for r in range(1, len(parts)):
            chosen = jnp.where(column == p ^ r, parts[r], chosen)
        found.append(chosen)
    return jnp.concatenate(found, axis=axis)


MARK = (8, 128), jnp.float32


def mix_kernel(*refs):
    *parts, query_ref, out_ref, mark_ref, acts = refs
    mark_ref[...] = jnp.zeros_like(mark_ref)
    half = parts[0].shape[0]
    first = lax.axis_index("dout") * half if len(parts) > 1 else 0
    for part, at in zip(parts, (first, half - first)):
        acts[pl.ds(pl.multiple_of(at, half), half), :] = part[...]

    def step(q, _):
        out_ref[q] = lax.dot_general(
            query_ref[q, 0], acts[...], (((1,), (1,)), ((), ())), preferred_element_type=jnp.float32
        )
        return 0

    lax.fori_loop(0, query_ref.shape[0], step, 0)


def mixed(parts, queries, flops, tokens=()):
    nq, _, depth, width = queries.shape
    tokens_here = sum(part.shape[0] for part in parts)
    outs = [((nq, depth, tokens_here), jnp.float32), MARK]
    scratch = [pltpu.VMEM((tokens_here, width), queries.dtype)]
    return call(mix_kernel, [*parts, queries], outs, flops, tokens, scratch)


def score_kernel(pieces, *refs):
    *parts, mix_ref, out_ref = refs
    size = mix_ref.shape[1] // pieces
    for p in range(pieces):
        grads = joined(parts[p::pieces], 1).astype(jnp.float32)
        for q in range(mix_ref.shape[0]):
            term = jnp.sum(grads * mix_ref[q, p * size : (p + 1) * size], axis=0, keepdims=True)
            out_ref[q : q + 1, :] = term if p == 0 else out_ref[q : q + 1, :] + term


def scores_of_grads(parts, mix, tokens=(), flops=1024):
    nq, _, count = mix.shape
    parts = [part if isinstance(part, list) else [part] for part in parts]
    kernel = functools.partial(score_kernel, len(parts[0]))
    return call(kernel, [*sum(parts, []), mix], [((nq, count), jnp.float32)], flops, tokens)[0]


def project_kernel(*refs):
    *parts, query_ref, out_ref, mark_ref, grads = refs
    mark_ref[...] = jnp.zeros_like(mark_ref)
    grads[...] = joined(parts, 0)

    def step(q, _):
        out_ref[q] = jnp.dot(grads[...], query_ref[q, 0], preferred_element_type=jnp.float32)
        return 0

    lax.fori_loop(0, query_ref.shape[0], step, 0)


def projected(parts, queries, flops, tokens=()):
    nq, _, depth, width = queries.shape
    count = sum(part.shape[0] for part in parts)
    outs = [((nq, count, width), jnp.float32), MARK]
    scratch = [pltpu.VMEM((count, depth), queries.dtype)]
    return call(project_kernel, [*parts, queries], outs, flops, tokens, scratch)


def finish_kernel(mine_ref, other_ref, proj_ref, out_ref):
    half, width = mine_ref.shape
    swapped = lax.axis_index("dout") == 1
    for h, (first, second) in enumerate(((mine_ref, other_ref), (other_ref, mine_ref))):
        acts = jnp.where(swapped, second[...], first[...]).astype(jnp.float32)
        for q in range(proj_ref.shape[0]):
            terms = acts * proj_ref[q, h * half : (h + 1) * half, :]
            lanes = terms[:, :128]
            for at in range(128, width, 128):
                lanes = lanes + terms[:, at : at + 128]
            out_ref[q : q + 1, h * half : (h + 1) * half] = jnp.sum(lanes.T, axis=0, keepdims=True)


def scores_of_acts(mine, other, proj, tokens=()):
    nq, count, _ = proj.shape
    return call(finish_kernel, [mine, other, proj], [((nq, count), jnp.float32)], tokens=tokens)[0]


def cut(activations, out_grads, queries, far, others, pieces):
    count, part = lax.axis_size("dp"), out_grads.shape[0] // lax.axis_size("din")
    rows, (tokens, width), dtype = queries.shape[2], activations.shape, out_grads.dtype
    half = tokens // 2
    if part % 128 or rows % 128:
        me, column = lax.axis_index("dp"), lax.axis_index("din")
        mine = lax.dynamic_slice_in_dim(activations, lax.axis_index("dout") * half, half, 0)
        share = lax.dynamic_slice_in_dim(out_grads, column * part, part, 0)
        away = [lax.dynamic_slice_in_dim(share, (me ^ d) * rows, rows, 1) for d in [far, *others]]
        own = lax.dynamic_slice_in_dim(out_grads, me * rows, rows, 1).T
        turned = [block.T for block in away[1:]]
        return (mine, away[0]), (queries, activations, own, *turned[:-1], *jnp.split(turned[-1], pieces))
    outs = [((half, width), activations.dtype), ((part, rows), dtype)]
    first = fetch(functools.partial(first_kernel, far), [activations, out_grads], outs, [], 2)
    outs = [(queries.shape, queries.dtype), (activations.shape, activations.dtype), ((rows, tokens), dtype)]
    outs += [((rows, part), dtype)] * (len(others) - 1) + [((rows // pieces, part), dtype)] * pieces
    scratch = [pltpu.VMEM((tokens, rows), dtype), pltpu.VMEM((len(others), part, rows), dtype)]
    arrays = [activations, out_grads, queries]
    return first, fetch(functools.partial(rest_kernel, others), arrays, outs, scratch, len(others) + 3)


def on_device(activations, out_grads, queries):
    count, spread = lax.axis_size("dp"), lax.axis_size("din")

    def to_columns(arrived):
        return [arrived] + [trade(arrived, {"din": r}) for r in range(1, spread)]

    def acts_of(block):
        return [block, trade(block, {"dout": 1})]

    far, late = count - 1, count - 2
    early = list(range(1, late))
    pieces = 2
    (mine, far_grads), (queries, own_acts, own, *sent) = cut(
        activations, out_grads, queries, far, early + [late], pieces
    )
    hops = [(mine, mine)]
    hops.append(pass_on(hops[0], 1, count))
    arrived = {d: trade(block, {"dp": d}) for d, block in zip([far, *early], [far_grads, *sent])}

    mix, token = mixed([own_acts], queries, SHORT)
    scores = scores_of_grads([own], mix)
    hops[1] = hold(list(hops[1]), [token])
    for step in range(2, count - 1):
        hops.append(pass_on(hops[-1], step, count))

    mixes, token = {}, scores
    for d in early:
        mixes[d], token = mixed(acts_of(from_partner(hops, d, count)), queries, SHORT, [token])
    tail = list(hold(sent[len(early) :], [token]))
    inner = range(count // 4, count - count // 4)
    routes = [[(z, z ^ late) for z in range(count) if (z ^ late in inner) == inward] for inward in (False, True)]
    outward, = hold([lax.ppermute(tail[0], "dp", routes[0])], [], LONG)
    sides = to_columns(hold([arrived[far]], [*hops[1], *[arrived[d] for d in early]])[0])
    block = from_partner(hops, late, count, [token] + sides)
    end = lax.ppermute(block, "dp", [(1, 0), (count - 2, count - 1)])
    hops.append((end, end))
    inward = lax.ppermute(chosen(tail[0], tail[0], [], count, [block]), "dp", routes[1])
    inward, = hold([inward], [], MIDDLE)
    tail = [chosen(outward, inward, inner, count), trade(tail[1], {"dp": late})]

    proj, token = projected(sides, queries, SHORT, [token])
    terms = []
    for d in early:
        sides = to_columns(hold([arrived[d]], hops[1])[0])
        token = scores_of_grads(sides, mixes[d], [token])
        terms.append(trade(token, {"dp": d}))

    mix, done = mixed(acts_of(block), queries, SHORT, [token])
    tail = [to_columns(hold([piece], [done if p else token], LONG)[0]) for p, piece in enumerate(tail)]
    block = from_partner(hops, far, count, [done])
    terms.append(trade(scores_of_acts(*acts_of(block), proj), {"dp": far}))
    terms.append(trade(scores_of_grads([list(sides) for sides in zip(*tail)], mix, (), LONG), {"dp": late}))
    return over_chips(sum(terms, scores), spread)


def over_chips(scores, spread):
    scores = scores + trade(scores, {"dout": 1})
    return scores + sum(trade(scores, {"din": r}) for r in range(1, spread))


def solution(mesh):
    placed = (P(("groups", "dp"), "din"), P(("groups", "dp"), "dout"), P(None, "dout", "dp", "din"))
    return jax.shard_map(
        on_device, mesh=mesh, in_specs=placed, out_specs=P(None, ("groups", "dp")), check_vma=False
    )
```

```python
import functools
import math

import jax
import jax.numpy as jnp
from jax import lax
from jax.experimental import pallas as pl
from jax.experimental.pallas import tpu as pltpu
from jax.sharding import PartitionSpec as P


LONG, SHORT = 14_000_000_000, 1_000_000


def trade(block, steps, backwards=False):
    axes = tuple(steps)
    sizes = [lax.axis_size(axis) for axis in axes]
    mask = 0
    for axis, size in zip(axes, sizes):
        mask = mask * size + steps[axis]
    route = [(i, i ^ mask) for i in range(math.prod(sizes))]
    return lax.ppermute(block, axes, route[::-1] if backwards else route)


def pass_on(block, step, count):
    up = lax.ppermute(block[0], "dp", [(i, i + 1) for i in range(step - 1, count - 1)])
    down = lax.ppermute(block[1], "dp", [(i, i - 1) for i in range(1, count - step + 1)])
    return up, down


ANYWHERE = pl.BlockSpec(memory_space=pl.ANY)
NEAR = pl.BlockSpec(memory_space=pltpu.VMEM)


def call(kernel, arrays, outs, flops=1024, tokens=(), scratch=()):
    skip = len(tokens)

    def body(*refs):
        kernel(*refs[: len(arrays)], *refs[len(arrays) + skip :])

    return pl.pallas_call(
        body,
        in_specs=[NEAR] * len(arrays) + [ANYWHERE] * skip,
        out_specs=[NEAR] * len(outs),
        out_shape=[pltpu.VMEM(shape, dtype) for shape, dtype in outs],
        scratch_shapes=list(scratch),
        compiler_params=pltpu.CompilerParams(vmem_limit_bytes=12 * 1024 * 1024),
        cost_estimate=pl.CostEstimate(flops=flops, bytes_accessed=1024, transcendentals=0),
    )(*[pltpu.with_memory_space_constraint(array, pltpu.VMEM) for array in arrays], *tokens)


def fetch(kernel, arrays, outs, scratch, copies):
    return pl.pallas_call(
        kernel,
        in_specs=[ANYWHERE] * len(arrays),
        out_specs=[NEAR] * len(outs),
        out_shape=[pltpu.VMEM(shape, dtype) for shape, dtype in outs],
        scratch_shapes=[*scratch, pltpu.SemaphoreType.DMA((copies,))],
        compiler_params=pltpu.CompilerParams(vmem_limit_bytes=12 * 1024 * 1024),
        cost_estimate=pl.CostEstimate(flops=1024, bytes_accessed=1024, transcendentals=0),
    )(*[pltpu.with_memory_space_constraint(array, pltpu.HBM) for array in arrays])


def grads_block(grads_ref, device, part, rows):
    first = pl.multiple_of(lax.axis_index("din") * part, part)
    return grads_ref.at[pl.ds(first, part), pl.ds(pl.multiple_of(device * rows, rows), rows)]


def first_kernel(far, acts_ref, grads_ref, mine_ref, far_ref, arrived):
    half = mine_ref.shape[0]
    rows = pl.ds(pl.multiple_of(lax.axis_index("dout") * half, half), half)
    block = grads_block(grads_ref, lax.axis_index("dp") ^ far, *far_ref.shape)
    copies = [
        pltpu.make_async_copy(acts_ref.at[rows, :], mine_ref, arrived.at[0]),
        pltpu.make_async_copy(block, far_ref, arrived.at[1]),
    ]
    for copy in copies:
        copy.start()
    for copy in copies:
        copy.wait()


def rest_kernel(steps, acts_ref, grads_ref, query_ref, near_query, near_acts, own_out, *refs):
    outs, own, blocks, arrived = list(refs[:-3]), refs[-3], refs[-2], refs[-1]
    me = lax.axis_index("dp")
    tokens, rows = own.shape
    copies = [pltpu.make_async_copy(grads_ref.at[:, pl.ds(pl.multiple_of(me * rows, rows), rows)], own, arrived.at[0])]
    for k, d in enumerate(steps):
        block = grads_block(grads_ref, me ^ d, *blocks.shape[1:])
        copies.append(pltpu.make_async_copy(block, blocks.at[k], arrived.at[1 + k]))
    copies.append(pltpu.make_async_copy(acts_ref, near_acts, arrived.at[len(steps) + 1]))
    copies.append(pltpu.make_async_copy(query_ref, near_query, arrived.at[len(steps) + 2]))
    for copy in copies:
        copy.start()
    for k in range(len(steps)):
        copies[1 + k].wait()
        turned, at = blocks[k].astype(jnp.float32).T.astype(blocks.dtype), 0
        while at < rows:
            out = outs.pop(0)
            out[...] = turned[at : at + out.shape[0]]
            at += out.shape[0]
    copies[0].wait()
    own_out[...] = own[...].astype(jnp.float32).T.astype(own_out.dtype)
    for copy in copies[-2:]:
        copy.wait()


def hold(blocks, tokens, flops=1024):
    count = len(blocks)
    return pl.pallas_call(
        lambda *refs: None,
        in_specs=[ANYWHERE] * (count + len(tokens)),
        out_specs=[ANYWHERE] * count,
        out_shape=[jax.ShapeDtypeStruct(block.shape, block.dtype) for block in blocks],
        input_output_aliases={i: i for i in range(count)},
        compiler_params=pltpu.CompilerParams(vmem_limit_bytes=1024 * 1024),
        cost_estimate=pl.CostEstimate(flops=flops, bytes_accessed=1024, transcendentals=0),
    )(*blocks, *tokens)


def pick_kernel(choice, *refs):
    *blocks, out_ref = refs
    me = lax.axis_index("dp")
    where = functools.reduce(lambda found, z: jnp.where(me == z, choice[z], found), range(len(choice)), 0)
    for k, block in enumerate(blocks):

        @pl.when(where == k)
        def _():
            out_ref[...] = block[...]


def from_partner(hops, d, count, tokens=()):
    sources, choice = [], []
    for z in range(count):
        away = z - (z ^ d)
        source = (abs(away), int(away < 0 and abs(away) < count - 1))
        if source not in sources:
            sources.append(source)
        choice.append(sources.index(source))
    blocks = [hops[step][way] for step, way in sources]
    outs = [(blocks[0].shape, blocks[0].dtype)]
    return call(functools.partial(pick_kernel, choice), blocks, outs, tokens=tokens)[0]


def joined(parts, axis):
    parts = [part[...] for part in parts]
    if len(parts) == 1:
        return parts[0]
    column, found = lax.axis_index("din"), []
    for p in range(len(parts)):
        chosen = parts[0]
        for r in range(1, len(parts)):
            chosen = jnp.where(column == p ^ r, parts[r], chosen)
        found.append(chosen)
    return jnp.concatenate(found, axis=axis)


MARK = (8, 128), jnp.float32


def mix_kernel(*refs):
    *parts, query_ref, out_ref, mark_ref, acts = refs
    mark_ref[...] = jnp.zeros_like(mark_ref)
    half = parts[0].shape[0]
    first = lax.axis_index("dout") * half if len(parts) > 1 else 0
    for part, at in zip(parts, (first, half - first)):
        acts[pl.ds(pl.multiple_of(at, half), half), :] = part[...]

    def step(q, _):
        out_ref[q] = lax.dot_general(
            query_ref[q, 0], acts[...], (((1,), (1,)), ((), ())), preferred_element_type=jnp.float32
        )
        return 0

    lax.fori_loop(0, query_ref.shape[0], step, 0)


def mixed(parts, queries, flops, tokens=()):
    nq, _, depth, width = queries.shape
    tokens_here = sum(part.shape[0] for part in parts)
    outs = [((nq, depth, tokens_here), jnp.float32), MARK]
    scratch = [pltpu.VMEM((tokens_here, width), queries.dtype)]
    return call(mix_kernel, [*parts, queries], outs, flops, tokens, scratch)


def score_kernel(pieces, *refs):
    *parts, mix_ref, out_ref = refs
    size = mix_ref.shape[1] // pieces
    for p in range(pieces):
        grads = joined(parts[p::pieces], 1).astype(jnp.float32)
        for q in range(mix_ref.shape[0]):
            term = jnp.sum(grads * mix_ref[q, p * size : (p + 1) * size], axis=0, keepdims=True)
            out_ref[q : q + 1, :] = term if p == 0 else out_ref[q : q + 1, :] + term


def scores_of_grads(parts, mix, tokens=(), flops=1024):
    nq, _, count = mix.shape
    parts = [part if isinstance(part, list) else [part] for part in parts]
    kernel = functools.partial(score_kernel, len(parts[0]))
    return call(kernel, [*sum(parts, []), mix], [((nq, count), jnp.float32)], flops, tokens)[0]


def project_kernel(*refs):
    *parts, query_ref, out_ref, mark_ref, grads = refs
    mark_ref[...] = jnp.zeros_like(mark_ref)
    grads[...] = joined(parts, 0)

    def step(q, _):
        out_ref[q] = jnp.dot(grads[...], query_ref[q, 0], preferred_element_type=jnp.float32)
        return 0

    lax.fori_loop(0, query_ref.shape[0], step, 0)


def projected(parts, queries, flops, tokens=()):
    nq, _, depth, width = queries.shape
    count = sum(part.shape[0] for part in parts)
    outs = [((nq, count, width), jnp.float32), MARK]
    scratch = [pltpu.VMEM((count, depth), queries.dtype)]
    return call(project_kernel, [*parts, queries], outs, flops, tokens, scratch)


def finish_kernel(mine_ref, other_ref, proj_ref, out_ref):
    half, width = mine_ref.shape
    swapped = lax.axis_index("dout") == 1
    for h, (first, second) in enumerate(((mine_ref, other_ref), (other_ref, mine_ref))):
        acts = jnp.where(swapped, second[...], first[...]).astype(jnp.float32)
        for q in range(proj_ref.shape[0]):
            terms = acts * proj_ref[q, h * half : (h + 1) * half, :]
            lanes = terms[:, :128]
            for at in range(128, width, 128):
                lanes = lanes + terms[:, at : at + 128]
            out_ref[q : q + 1, h * half : (h + 1) * half] = jnp.sum(lanes.T, axis=0, keepdims=True)


def scores_of_acts(mine, other, proj, tokens=()):
    nq, count, _ = proj.shape
    return call(finish_kernel, [mine, other, proj], [((nq, count), jnp.float32)], tokens=tokens)[0]


def cut(activations, out_grads, queries, far, others, pieces):
    count, part = lax.axis_size("dp"), out_grads.shape[0] // lax.axis_size("din")
    rows, (tokens, width), dtype = queries.shape[2], activations.shape, out_grads.dtype
    half = tokens // 2
    if part % 128 or rows % 128:
        me, column = lax.axis_index("dp"), lax.axis_index("din")
        mine = lax.dynamic_slice_in_dim(activations, lax.axis_index("dout") * half, half, 0)
        share = lax.dynamic_slice_in_dim(out_grads, column * part, part, 0)
        away = [lax.dynamic_slice_in_dim(share, (me ^ d) * rows, rows, 1) for d in [far, *others]]
        own = lax.dynamic_slice_in_dim(out_grads, me * rows, rows, 1).T
        turned = [block.T for block in away[1:]]
        return (mine, away[0]), (queries, activations, own, *turned[:-1], *jnp.split(turned[-1], pieces))
    outs = [((half, width), activations.dtype), ((part, rows), dtype)]
    first = fetch(functools.partial(first_kernel, far), [activations, out_grads], outs, [], 2)
    outs = [(queries.shape, queries.dtype), (activations.shape, activations.dtype), ((rows, tokens), dtype)]
    outs += [((rows, part), dtype)] * (len(others) - 1) + [((rows // pieces, part), dtype)] * pieces
    scratch = [pltpu.VMEM((tokens, rows), dtype), pltpu.VMEM((len(others), part, rows), dtype)]
    arrays = [activations, out_grads, queries]
    return first, fetch(functools.partial(rest_kernel, others), arrays, outs, scratch, len(others) + 3)


def on_device(activations, out_grads, queries):
    count, spread = lax.axis_size("dp"), lax.axis_size("din")

    def to_columns(arrived):
        return [arrived] + [trade(arrived, {"din": r}) for r in range(1, spread)]

    def acts_of(block):
        return [block, trade(block, {"dout": 1})]

    far, late = count - 1, count - 2
    early = list(range(1, late))
    pieces = 2
    (mine, far_grads), (queries, own_acts, own, *sent) = cut(
        activations, out_grads, queries, far, early + [late], pieces
    )
    hops = [(mine, mine)]
    hops.append(pass_on(hops[0], 1, count))
    arrived = {d: trade(block, {"dp": d}) for d, block in zip([far, *early], [far_grads, *sent])}

    mix, token = mixed([own_acts], queries, SHORT)
    scores = scores_of_grads([own], mix)
    hops[1] = hold(list(hops[1]), [token])
    for step in range(2, count - 1):
        hops.append(pass_on(hops[-1], step, count))

    mixes, token = {}, scores
    for d in early:
        mixes[d], token = mixed(acts_of(from_partner(hops, d, count)), queries, SHORT, [token])
    tail = [trade(hold([block], [token, *hops[-1]])[0], {"dp": late}) for block in sent[len(early) :]]
    sides = to_columns(hold([arrived[far]], [*hops[1], *[arrived[d] for d in early]])[0])
    block = from_partner(hops, late, count, [token] + sides)
    end = lax.ppermute(block, "dp", [(1, 0), (count - 2, count - 1)])
    hops.append((end, end))

    proj, token = projected(sides, queries, SHORT, [token])
    terms = []
    for d in early:
        sides = to_columns(hold([arrived[d]], hops[1])[0])
        token = scores_of_grads(sides, mixes[d], [token])
        terms.append(trade(token, {"dp": d}))

    mix, done = mixed(acts_of(block), queries, SHORT, [token])
    tail = [to_columns(hold([piece], [done if p else token], LONG)[0]) for p, piece in enumerate(tail)]
    block = from_partner(hops, far, count, [done])
    terms.append(trade(scores_of_acts(*acts_of(block), proj), {"dp": far}))
    terms.append(trade(scores_of_grads([list(sides) for sides in zip(*tail)], mix, (), LONG), {"dp": late}))
    return over_chips(sum(terms, scores), spread)


def over_chips(scores, spread):
    scores = scores + trade(scores, {"dout": 1})
    return scores + sum(trade(scores, {"din": r}) for r in range(1, spread))


def solution(mesh):
    placed = (P(("groups", "dp"), "din"), P(("groups", "dp"), "dout"), P(None, "dout", "dp", "din"))
    return jax.shard_map(
        on_device, mesh=mesh, in_specs=placed, out_specs=P(None, ("groups", "dp")), check_vma=False
    )
```

```python
import functools
import math

import jax
import jax.numpy as jnp
from jax import lax
from jax.experimental import pallas as pl
from jax.experimental.pallas import tpu as pltpu
from jax.sharding import PartitionSpec as P


LONG, SHORT = 14_000_000_000, 1_000_000


def trade(block, steps, backwards=False):
    axes = tuple(steps)
    sizes = [lax.axis_size(axis) for axis in axes]
    mask = 0
    for axis, size in zip(axes, sizes):
        mask = mask * size + steps[axis]
    route = [(i, i ^ mask) for i in range(math.prod(sizes))]
    return lax.ppermute(block, axes, route[::-1] if backwards else route)


def pass_on(block, step, count):
    up = lax.ppermute(block[0], "dp", [(i, i + 1) for i in range(step - 1, count - 1)])
    down = lax.ppermute(block[1], "dp", [(i, i - 1) for i in range(1, count - step + 1)])
    return up, down


ANYWHERE = pl.BlockSpec(memory_space=pl.ANY)
NEAR = pl.BlockSpec(memory_space=pltpu.VMEM)


def call(kernel, arrays, outs, flops=1024, tokens=(), scratch=()):
    skip = len(tokens)

    def body(*refs):
        kernel(*refs[: len(arrays)], *refs[len(arrays) + skip :])

    return pl.pallas_call(
        body,
        in_specs=[NEAR] * len(arrays) + [ANYWHERE] * skip,
        out_specs=[NEAR] * len(outs),
        out_shape=[pltpu.VMEM(shape, dtype) for shape, dtype in outs],
        scratch_shapes=list(scratch),
        compiler_params=pltpu.CompilerParams(vmem_limit_bytes=12 * 1024 * 1024),
        cost_estimate=pl.CostEstimate(flops=flops, bytes_accessed=1024, transcendentals=0),
    )(*[pltpu.with_memory_space_constraint(array, pltpu.VMEM) for array in arrays], *tokens)


def fetch(kernel, arrays, outs, scratch, copies):
    return pl.pallas_call(
        kernel,
        in_specs=[ANYWHERE] * len(arrays),
        out_specs=[NEAR] * len(outs),
        out_shape=[pltpu.VMEM(shape, dtype) for shape, dtype in outs],
        scratch_shapes=[*scratch, pltpu.SemaphoreType.DMA((copies,))],
        compiler_params=pltpu.CompilerParams(vmem_limit_bytes=12 * 1024 * 1024),
        cost_estimate=pl.CostEstimate(flops=1024, bytes_accessed=1024, transcendentals=0),
    )(*[pltpu.with_memory_space_constraint(array, pltpu.HBM) for array in arrays])


def grads_block(grads_ref, device, part, rows):
    first = pl.multiple_of(lax.axis_index("din") * part, part)
    return grads_ref.at[pl.ds(first, part), pl.ds(pl.multiple_of(device * rows, rows), rows)]


def first_kernel(far, acts_ref, grads_ref, mine_ref, far_ref, arrived):
    half = mine_ref.shape[0]
    rows = pl.ds(pl.multiple_of(lax.axis_index("dout") * half, half), half)
    block = grads_block(grads_ref, lax.axis_index("dp") ^ far, *far_ref.shape)
    copies = [
        pltpu.make_async_copy(acts_ref.at[rows, :], mine_ref, arrived.at[0]),
        pltpu.make_async_copy(block, far_ref, arrived.at[1]),
    ]
    for copy in copies:
        copy.start()
    for copy in copies:
        copy.wait()


def rest_kernel(steps, acts_ref, grads_ref, query_ref, near_query, near_acts, own_out, *refs):
    outs, own, blocks, arrived = list(refs[:-3]), refs[-3], refs[-2], refs[-1]
    me = lax.axis_index("dp")
    tokens, rows = own.shape
    copies = [pltpu.make_async_copy(grads_ref.at[:, pl.ds(pl.multiple_of(me * rows, rows), rows)], own, arrived.at[0])]
    for k, d in enumerate(steps):
        block = grads_block(grads_ref, me ^ d, *blocks.shape[1:])
        copies.append(pltpu.make_async_copy(block, blocks.at[k], arrived.at[1 + k]))
    copies.append(pltpu.make_async_copy(acts_ref, near_acts, arrived.at[len(steps) + 1]))
    copies.append(pltpu.make_async_copy(query_ref, near_query, arrived.at[len(steps) + 2]))
    for copy in copies:
        copy.start()
    for k in range(len(steps)):
        copies[1 + k].wait()
        turned, at = blocks[k].astype(jnp.float32).T.astype(blocks.dtype), 0
        while at < rows:
            out = outs.pop(0)
            out[...] = turned[at : at + out.shape[0]]
            at += out.shape[0]
    copies[0].wait()
    own_out[...] = own[...].astype(jnp.float32).T.astype(own_out.dtype)
    for copy in copies[-2:]:
        copy.wait()


def hold(blocks, tokens, flops=1024):
    count = len(blocks)
    return pl.pallas_call(
        lambda *refs: None,
        in_specs=[ANYWHERE] * (count + len(tokens)),
        out_specs=[ANYWHERE] * count,
        out_shape=[jax.ShapeDtypeStruct(block.shape, block.dtype) for block in blocks],
        input_output_aliases={i: i for i in range(count)},
        compiler_params=pltpu.CompilerParams(vmem_limit_bytes=1024 * 1024),
        cost_estimate=pl.CostEstimate(flops=flops, bytes_accessed=1024, transcendentals=0),
    )(*blocks, *tokens)


def pick_kernel(choice, *refs):
    *blocks, out_ref = refs
    me = lax.axis_index("dp")
    where = functools.reduce(lambda found, z: jnp.where(me == z, choice[z], found), range(len(choice)), 0)
    for k, block in enumerate(blocks):

        @pl.when(where == k)
        def _():
            out_ref[...] = block[...]


def from_partner(hops, d, count, tokens=()):
    sources, choice = [], []
    for z in range(count):
        away = z - (z ^ d)
        source = (abs(away), int(away < 0 and abs(away) < count - 1))
        if source not in sources:
            sources.append(source)
        choice.append(sources.index(source))
    blocks = [hops[step][way] for step, way in sources]
    outs = [(blocks[0].shape, blocks[0].dtype)]
    return call(functools.partial(pick_kernel, choice), blocks, outs, tokens=tokens)[0]


def joined(parts, axis):
    parts = [part[...] for part in parts]
    if len(parts) == 1:
        return parts[0]
    column, found = lax.axis_index("din"), []
    for p in range(len(parts)):
        chosen = parts[0]
        for r in range(1, len(parts)):
            chosen = jnp.where(column == p ^ r, parts[r], chosen)
        found.append(chosen)
    return jnp.concatenate(found, axis=axis)


MARK = (8, 128), jnp.float32


def mix_kernel(*refs):
    *parts, query_ref, out_ref, mark_ref, acts = refs
    mark_ref[...] = jnp.zeros_like(mark_ref)
    half = parts[0].shape[0]
    first = lax.axis_index("dout") * half if len(parts) > 1 else 0
    for part, at in zip(parts, (first, half - first)):
        acts[pl.ds(pl.multiple_of(at, half), half), :] = part[...]

    def step(q, _):
        out_ref[q] = lax.dot_general(
            query_ref[q, 0], acts[...], (((1,), (1,)), ((), ())), preferred_element_type=jnp.float32
        )
        return 0

    lax.fori_loop(0, query_ref.shape[0], step, 0)


def mixed(parts, queries, flops, tokens=()):
    nq, _, depth, width = queries.shape
    tokens_here = sum(part.shape[0] for part in parts)
    outs = [((nq, depth, tokens_here), jnp.float32), MARK]
    scratch = [pltpu.VMEM((tokens_here, width), queries.dtype)]
    return call(mix_kernel, [*parts, queries], outs, flops, tokens, scratch)


def score_kernel(pieces, *refs):
    *parts, mix_ref, out_ref = refs
    size = mix_ref.shape[1] // pieces
    for p in range(pieces):
        grads = joined(parts[p::pieces], 1).astype(jnp.float32)
        for q in range(mix_ref.shape[0]):
            term = jnp.sum(grads * mix_ref[q, p * size : (p + 1) * size], axis=0, keepdims=True)
            out_ref[q : q + 1, :] = term if p == 0 else out_ref[q : q + 1, :] + term


def scores_of_grads(parts, mix, tokens=(), flops=1024):
    nq, _, count = mix.shape
    parts = [part if isinstance(part, list) else [part] for part in parts]
    kernel = functools.partial(score_kernel, len(parts[0]))
    return call(kernel, [*sum(parts, []), mix], [((nq, count), jnp.float32)], flops, tokens)[0]


def project_kernel(*refs):
    *parts, query_ref, out_ref, mark_ref, grads = refs
    mark_ref[...] = jnp.zeros_like(mark_ref)
    grads[...] = joined(parts, 0)

    def step(q, _):
        out_ref[q] = jnp.dot(grads[...], query_ref[q, 0], preferred_element_type=jnp.float32)
        return 0

    lax.fori_loop(0, query_ref.shape[0], step, 0)


def projected(parts, queries, flops, tokens=()):
    nq, _, depth, width = queries.shape
    count = sum(part.shape[0] for part in parts)
    outs = [((nq, count, width), jnp.float32), MARK]
    scratch = [pltpu.VMEM((count, depth), queries.dtype)]
    return call(project_kernel, [*parts, queries], outs, flops, tokens, scratch)


def finish_kernel(mine_ref, other_ref, proj_ref, out_ref):
    half, width = mine_ref.shape
    swapped = lax.axis_index("dout") == 1
    for h, (first, second) in enumerate(((mine_ref, other_ref), (other_ref, mine_ref))):
        acts = jnp.where(swapped, second[...], first[...]).astype(jnp.float32)
        for q in range(proj_ref.shape[0]):
            terms = acts * proj_ref[q, h * half : (h + 1) * half, :]
            lanes = terms[:, :128]
            for at in range(128, width, 128):
                lanes = lanes + terms[:, at : at + 128]
            out_ref[q : q + 1, h * half : (h + 1) * half] = jnp.sum(lanes.T, axis=0, keepdims=True)


def scores_of_acts(mine, other, proj, tokens=()):
    nq, count, _ = proj.shape
    return call(finish_kernel, [mine, other, proj], [((nq, count), jnp.float32)], tokens=tokens)[0]


def cut(activations, out_grads, queries, far, others, pieces):
    count, part = lax.axis_size("dp"), out_grads.shape[0] // lax.axis_size("din")
    rows, (tokens, width), dtype = queries.shape[2], activations.shape, out_grads.dtype
    half = tokens // 2
    if part % 128 or rows % 128:
        me, column = lax.axis_index("dp"), lax.axis_index("din")
        mine = lax.dynamic_slice_in_dim(activations, lax.axis_index("dout") * half, half, 0)
        share = lax.dynamic_slice_in_dim(out_grads, column * part, part, 0)
        away = [lax.dynamic_slice_in_dim(share, (me ^ d) * rows, rows, 1) for d in [far, *others]]
        own = lax.dynamic_slice_in_dim(out_grads, me * rows, rows, 1).T
        turned = [block.T for block in away[1:]]
        return (mine, away[0]), (queries, activations, own, *turned[:-1], *jnp.split(turned[-1], pieces))
    outs = [((half, width), activations.dtype), ((part, rows), dtype)]
    first = fetch(functools.partial(first_kernel, far), [activations, out_grads], outs, [], 2)
    outs = [(queries.shape, queries.dtype), (activations.shape, activations.dtype), ((rows, tokens), dtype)]
    outs += [((rows, part), dtype)] * (len(others) - 1) + [((rows // pieces, part), dtype)] * pieces
    scratch = [pltpu.VMEM((tokens, rows), dtype), pltpu.VMEM((len(others), part, rows), dtype)]
    arrays = [activations, out_grads, queries]
    return first, fetch(functools.partial(rest_kernel, others), arrays, outs, scratch, len(others) + 3)


def on_device(activations, out_grads, queries):
    count, spread = lax.axis_size("dp"), lax.axis_size("din")

    def to_columns(arrived):
        return [arrived] + [trade(arrived, {"din": r}) for r in range(1, spread)]

    def acts_of(block):
        return [block, trade(block, {"dout": 1})]

    far, late = count - 1, count - 2
    early = list(range(1, late))
    pieces = 2
    (mine, far_grads), (queries, own_acts, own, *sent) = cut(
        activations, out_grads, queries, far, early + [late], pieces
    )
    hops = [(mine, mine)]
    hops.append(pass_on(hops[0], 1, count))
    arrived = {d: trade(block, {"dp": d}) for d, block in zip([far, *early], [far_grads, *sent])}

    mix, token = mixed([own_acts], queries, SHORT)
    scores = scores_of_grads([own], mix)
    hops[1] = hold(list(hops[1]), [token])
    for step in range(2, count - 1):
        hops.append(pass_on(hops[-1], step, count))

    mixes, token = {}, scores
    for d in early:
        mixes[d], token = mixed(acts_of(from_partner(hops, d, count)), queries, SHORT, [token])
    tail = [trade(hold([block], [token, *hops[-1]])[0], {"dp": late}) for block in sent[len(early) :]]
    sides = to_columns(hold([arrived[far]], [*hops[1], *[arrived[d] for d in early]])[0])
    block = from_partner(hops, late, count, [token] + sides)
    end = lax.ppermute(block, "dp", [(1, 0), (count - 2, count - 1)])
    hops.append((end, end))

    proj, token = projected(sides, queries, SHORT, [token])
    terms = []
    for d in early:
        sides = to_columns(hold([arrived[d]], hops[1])[0])
        token = scores_of_grads(sides, mixes[d], [token])
        terms.append(trade(token, {"dp": d}))

    mix, done = mixed(acts_of(block), queries, SHORT, [token])
    tail = [to_columns(hold([piece], [done], LONG)[0]) for piece in tail]
    block = from_partner(hops, far, count, [done])
    terms.append(trade(scores_of_acts(*acts_of(block), proj), {"dp": far}))
    terms.append(trade(scores_of_grads([list(sides) for sides in zip(*tail)], mix, (), LONG), {"dp": late}))
    return over_chips(sum(terms, scores), spread)


def over_chips(scores, spread):
    scores = scores + trade(scores, {"dout": 1})
    return scores + sum(trade(scores, {"din": r}) for r in range(1, spread))


def solution(mesh):
    placed = (P(("groups", "dp"), "din"), P(("groups", "dp"), "dout"), P(None, "dout", "dp", "din"))
    return jax.shard_map(
        on_device, mesh=mesh, in_specs=placed, out_specs=P(None, ("groups", "dp")), check_vma=False
    )
```
